256 devices in a mesh: tm: 16 (over y_hi, z), height: 16 (over y_lo, x, core).
Axes of the slice: x: 4, y: 4 (y_hi: 2, y_lo: 2; y = y_hi * 2 + y_lo), z: 8, core: 2. Of those that a mesh axis runs over, the one named last changes fastest.
Arguments:
- saved: bfloat16 [2, 4, 32, 128, 16, 1536], P(None, None, 'tm', 'height'), may hold values from -600 to 600
- gains: float32 [2, 2, 12, 128], replicated, may hold values from 0.5 to 6
Outputs:
- grads: bfloat16 [2, 3, 32, 128, 16, 1536], P(None, None, 'tm', 'height')
- gain_grads: float32 [2, 2, 12, 128], replicated
The draws below stay inside these ranges and needn't reach their ends.
All inputs are finite; a program needn't handle non-finite values.
Results may differ from the reference program's by a relative error of at most 0.0039.
The reference program's roundings to bfloat16 on the way count: a program that leaves them out, or rounds other values in their place, can miss the bound.
Values may be sent and summed in bfloat16 or wider, within the bound.
A program may use at most 128 MiB of HBM per device.

```python
import math
import jax
import jax.numpy as jnp
from jax import lax

HEADS = 12
HD = 128
WT = 2
WH = 8
WW = 16
COLS = 16
FRAMES = 32
ROWS = 128


def draw_saved(key, part):
    key = jax.random.fold_in(key, 11)
    feats = HEADS * HD
    layout = (FRAMES, ROWS, COLS, feats)
    blocks = []
    for block in range(2):
        keys = jax.random.split(jax.random.fold_in(key, block), 12)
        arrays = []
        for index in range(4):
            base = jnp.clip(jax.random.normal(keys[index], layout, jnp.float32), -6.0, 6.0)
            arrays.append(base)
        row_q = jnp.exp(jax.random.uniform(keys[4], (FRAMES, ROWS, COLS, 1)) * math.log(10.0))
        col_q = jnp.exp(jax.random.uniform(keys[5], (feats,)) * math.log(10.0))
        row_k = jnp.exp(jax.random.uniform(keys[6], (FRAMES, ROWS, COLS, 1)) * math.log(10.0))
        col_k = jnp.exp(jax.random.uniform(keys[7], (feats,)) * math.log(10.0))
        q_raw = arrays[0] * row_q * col_q
        k_raw = arrays[1] * row_k * col_k
        ramp = 0.5 + jnp.arange(FRAMES, dtype=jnp.float32)[:, None, None, None] / (FRAMES - 1)
        out_grad = arrays[3] * ramp
        blocks.append(jnp.stack([q_raw, k_raw, arrays[2], out_grad]))
    return jnp.clip(jnp.stack(blocks), -600.0, 600.0).astype(jnp.bfloat16)


def draw_gains(key, part):
    key = jax.random.fold_in(key, 12)
    lower, upper = (0.5, 2.0)
    draws = jax.random.uniform(key, (2, 2, HEADS, HD), jnp.float32, math.log(lower), math.log(upper))
    return jnp.exp(draws)


def setup_inputs(seed: int = 0) -> dict:
    key_of = jax.random.split(jax.random.key(seed), 3)
    saved = draw_saved(jax.random.fold_in(key_of[2], 71), 0)
    gains = draw_gains(jax.random.fold_in(key_of[2], 71), 0)
    return {"saved": saved, "gains": gains}


EPSILON = 1e-06

def windows(array):
    frames, rows, cols, feats = array.shape
    blocked = array.reshape(frames // WT, WT, rows // WH, WH, cols // WW, WW, HEADS, HD)
    blocked = blocked.transpose(0, 2, 4, 6, 1, 3, 5, 7)
    return blocked.reshape(-1, HEADS, WT * WH * WW, HD)

def unwindows(blocked, layout):
    frames, rows, cols, feats = layout
    grid = blocked.reshape(frames // WT, rows // WH, cols // WW, HEADS, WT, WH, WW, HD)
    return grid.transpose(0, 4, 1, 5, 2, 6, 3, 7).reshape(frames, rows, cols, feats)

def raw_grad(norm_grad, unit, inverse, gain):
    scaled = norm_grad * gain[:, None, :]
    return (inverse * (scaled - unit * lax.optimization_barrier(jnp.mean(scaled * unit, -1, keepdims=True)))).astype(jnp.bfloat16)

def window_grad(q_raw, k_raw, values_in, out_grad, gain_q, gain_k):
    scale = HD ** (-0.5)
    q_full = q_raw.astype(jnp.float32)
    k_full = k_raw.astype(jnp.float32)
    inv_q = lax.rsqrt(lax.optimization_barrier(jnp.mean(q_full * q_full, -1, keepdims=True)) + EPSILON)
    inv_k = lax.rsqrt(lax.optimization_barrier(jnp.mean(k_full * k_full, -1, keepdims=True)) + EPSILON)
    unit_q = q_full * inv_q
    unit_k = k_full * inv_k
    q_norm = (unit_q * gain_q[:, None, :]).astype(jnp.bfloat16).astype(jnp.float32)
    k_norm = (unit_k * gain_k[:, None, :]).astype(jnp.bfloat16).astype(jnp.float32)
    scores = jnp.einsum('hqd,hkd->hqk', q_norm, k_norm) * scale
    attn_probs = jnp.exp(scores - lax.optimization_barrier(jnp.max(scores, -1, keepdims=True)))
    attn_probs = attn_probs / lax.optimization_barrier(jnp.sum(attn_probs, -1, keepdims=True))
    probs_low = attn_probs.astype(jnp.bfloat16).astype(jnp.float32)
    out_full = out_grad.astype(jnp.float32)
    prob_grad = jnp.einsum('hqd,hkd->hqk', out_full, values_in.astype(jnp.float32))
    score_grad = attn_probs * (prob_grad - lax.optimization_barrier(jnp.sum(attn_probs * prob_grad, -1, keepdims=True)))
    score_grad = score_grad.astype(jnp.bfloat16).astype(jnp.float32)
    value_grad = jnp.einsum('hqk,hqd->hkd', probs_low, out_full).astype(jnp.bfloat16)
    qn_grad = jnp.einsum('hqk,hkd->hqd', score_grad, k_norm) * scale
    kn_grad = jnp.einsum('hqk,hqd->hkd', score_grad, q_norm) * scale
    gain_q_grad = lax.optimization_barrier(jnp.sum(qn_grad * unit_q, axis=1))
    gain_k_grad = lax.optimization_barrier(jnp.sum(kn_grad * unit_k, axis=1))
    return (raw_grad(qn_grad, unit_q, inv_q, gain_q), raw_grad(kn_grad, unit_k, inv_k, gain_k), value_grad, gain_q_grad, gain_k_grad)

def block_grad(stacked, gain_pair):
    layout = stacked.shape[1:]
    pieces = tuple((windows(stacked[index]) for index in range(4)))

    def single(items):
        return window_grad(items[0], items[1], items[2], items[3], gain_pair[0], gain_pair[1])
    results = lax.map(single, pieces)
    grads_block = jnp.stack([unwindows(results[index], layout) for index in range(3)])
    gains_block = jnp.stack([lax.optimization_barrier(jnp.sum(results[3], 0)), lax.optimization_barrier(jnp.sum(results[4], 0))])
    return (grads_block, gains_block)

def reference(saved, gains):
    half_t, half_h, half_w = (WT // 2, WH // 2, WW // 2)
    grads_zero, gains_zero = block_grad(saved[0], gains[0])
    shifted = jnp.roll(saved[1], (-half_t, -half_h, -half_w), axis=(1, 2, 3))
    grads_rolled, gains_one = block_grad(shifted, gains[1])
    grads_one = jnp.roll(grads_rolled, (half_t, half_h, half_w), axis=(1, 2, 3))
    return (jnp.stack([grads_zero, grads_one]), jnp.stack([gains_zero, gains_one]))
```

```python
import functools
import math

import jax
import jax.numpy as jnp
from jax import lax
from jax.experimental import pallas as pl
from jax.experimental.pallas import tpu as pltpu
from jax.sharding import PartitionSpec as P

HEADS = 12
HD = 128
WT = 2
WH = 8
WW = 16
HALF_H = WH // 2
TOKENS = WT * WH * WW
HALF_HEADS = HEADS // 2
GAIN_ROWS = 2 * 2 * HEADS

EPSILON = 1e-06
SCALE = HD ** (-0.5)
EXP2_SCALE = SCALE * math.log2(math.e)

MESH = pl.DeviceIdType.MESH
NT = (((1,), (1,)), ((), ()))
NN = (((1,), (0,)), ((), ()))
TN = (((0,), (0,)), ((), ()))


def matmul(a, b, dims):
    return lax.dot_general(a, b, dims, preferred_element_type=jnp.float32)


def head_grad(q_raw, k_raw, values_in, out_grad, gain_q, gain_k):
    q_full = q_raw.astype(jnp.float32)
    k_full = k_raw.astype(jnp.float32)
    inv_q = lax.rsqrt(jnp.mean(q_full * q_full, -1, keepdims=True) + EPSILON)
    inv_k = lax.rsqrt(jnp.mean(k_full * k_full, -1, keepdims=True) + EPSILON)
    unit_q = q_full * inv_q
    unit_k = k_full * inv_k
    q_norm = (unit_q * gain_q).astype(jnp.bfloat16)
    k_norm = (unit_k * gain_k).astype(jnp.bfloat16)
    scores = matmul(k_norm, q_norm, NT)
    prob_grad = matmul(values_in, out_grad, NT)
    top = jnp.max(scores, 0, keepdims=True)
    probs = jnp.exp2((scores - top) * EXP2_SCALE)
    probs = probs * (1.0 / jnp.sum(probs, 0, keepdims=True))
    delta = jnp.sum(probs * prob_grad, 0, keepdims=True)
    score_grad = (probs * (prob_grad - delta)).astype(jnp.bfloat16)
    value_grad = matmul(probs.astype(jnp.bfloat16), out_grad, NN).astype(jnp.bfloat16)
    kn_grad = matmul(score_grad, q_norm, NN)
    qn_grad = matmul(score_grad, k_norm, TN)

    def raw_grad(norm_grad, unit, inverse, gain):
        along = norm_grad * unit
        gain_grad = jnp.sum(along, 0, keepdims=True) * SCALE
        scaled_gain = gain * SCALE
        mean = jnp.mean(along * scaled_gain, -1, keepdims=True)
        raw = inverse * (norm_grad * scaled_gain - unit * mean)
        return raw.astype(jnp.bfloat16), gain_grad

    q_grad, gain_q_grad = raw_grad(qn_grad, unit_q, inv_q, gain_q)
    k_grad, gain_k_grad = raw_grad(kn_grad, unit_k, inv_k, gain_k)
    return (q_grad, k_grad, value_grad), gain_q_grad, gain_k_grad


def kernel(
    n_t, n_h,
    saved, gains, out, gain_out,
    x0, x1, y0, y1, part, piece_in, piece_mid, total,
    load0, load1, store0, store1,
    in_send, in_recv, out_send, out_recv, gain_send, gain_recv,
):
    t = lax.axis_index("tm")
    h = lax.axis_index("height")
    rows = GAIN_ROWS // n_h

    def t_at(shift):
        return lax.rem(t + shift + n_t, n_t)

    def h_at(shift):
        return lax.rem(h + shift + n_h, n_h)

    def features(head):
        return pl.ds(pl.multiple_of(head * HD, HD), HD)

    def unit(u):
        role = lax.rem(u, 2)
        return role, role * HALF_HEADS + u // 2

    def quadrant(u, slot):
        role, head = unit(u)
        frame = 1 - role if slot < 2 else role
        first = HALF_H if slot % 2 == 0 else 0
        return frame, pl.ds(first, HALF_H), head

    def owner(u, slot):
        role, _ = unit(u)
        shift = 0 if slot < 2 else 1 - 2 * role
        return (t_at(shift), h_at(slot % 2))

    def worker(u, slot):
        role, _ = unit(u)
        shift = 0 if slot < 2 else 2 * role - 1
        return (t_at(shift), h_at(-(slot % 2)))

    def in_copy(u, slot):
        frame, band, head = quadrant(u, slot)
        return pltpu.make_async_remote_copy(
            src_ref=saved.at[1, :, frame, band, :, features(head)],
            dst_ref=x1.at[u, :, slot],
            send_sem=in_send.at[u, slot - 1],
            recv_sem=in_recv.at[u, slot - 1],
            device_id=worker(u, slot),
            device_id_type=MESH,
        )

    def in_local(u):
        frame, band, head = quadrant(u, 0)
        return pltpu.make_async_copy(
            saved.at[1, :, frame, band, :, features(head)], x1.at[u, :, 0], load1.at[u]
        )

    def out_copy(u, slot):
        frame, band, head = quadrant(u, slot)
        return pltpu.make_async_remote_copy(
            src_ref=y1.at[u, :, slot],
            dst_ref=out.at[1, :, frame, band, :, features(head)],
            send_sem=out_send.at[u, slot - 1],
            recv_sem=out_recv.at[u, slot - 1],
            device_id=owner(u, slot),
            device_id_type=MESH,
        )

    def out_local(u):
        frame, band, head = quadrant(u, 0)
        return pltpu.make_async_copy(
            y1.at[u, :, 0], out.at[1, :, frame, band, :, features(head)], store1.at[u]
        )

    def load(head):
        return pltpu.make_async_copy(
            saved.at[0, :, :, :, :, features(head)], x0.at[head], load0.at[head]
        )

    def store(head):
        return pltpu.make_async_copy(
            y0.at[head], out.at[0, :, :, :, :, features(head)], store0.at[head]
        )

    def each(count, body):
        lax.fori_loop(0, count, lambda i, carry: (body(i), carry)[1], 0)

    def start_local(u):
        load(u).start()
        in_local(u).start()

    each(HEADS, start_local)
    barrier = pltpu.get_barrier_semaphore()

    def greet(t_to, h_to):
        pl.semaphore_signal(barrier, inc=1, device_id=(t_to, h_to), device_id_type=MESH)

    for dt in (-1, 1):
        for dh in (-1, 1):
            greet(t_at(dt), h_at(dh))
    each(n_h - 1, lambda i: greet(t, h_at(i + 1)))
    each(n_t - 1, lambda i: greet(t_at(i + 1), h))
    pl.semaphore_wait(barrier, 4 + (n_h - 1) + (n_t - 1))

    def start_inputs(u):
        for slot in (2, 3, 1):
            in_copy(u, slot).start()

    each(HEADS, start_inputs)

    def compute(source, target, index, block, head):
        operands = [source[index, a].reshape(TOKENS, HD) for a in range(4)]
        gain_q = gains[block, head, 0:1, :]
        gain_k = gains[block, head, 1:2, :]
        grads, gain_q_grad, gain_k_grad = head_grad(*operands, gain_q, gain_k)
        for a in range(3):
            target[index, a] = grads[a].reshape(target.shape[2:])
        row = 2 * (block * HEADS + head)
        part[row] = gain_q_grad
        part[row + 1] = gain_k_grad

    def step(u):
        load(u).wait()
        compute(x0, y0, u, 0, u)
        store(u).start()
        in_local(u).wait()
        for slot in (1, 2, 3):
            in_copy(u, slot).wait_recv()
        compute(x1, y1, u, 1, unit(u)[1])
        for slot in (2, 3, 1):
            out_copy(u, slot).start()
        out_local(u).start()

    each(HEADS, step)

    def piece(index):
        return pl.ds(index * rows, rows)

    def scatter(k):
        return pltpu.make_async_remote_copy(
            src_ref=part.at[piece(h_at(k))],
            dst_ref=piece_in.at[h],
            send_sem=gain_send.at[0, k],
            recv_sem=gain_recv.at[0, k],
            device_id=(t, h_at(k)),
            device_id_type=MESH,
        )

    def exchange(k):
        return pltpu.make_async_remote_copy(
            src_ref=piece_mid.at[t],
            dst_ref=piece_mid.at[t],
            send_sem=gain_send.at[1, k],
            recv_sem=gain_recv.at[1, k],
            device_id=(t_at(k), h),
            device_id_type=MESH,
        )

    def gather(k):
        return pltpu.make_async_remote_copy(
            src_ref=total.at[piece(h)],
            dst_ref=total.at[piece(h)],
            send_sem=gain_send.at[2, k],
            recv_sem=gain_recv.at[2, k],
            device_id=(t, h_at(k)),
            device_id_type=MESH,
        )

    each(n_h - 1, lambda i: scatter(i + 1).start())
    piece_in[h] = part[piece(h)]
    each(n_h - 1, lambda i: scatter(i + 1).wait_recv())
    piece_mid[t] = jnp.sum(piece_in[...], 0)
    each(n_t - 1, lambda i: exchange(i + 1).start())
    each(n_t - 1, lambda i: exchange(i + 1).wait_recv())
    total[piece(h)] = jnp.sum(piece_mid[...], 0)
    each(n_h - 1, lambda i: gather(i + 1).start())
    each(n_h - 1, lambda i: gather(i + 1).wait_recv())
    for row in range(GAIN_ROWS):
        block, rest = divmod(row, 2 * HEADS)
        head, side = divmod(rest, 2)
        gain_out[block, head, side : side + 1, :] = total[row]
    each(n_h - 1, lambda i: scatter(i + 1).wait_send())
    each(n_t - 1, lambda i: exchange(i + 1).wait_send())
    each(n_h - 1, lambda i: gather(i + 1).wait_send())

    def finish(u):
        store(u).wait()
        out_local(u).wait()
        for slot in (1, 2, 3):
            in_copy(u, slot).wait_send()
            out_copy(u, slot).wait()

    each(HEADS, finish)


def solution(mesh):
    n_t, n_h = mesh.shape["tm"], mesh.shape["height"]
    rows = GAIN_ROWS // n_h
    dma = pltpu.SemaphoreType.DMA

    def shards(saved, gains):
        grads_shape = (2, 3) + saved.shape[2:]
        half_window = (HALF_H, WW, HD)
        grads, gain_grads = pl.pallas_call(
            functools.partial(kernel, n_t, n_h),
            out_shape=(
                jax.ShapeDtypeStruct(grads_shape, jnp.bfloat16),
                jax.ShapeDtypeStruct((2, HEADS, 2, HD), jnp.float32),
            ),
            in_specs=[
                pl.BlockSpec(memory_space=pl.ANY),
                pl.BlockSpec(memory_space=pltpu.VMEM),
            ],
            out_specs=(
                pl.BlockSpec(memory_space=pl.ANY),
                pl.BlockSpec(memory_space=pltpu.VMEM),
            ),
            scratch_shapes=[
                pltpu.VMEM((HEADS, 4, WT, WH, WW, HD), jnp.bfloat16),
                pltpu.VMEM((HEADS, 4, 4) + half_window, jnp.bfloat16),
                pltpu.VMEM((HEADS, 3, WT, WH, WW, HD), jnp.bfloat16),
                pltpu.VMEM((HEADS, 3, 4) + half_window, jnp.bfloat16),
                pltpu.VMEM((GAIN_ROWS, 1, HD), jnp.float32),
                pltpu.VMEM((n_h, rows, 1, HD), jnp.float32),
                pltpu.VMEM((n_t, rows, 1, HD), jnp.float32),
                pltpu.VMEM((GAIN_ROWS, 1, HD), jnp.float32),
                dma((HEADS,)),
                dma((HEADS,)),
                dma((HEADS,)),
                dma((HEADS,)),
                dma((HEADS, 3)),
                dma((HEADS, 3)),
                dma((HEADS, 3)),
                dma((HEADS, 3)),
                dma((3, max(n_t, n_h))),
                dma((3, max(n_t, n_h))),
            ],
            compiler_params=pltpu.CompilerParams(
                collective_id=0, has_side_effects=True, vmem_limit_bytes=56 * 2**20
            ),
            cost_estimate=pl.CostEstimate(
                flops=2 * HEADS * 5 * 2 * TOKENS * TOKENS * HD,
                bytes_accessed=14 * HEADS * TOKENS * HD * 2,
                transcendentals=2 * HEADS * TOKENS * TOKENS,
            ),
        )(saved, gains.transpose(0, 2, 1, 3))
        return grads, gain_grads.transpose(0, 2, 1, 3)

    return jax.shard_map(
        shards,
        mesh=mesh,
        in_specs=(P(None, None, "tm", "height", None, None), P()),
        out_specs=(P(None, None, "tm", "height", None, None), P()),
        check_vma=False,
    )
```

```python
import functools
import math

import jax
import jax.numpy as jnp
from jax import lax
from jax.experimental import pallas as pl
from jax.experimental.pallas import tpu as pltpu
from jax.sharding import PartitionSpec as P

HEADS = 12
HD = 128
WT = 2
WH = 8
WW = 16
HALF_H = WH // 2
TOKENS = WT * WH * WW
HALF_HEADS = HEADS // 2
GAIN_ROWS = 2 * 2 * HEADS

EPSILON = 1e-06
SCALE = HD ** (-0.5)
EXP2_SCALE = SCALE * math.log2(math.e)

MESH = pl.DeviceIdType.MESH
NT = (((1,), (1,)), ((), ()))
NN = (((1,), (0,)), ((), ()))
TN = (((0,), (0,)), ((), ()))


def matmul(a, b, dims):
    return lax.dot_general(a, b, dims, preferred_element_type=jnp.float32)


def head_grad(q_raw, k_raw, values_in, out_grad, gain_q, gain_k):
    q_full = q_raw.astype(jnp.float32)
    k_full = k_raw.astype(jnp.float32)
    inv_q = lax.rsqrt(jnp.mean(q_full * q_full, -1, keepdims=True) + EPSILON)
    inv_k = lax.rsqrt(jnp.mean(k_full * k_full, -1, keepdims=True) + EPSILON)
    unit_q = q_full * inv_q
    unit_k = k_full * inv_k
    q_norm = (unit_q * gain_q).astype(jnp.bfloat16)
    k_norm = (unit_k * gain_k).astype(jnp.bfloat16)
    scores = matmul(k_norm, q_norm, NT)
    prob_grad = matmul(values_in, out_grad, NT)
    top = jnp.max(scores, 0, keepdims=True)
    probs = jnp.exp2((scores - top) * EXP2_SCALE)
    probs = probs * (1.0 / jnp.sum(probs, 0, keepdims=True))
    delta = jnp.sum(probs * prob_grad, 0, keepdims=True)
    score_grad = (probs * (prob_grad - delta)).astype(jnp.bfloat16)
    value_grad = matmul(probs.astype(jnp.bfloat16), out_grad, NN).astype(jnp.bfloat16)
    kn_grad = matmul(score_grad, q_norm, NN)
    qn_grad = matmul(score_grad, k_norm, TN)

    def raw_grad(norm_grad, unit, inverse, gain):
        along = norm_grad * unit
        gain_grad = jnp.sum(along, 0, keepdims=True) * SCALE
        scaled_gain = gain * SCALE
        mean = jnp.mean(along * scaled_gain, -1, keepdims=True)
        raw = inverse * (norm_grad * scaled_gain - unit * mean)
        return raw.astype(jnp.bfloat16), gain_grad

    q_grad, gain_q_grad = raw_grad(qn_grad, unit_q, inv_q, gain_q)
    k_grad, gain_k_grad = raw_grad(kn_grad, unit_k, inv_k, gain_k)
    return (q_grad, k_grad, value_grad), gain_q_grad, gain_k_grad


def each(count, body):
    lax.fori_loop(0, count, lambda i, carry: (body(i), carry)[1], 0)


def still_kernel(saved, gains, grads, sums):
    head = pl.program_id(0)
    operands = [saved[0, a].reshape(TOKENS, HD) for a in range(4)]
    results, gain_q_grad, gain_k_grad = head_grad(
        *operands, gains[0, head, 0:1, :], gains[0, head, 1:2, :]
    )
    for a in range(3):
        grads[0, a] = results[a].reshape(grads.shape[2:])
    sums[head, 0:1, :] = gain_q_grad
    sums[head, 1:2, :] = gain_k_grad


def shifted_kernel(
    n_t, n_h,
    saved, gains, grads, sums,
    x1, w1, load1, in_send, in_recv, out_send, out_recv,
):
    t = lax.axis_index("tm")
    h = lax.axis_index("height")

    def t_at(shift):
        return lax.rem(t + shift + n_t, n_t)

    def h_at(shift):
        return lax.rem(h + shift + n_h, n_h)

    def features(head):
        return pl.ds(pl.multiple_of(head * HD, HD), HD)

    def unit(u):
        role = lax.rem(u, 2)
        return role, role * HALF_HEADS + u // 2

    def quadrant(u, slot):
        role, head = unit(u)
        frame = 1 - role if slot < 2 else role
        first = HALF_H if slot % 2 == 0 else 0
        return frame, pl.ds(first, HALF_H), head

    def owner(u, slot):
        role, _ = unit(u)
        shift = 0 if slot < 2 else 1 - 2 * role
        return (t_at(shift), h_at(slot % 2))

    def worker(u, slot):
        role, _ = unit(u)
        shift = 0 if slot < 2 else 2 * role - 1
        return (t_at(shift), h_at(-(slot % 2)))

    def in_copy(u, slot):
        frame, band, head = quadrant(u, slot)
        return pltpu.make_async_remote_copy(
            src_ref=saved.at[1, :, frame, band, :, features(head)],
            dst_ref=x1.at[u, :, slot],
            send_sem=in_send.at[u, slot - 1],
            recv_sem=in_recv.at[u, slot - 1],
            device_id=worker(u, slot),
            device_id_type=MESH,
        )

    def in_local(u):
        frame, band, head = quadrant(u, 0)
        return pltpu.make_async_copy(
            saved.at[1, :, frame, band, :, features(head)], x1.at[u, :, 0], load1.at[u]
        )

    def out_copy(u, slot):
        frame, band, head = quadrant(u, slot)
        return pltpu.make_async_remote_copy(
            src_ref=w1.at[u, :, slot - 1],
            dst_ref=grads.at[head, :, frame, band],
            send_sem=out_send.at[u, slot - 1],
            recv_sem=out_recv.at[u, slot - 1],
            device_id=owner(u, slot),
            device_id_type=MESH,
        )

    each(HEADS, lambda u: in_local(u).start())
    barrier = pltpu.get_barrier_semaphore()
    for dt in (-1, 0, 1):
        for dh in (-1, 0, 1):
            if dt or dh:
                pl.semaphore_signal(
                    barrier, inc=1, device_id=(t_at(dt), h_at(dh)), device_id_type=MESH
                )
    pl.semaphore_wait(barrier, 8)

    def start_inputs(u):
        for slot in (2, 3, 1):
            in_copy(u, slot).start()

    each(HEADS, start_inputs)

    def step(u):
        in_local(u).wait()
        for slot in (1, 2, 3):
            in_copy(u, slot).wait_recv()
        frame, band, head = quadrant(u, 0)
        operands = [x1[u, a].reshape(TOKENS, HD) for a in range(4)]
        results, gain_q_grad, gain_k_grad = head_grad(
            *operands, gains[1, head, 0:1, :], gains[1, head, 1:2, :]
        )
        for a in range(3):
            quads = results[a].reshape(4, HALF_H, WW, HD)
            w1[u, a] = quads[1:]
            grads[head, a, frame, band] = quads[0]
        sums[head, 0:1, :] = gain_q_grad
        sums[head, 1:2, :] = gain_k_grad
        for slot in (2, 3, 1):
            out_copy(u, slot).start()

    each(HEADS, step)

    def finish(u):
        for slot in (1, 2, 3):
            in_copy(u, slot).wait_send()
            out_copy(u, slot).wait()

    each(HEADS, finish)


def sum_kernel(n_t, n_h, sums0, sums1, out, part, piece_in, piece_mid, total, gain_send, gain_recv):
    t = lax.axis_index("tm")
    h = lax.axis_index("height")
    rows = GAIN_ROWS // n_h

    def t_at(shift):
        return lax.rem(t + shift + n_t, n_t)

    def h_at(shift):
        return lax.rem(h + shift + n_h, n_h)

    barrier = pltpu.get_barrier_semaphore()

    def greet(t_to, h_to):
        pl.semaphore_signal(barrier, inc=1, device_id=(t_to, h_to), device_id_type=MESH)

    each(n_h - 1, lambda i: greet(t, h_at(i + 1)))
    each(n_t - 1, lambda i: greet(t_at(i + 1), h))
    for row in range(GAIN_ROWS):
        block, rest = divmod(row, 2 * HEADS)
        head, side = divmod(rest, 2)
        part[row] = (sums0, sums1)[block][head, side : side + 1, :]
    pl.semaphore_wait(barrier, (n_h - 1) + (n_t - 1))

    def piece(index):
        return pl.ds(index * rows, rows)

    def scatter(k):
        return pltpu.make_async_remote_copy(
            src_ref=part.at[piece(h_at(k))],
            dst_ref=piece_in.at[h],
            send_sem=gain_send.at[0, k],
            recv_sem=gain_recv.at[0, k],
            device_id=(t, h_at(k)),
            device_id_type=MESH,
        )

    def exchange(k):
        return pltpu.make_async_remote_copy(
            src_ref=piece_mid.at[t],
            dst_ref=piece_mid.at[t],
            send_sem=gain_send.at[1, k],
            recv_sem=gain_recv.at[1, k],
            device_id=(t_at(k), h),
            device_id_type=MESH,
        )

    def gather(k):
        return pltpu.make_async_remote_copy(
            src_ref=total.at[piece(h)],
            dst_ref=total.at[piece(h)],
            send_sem=gain_send.at[2, k],
            recv_sem=gain_recv.at[2, k],
            device_id=(t, h_at(k)),
            device_id_type=MESH,
        )

    each(n_h - 1, lambda i: scatter(i + 1).start())
    piece_in[h] = part[piece(h)]
    each(n_h - 1, lambda i: scatter(i + 1).wait_recv())
    piece_mid[t] = jnp.sum(piece_in[...], 0)
    each(n_t - 1, lambda i: exchange(i + 1).start())
    each(n_t - 1, lambda i: exchange(i + 1).wait_recv())
    total[piece(h)] = jnp.sum(piece_mid[...], 0)
    each(n_h - 1, lambda i: gather(i + 1).start())
    each(n_h - 1, lambda i: gather(i + 1).wait_recv())
    for row in range(GAIN_ROWS):
        block, rest = divmod(row, 2 * HEADS)
        head, side = divmod(rest, 2)
        out[block, head, side : side + 1, :] = total[row]
    each(n_h - 1, lambda i: scatter(i + 1).wait_send())
    each(n_t - 1, lambda i: exchange(i + 1).wait_send())
    each(n_h - 1, lambda i: gather(i + 1).wait_send())


def place_kernel(grads_in, shifted, sums, grads, sums_out, sem):
    def place(head):
        return pltpu.make_async_copy(
            shifted.at[head],
            grads.at[1, :, :, :, :, pl.ds(pl.multiple_of(head * HD, HD), HD)],
            sem.at[head],
        )

    each(HEADS, lambda head: place(head).start())
    sums_out[...] = sums[...]
    each(HEADS, lambda head: place(head).wait())


def solution(mesh):
    n_t, n_h = mesh.shape["tm"], mesh.shape["height"]
    rows = GAIN_ROWS // n_h
    dma = pltpu.SemaphoreType.DMA
    far = pl.BlockSpec(memory_space=pl.ANY)
    near = pl.BlockSpec(memory_space=pltpu.VMEM)
    window = (WT, WH, WW, HD)
    half_window = (HALF_H, WW, HD)
    sums_shape = jax.ShapeDtypeStruct((HEADS, 2, HD), jnp.float32)
    both_sums_shape = jax.ShapeDtypeStruct((2, HEADS, 2, HD), jnp.float32)

    def shards(saved, gains):
        saved = pltpu.with_memory_space_constraint(saved, pltpu.HBM)
        gains = gains.transpose(0, 2, 1, 3)
        grads_shape = jax.ShapeDtypeStruct((2, 3) + saved.shape[2:], jnp.bfloat16)
        still, still_sums = pl.pallas_call(
            still_kernel,
            grid=(HEADS,),
            out_shape=(grads_shape, sums_shape),
            in_specs=[pl.BlockSpec((1, 4) + window, lambda i: (0, 0, 0, 0, 0, i)), near],
            out_specs=(pl.BlockSpec((1, 3) + window, lambda i: (0, 0, 0, 0, 0, i)), near),
            compiler_params=pltpu.CompilerParams(vmem_limit_bytes=40 * 2**20),
        )(saved, gains)
        shifted, shifted_sums = pl.pallas_call(
            functools.partial(shifted_kernel, n_t, n_h),
            out_shape=(pltpu.VMEM((HEADS, 3) + window, jnp.bfloat16), sums_shape),
            in_specs=[far, near],
            out_specs=(near, near),
            scratch_shapes=[
                pltpu.VMEM((HEADS, 4, 4) + half_window, jnp.bfloat16),
                pltpu.VMEM((HEADS, 3, 3) + half_window, jnp.bfloat16),
                dma((HEADS,)),
                dma((HEADS, 3)),
                dma((HEADS, 3)),
                dma((HEADS, 3)),
                dma((HEADS, 3)),
            ],
            compiler_params=pltpu.CompilerParams(
                collective_id=0, has_side_effects=True, vmem_limit_bytes=40 * 2**20
            ),
        )(saved, gains)
        sums = pl.pallas_call(
            functools.partial(sum_kernel, n_t, n_h),
            out_shape=both_sums_shape,
            in_specs=[near, near],
            out_specs=near,
            scratch_shapes=[
                pltpu.VMEM((GAIN_ROWS, 1, HD), jnp.float32),
                pltpu.VMEM((n_h, rows, 1, HD), jnp.float32),
                pltpu.VMEM((n_t, rows, 1, HD), jnp.float32),
                pltpu.VMEM((GAIN_ROWS, 1, HD), jnp.float32),
                dma((3, max(n_t, n_h))),
                dma((3, max(n_t, n_h))),
            ],
            compiler_params=pltpu.CompilerParams(collective_id=1, has_side_effects=True),
        )(still_sums, shifted_sums)
        grads, sums = pl.pallas_call(
            place_kernel,
            out_shape=(grads_shape, both_sums_shape),
            in_specs=[far, near, near],
            out_specs=(far, near),
            scratch_shapes=[dma((HEADS,))],
            input_output_aliases={0: 0},
        )(still, shifted, sums)
        return grads, sums.transpose(0, 2, 1, 3)

    return jax.shard_map(
        shards,
        mesh=mesh,
        in_specs=(P(None, None, "tm", "height", None, None), P()),
        out_specs=(P(None, None, "tm", "height", None, None), P()),
        check_vma=False,
    )
```

```python
import functools
import math

import jax
import jax.numpy as jnp
from jax import lax
from jax.experimental import pallas as pl
from jax.experimental.pallas import tpu as pltpu
from jax.sharding import PartitionSpec as P

HEADS = 12
HD = 128
WT = 2
WH = 8
WW = 16
HALF_H = WH // 2
TOKENS = WT * WH * WW
ROLES = 4

EPSILON = 1e-06
SCALE = HD ** (-0.5)
EXP2_SCALE = SCALE * math.log2(math.e)

MESH = pl.DeviceIdType.MESH
NT = (((1,), (1,)), ((), ()))
NN = (((1,), (0,)), ((), ()))
TN = (((0,), (0,)), ((), ()))


def matmul(a, b, dims):
    return lax.dot_general(a, b, dims, preferred_element_type=jnp.float32)


def head_grad(q_raw, k_raw, values_in, out_grad, gain_q, gain_k):
    q_full = q_raw.astype(jnp.float32)
    k_full = k_raw.astype(jnp.float32)
    inv_q = lax.rsqrt(jnp.mean(q_full * q_full, -1, keepdims=True) + EPSILON)
    inv_k = lax.rsqrt(jnp.mean(k_full * k_full, -1, keepdims=True) + EPSILON)
    unit_q = q_full * inv_q
    unit_k = k_full * inv_k
    q_norm = (unit_q * gain_q).astype(jnp.bfloat16)
    k_norm = (unit_k * gain_k).astype(jnp.bfloat16)
    scores = matmul(k_norm, q_norm, NT)
    prob_grad = matmul(values_in, out_grad, NT)
    top = jnp.max(scores, 0, keepdims=True)
    probs = jnp.exp2((scores - top) * EXP2_SCALE)
    probs = probs * (1.0 / jnp.sum(probs, 0, keepdims=True))
    delta = jnp.sum(probs * prob_grad, 0, keepdims=True)
    score_grad = (probs * (prob_grad - delta)).astype(jnp.bfloat16)
    value_grad = matmul(probs.astype(jnp.bfloat16), out_grad, NN).astype(jnp.bfloat16)
    kn_grad = matmul(score_grad, q_norm, NN)
    qn_grad = matmul(score_grad, k_norm, TN)

    def raw_grad(norm_grad, unit, inverse, gain):
        along = norm_grad * unit
        gain_grad = jnp.sum(along, 0, keepdims=True) * SCALE
        scaled_gain = gain * SCALE
        mean = jnp.mean(along * scaled_gain, -1, keepdims=True)
        raw = inverse * (norm_grad * scaled_gain - unit * mean)
        return raw.astype(jnp.bfloat16), gain_grad

    q_grad, gain_q_grad = raw_grad(qn_grad, unit_q, inv_q, gain_q)
    k_grad, gain_k_grad = raw_grad(kn_grad, unit_k, inv_k, gain_k)
    return (q_grad, k_grad, value_grad), gain_q_grad, gain_k_grad


def each(count, body):
    lax.fori_loop(0, count, lambda i, carry: (body(i), carry)[1], 0)


def groups(size):
    low = min(size, 4)
    return (1, low), (low, size // low)


def grad_kernel(
    n_t, n_h,
    saved, gains_far, grads, gain_grads,
    x0, x1, w1, gains, sums, stages, totals,
    load_gains, load0, load1, in_send, in_recv, out_send, out_recv, sum_send, sum_recv,
):
    t = lax.axis_index("tm")
    h = lax.axis_index("height")

    def at(dt, dh):
        return (lax.rem(t + dt + n_t, n_t), lax.rem(h + dh + n_h, n_h))

    def features(head):
        return pl.ds(pl.multiple_of(head * HD, HD), HD)

    def unit(u):
        role = lax.rem(u, ROLES)
        return lax.rem(role, 2), role // 2, role * (HEADS // ROLES) + u // ROLES

    def holder(u, slot):
        rt, rh, _ = unit(u)
        return (rt if slot < 2 else 1 - rt), (rh if slot % 2 == 0 else 1 - rh)

    def quadrant(u, slot):
        a, b = holder(u, slot)
        return 1 - a, pl.ds((1 - b) * HALF_H, HALF_H), slice(None), features(unit(u)[2])

    def owner(u, slot):
        (rt, rh, _), (a, b) = unit(u), holder(u, slot)
        return at(a - rt, b - rh)

    def worker(u, slot):
        (rt, rh, _), (a, b) = unit(u), holder(u, slot)
        return at(rt - a, rh - b)

    def in_copy(u, slot):
        return pltpu.make_async_remote_copy(
            src_ref=saved.at[(1, slice(None)) + quadrant(u, slot)],
            dst_ref=x1.at[u, :, slot],
            send_sem=in_send.at[u, slot - 1],
            recv_sem=in_recv.at[u, slot - 1],
            device_id=worker(u, slot),
            device_id_type=MESH,
        )

    def in_local(u):
        return pltpu.make_async_copy(
            saved.at[(1, slice(None)) + quadrant(u, 0)], x1.at[u, :, 0], load1.at[u]
        )

    def out_copy(u, slot):
        return pltpu.make_async_remote_copy(
            src_ref=w1.at[u, :, slot - 1],
            dst_ref=grads.at[(1, slice(None)) + quadrant(u, slot)],
            send_sem=out_send.at[u, slot - 1],
            recv_sem=out_recv.at[u, slot - 1],
            device_id=owner(u, slot),
            device_id_type=MESH,
        )

    def load(a):
        return pltpu.make_async_copy(saved.at[0, a], x0.at[a], load0.at[a])

    (h_low, h_high), (t_low, t_high) = groups(n_h), groups(n_t)
    plan = [("height",) + h_low, ("height",) + h_high, ("tm",) + t_low, ("tm",) + t_high]

    def place(axis, stride, count):
        return lax.rem((h if axis == "height" else t) // stride, count)

    def peer(axis, stride, count, k):
        mine = place(axis, stride, count)
        other = lax.rem(mine + k, count)
        shift = (other - mine) * stride
        return other, (at(0, shift) if axis == "height" else at(shift, 0))

    gains_copy = pltpu.make_async_copy(gains_far, gains, load_gains)
    gains_copy.start()
    each(4, lambda a: load(a).start())
    each(HEADS, lambda u: in_local(u).start())

    barrier = pltpu.get_barrier_semaphore()

    def greet(device):
        pl.semaphore_signal(barrier, inc=1, device_id=device, device_id_type=MESH)

    greeted = 0
    for dt in (-1, 0, 1):
        for dh in (-1, 0, 1):
            if dt or dh:
                greet(at(dt, dh))
                greeted += 1
    for group in plan:
        for k in range(1, group[2]):
            greet(peer(*group, k)[1])
            greeted += 1
    pl.semaphore_wait(barrier, greeted)

    def start_inputs(u):
        for slot in (2, 3, 1):
            in_copy(u, slot).start()

    each(HEADS, start_inputs)
    gains_copy.wait()
    each(4, lambda a: load(a).wait())

    def compute(operands, block, head):
        results, gain_q_grad, gain_k_grad = head_grad(
            *(x.reshape(TOKENS, HD) for x in operands),
            gains[block, head, 0:1, :],
            gains[block, head, 1:2, :],
        )
        sums[block * HEADS + head, 0:1, :] = gain_q_grad
        sums[block * HEADS + head, 1:2, :] = gain_k_grad
        return results

    def step(u):
        results = compute([x0[a, :, :, :, features(u)] for a in range(4)], 0, u)
        for a in range(3):
            grads[0, a, :, :, :, features(u)] = results[a].reshape(WT, WH, WW, HD)
        in_local(u).wait()
        for slot in (1, 2, 3):
            in_copy(u, slot).wait_recv()
        results = compute([x1[u, a] for a in range(4)], 1, unit(u)[2])
        for a in range(3):
            quads = results[a].reshape(4, HALF_H, WW, HD)
            w1[u, a] = quads[1:]
            grads[(1, a) + quadrant(u, 0)] = quads[0]
        for slot in (2, 3, 1):
            out_copy(u, slot).start()

    each(HEADS, step)

    size = 2 * HEADS // h_low[1]

    def sum_copy(index, k):
        other, device = peer(*plan[index % 4], k)
        mine = place(*plan[index % 4])
        if index == 0:
            source, target = sums.at[pl.ds(other * size, size)], stages.at[0, mine]
        elif index < 4:
            source = target = stages.at[index, mine]
        else:
            source = target = totals.at[pl.ds(mine * size, size)]
        return pltpu.make_async_remote_copy(
            src_ref=source,
            dst_ref=target,
            send_sem=sum_send.at[index, k],
            recv_sem=sum_recv.at[index, k],
            device_id=device,
            device_id_type=MESH,
        )

    here = pl.ds(place(*plan[0]) * size, size)
    for index in range(5):
        count = plan[index % 4][2]
        if index == 0:
            value = sums[here]
        if index < 4:
            stages[index, place(*plan[index])] = value
        else:
            totals[here] = value
        for k in range(1, count):
            sum_copy(index, k).start()
        for k in range(1, count):
            sum_copy(index, k).wait_recv()
        if index < 4:
            value = functools.reduce(jnp.add, [stages[index, i] for i in range(count)])
    gain_grads[...] = totals[...].reshape(2, HEADS, 2, HD)
    for index in range(5):
        for k in range(1, plan[index % 4][2]):
            sum_copy(index, k).wait_send()

    def finish(u):
        for slot in (1, 2, 3):
            in_copy(u, slot).wait_send()
            out_copy(u, slot).wait()

    each(HEADS, finish)


def write_kernel(grads_in, sums_in, grads, sums, sem):
    def write(index):
        block, a = index // 3, lax.rem(index, 3)
        return pltpu.make_async_copy(grads_in.at[block, a], grads.at[block, a], sem.at[index])

    each(6, lambda index: write(index).start())
    sums[...] = sums_in[...]
    each(6, lambda index: write(index).wait())


def solution(mesh):
    n_t, n_h = mesh.shape["tm"], mesh.shape["height"]
    dma = pltpu.SemaphoreType.DMA
    far = pl.BlockSpec(memory_space=pl.ANY)
    near = pl.BlockSpec(memory_space=pltpu.VMEM)
    quads = (4, HALF_H, WW, HD)
    gain_shape = jax.ShapeDtypeStruct((2, HEADS, 2, HD), jnp.float32)

    def shards(saved, gains):
        saved = pltpu.with_memory_space_constraint(saved, pltpu.HBM)
        gains = pltpu.with_memory_space_constraint(gains.transpose(0, 2, 1, 3), pltpu.HBM)
        grads_shape = (2, 3) + saved.shape[2:]
        grads, gain_grads = pl.pallas_call(
            functools.partial(grad_kernel, n_t, n_h),
            out_shape=(pltpu.VMEM(grads_shape, jnp.bfloat16), gain_shape),
            in_specs=[far, far],
            out_specs=(near, near),
            scratch_shapes=[
                pltpu.VMEM(saved.shape[1:], jnp.bfloat16),
                pltpu.VMEM((HEADS, 4) + quads, jnp.bfloat16),
                pltpu.VMEM((HEADS, 3, 3) + quads[1:], jnp.bfloat16),
                pltpu.VMEM((2, HEADS, 2, HD), jnp.float32),
                pltpu.VMEM((2 * HEADS, 2, HD), jnp.float32),
                pltpu.VMEM((4, 4, 2 * HEADS // min(n_h, 4), 2, HD), jnp.float32),
                pltpu.VMEM((2 * HEADS, 2, HD), jnp.float32),
                dma,
                dma((4,)),
                dma((HEADS,)),
                dma((HEADS, 3)),
                dma((HEADS, 3)),
                dma((HEADS, 3)),
                dma((HEADS, 3)),
                dma((5, 4)),
                dma((5, 4)),
            ],
            compiler_params=pltpu.CompilerParams(
                collective_id=0, has_side_effects=True, vmem_limit_bytes=40 * 2**20
            ),
        )(saved, gains)
        grads, gain_grads = pl.pallas_call(
            write_kernel,
            out_shape=(jax.ShapeDtypeStruct(grads_shape, jnp.bfloat16), gain_shape),
            in_specs=[near, near],
            out_specs=(far, near),
            scratch_shapes=[dma((6,))],
        )(grads, gain_grads)
        return grads, gain_grads.transpose(0, 2, 1, 3)

    return jax.shard_map(
        shards,
        mesh=mesh,
        in_specs=(P(None, None, "tm", "height", None, None), P()),
        out_specs=(P(None, None, "tm", "height", None, None), P()),
        check_vma=False,
    )
```

```python
import functools
import math

import jax
import jax.numpy as jnp
from jax import lax
from jax.experimental import pallas as pl
from jax.experimental.pallas import tpu as pltpu
from jax.sharding import PartitionSpec as P

HEADS = 12
HD = 128
WT = 2
WH = 8
WW = 16
HALF_H = WH // 2
TOKENS = WT * WH * WW
ROLES = 4
BATCH = 4

EPSILON = 1e-06
SCALE = HD ** (-0.5)
EXP2_SCALE = SCALE * math.log2(math.e)

MESH = pl.DeviceIdType.MESH
NT = (((1,), (1,)), ((), ()))
NN = (((1,), (0,)), ((), ()))
TN = (((0,), (0,)), ((), ()))


def matmul(a, b, dims):
    return lax.dot_general(a, b, dims, preferred_element_type=jnp.float32)


def head_grad(q_raw, k_raw, values_in, out_grad, gain_q, gain_k):
    q_full = q_raw.astype(jnp.float32)
    k_full = k_raw.astype(jnp.float32)
    inv_q = lax.rsqrt(jnp.mean(q_full * q_full, -1, keepdims=True) + EPSILON)
    inv_k = lax.rsqrt(jnp.mean(k_full * k_full, -1, keepdims=True) + EPSILON)
    unit_q = q_full * inv_q
    unit_k = k_full * inv_k
    q_norm = (unit_q * gain_q).astype(jnp.bfloat16)
    k_norm = (unit_k * gain_k).astype(jnp.bfloat16)
    scores = matmul(k_norm, q_norm, NT)
    prob_grad = matmul(values_in, out_grad, NT)
    top = jnp.max(scores, 0, keepdims=True)
    probs = jnp.exp2((scores - top) * EXP2_SCALE)
    probs = probs * (1.0 / jnp.sum(probs, 0, keepdims=True))
    delta = jnp.sum(probs * prob_grad, 0, keepdims=True)
    score_grad = (probs * (prob_grad - delta)).astype(jnp.bfloat16)
    value_grad = matmul(probs.astype(jnp.bfloat16), out_grad, NN).astype(jnp.bfloat16)
    kn_grad = matmul(score_grad, q_norm, NN)
    qn_grad = matmul(score_grad, k_norm, TN)

    def raw_grad(norm_grad, unit, inverse, gain):
        along = norm_grad * unit
        gain_grad = jnp.sum(along, 0, keepdims=True) * SCALE
        scaled_gain = gain * SCALE
        mean = jnp.mean(along * scaled_gain, -1, keepdims=True)
        raw = inverse * (norm_grad * scaled_gain - unit * mean)
        return raw.astype(jnp.bfloat16), gain_grad

    q_grad, gain_q_grad = raw_grad(qn_grad, unit_q, inv_q, gain_q)
    k_grad, gain_k_grad = raw_grad(kn_grad, unit_k, inv_k, gain_k)
    return (q_grad, k_grad, value_grad), gain_q_grad, gain_k_grad


def each(count, body):
    lax.fori_loop(0, count, lambda i, carry: (body(i), carry)[1], 0)


def groups(size):
    low = min(size, 4)
    return (1, low), (low, size // low)


def grad_kernel(
    n_t, n_h,
    saved, gains_far, grads, gain_grads,
    x0, x1, w1, gains, sums, stages, totals,
    load_gains, load0, load1, in_send, in_recv, out_send, out_recv, sum_send, sum_recv,
):
    t = lax.axis_index("tm")
    h = lax.axis_index("height")

    def at(dt, dh):
        return (lax.rem(t + dt + n_t, n_t), lax.rem(h + dh + n_h, n_h))

    def features(head):
        return pl.ds(pl.multiple_of(head * HD, HD), HD)

    def unit(u):
        role = lax.rem(u, ROLES)
        return lax.rem(role, 2), role // 2, role * (HEADS // ROLES) + u // ROLES

    def holder(u, slot):
        rt, rh, _ = unit(u)
        return (rt if slot < 2 else 1 - rt), (rh if slot % 2 == 0 else 1 - rh)

    def quadrant(u, slot):
        a, b = holder(u, slot)
        return 1 - a, pl.ds((1 - b) * HALF_H, HALF_H), slice(None), features(unit(u)[2])

    def owner(u, slot):
        (rt, rh, _), (a, b) = unit(u), holder(u, slot)
        return at(a - rt, b - rh)

    def worker(u, slot):
        (rt, rh, _), (a, b) = unit(u), holder(u, slot)
        return at(rt - a, rh - b)

    def in_copy(u, slot):
        return pltpu.make_async_remote_copy(
            src_ref=saved.at[(1, slice(None)) + quadrant(u, slot)],
            dst_ref=x1.at[u, :, slot],
            send_sem=in_send.at[u, slot - 1],
            recv_sem=in_recv.at[u, slot - 1],
            device_id=worker(u, slot),
            device_id_type=MESH,
        )

    def in_local(u):
        return pltpu.make_async_copy(
            saved.at[(1, slice(None)) + quadrant(u, 0)], x1.at[u, :, 0], load1.at[u]
        )

    def out_copy(u, slot):
        return pltpu.make_async_remote_copy(
            src_ref=w1.at[u, :, slot - 1],
            dst_ref=grads.at[(1, slice(None)) + quadrant(u, slot)],
            send_sem=out_send.at[u, slot - 1],
            recv_sem=out_recv.at[u, slot - 1],
            device_id=owner(u, slot),
            device_id_type=MESH,
        )

    def load(a):
        return pltpu.make_async_copy(saved.at[0, a], x0.at[a], load0.at[a])

    (h_low, h_high), (t_low, t_high) = groups(n_h), groups(n_t)
    plan = [("height",) + h_low, ("height",) + h_high, ("tm",) + t_low, ("tm",) + t_high]

    def place(axis, stride, count):
        return lax.rem((h if axis == "height" else t) // stride, count)

    def peer(axis, stride, count, k):
        mine = place(axis, stride, count)
        other = lax.rem(mine + k, count)
        shift = (other - mine) * stride
        return other, (at(0, shift) if axis == "height" else at(shift, 0))

    gains_copy = pltpu.make_async_copy(gains_far, gains, load_gains)
    gains_copy.start()
    each(4, lambda a: load(a).start())
    each(HEADS, lambda u: in_local(u).start())

    barrier = pltpu.get_barrier_semaphore()

    def greet(device):
        pl.semaphore_signal(barrier, inc=1, device_id=device, device_id_type=MESH)

    greeted = 0
    for dt in (-1, 0, 1):
        for dh in (-1, 0, 1):
            if dt or dh:
                greet(at(dt, dh))
                greeted += 1
    for group in plan:
        for k in range(1, group[2]):
            greet(peer(*group, k)[1])
            greeted += 1
    pl.semaphore_wait(barrier, greeted)

    def start_inputs(u):
        for slot in (2, 3, 1):
            in_copy(u, slot).start()

    each(HEADS, start_inputs)
    gains_copy.wait()
    each(4, lambda a: load(a).wait())

    def compute(operands, block, head):
        results, gain_q_grad, gain_k_grad = head_grad(
            *(x.reshape(TOKENS, HD) for x in operands),
            gains[block, head, 0:1, :],
            gains[block, head, 1:2, :],
        )
        sums[block * HEADS + head, 0:1, :] = gain_q_grad
        sums[block * HEADS + head, 1:2, :] = gain_k_grad
        return results

    def step(u):
        results = compute([x0[a, :, :, :, features(u)] for a in range(4)], 0, u)
        for a in range(3):
            grads[0, a, :, :, :, features(u)] = results[a].reshape(WT, WH, WW, HD)
        in_local(u).wait()
        for slot in (1, 2, 3):
            in_copy(u, slot).wait_recv()
        results = compute([x1[u, a] for a in range(4)], 1, unit(u)[2])
        for a in range(3):
            quads = results[a].reshape(4, HALF_H, WW, HD)
            w1[u, a] = quads[1:]
            grads[(1, a) + quadrant(u, 0)] = quads[0]

        def start_outputs(v):
            for slot in (2, 3, 1):
                out_copy(v, slot).start()

        @pl.when(u >= HEADS - HEADS // BATCH)
        def _():
            first = (u - (HEADS - HEADS // BATCH)) * BATCH
            each(BATCH, lambda i: start_outputs(first + i))

    each(HEADS, step)

    size = 2 * HEADS // h_low[1]

    def sum_copy(index, k):
        other, device = peer(*plan[index % 4], k)
        mine = place(*plan[index % 4])
        if index == 0:
            source, target = sums.at[pl.ds(other * size, size)], stages.at[0, mine]
        elif index < 4:
            source = target = stages.at[index, mine]
        else:
            source = target = totals.at[pl.ds(mine * size, size)]
        return pltpu.make_async_remote_copy(
            src_ref=source,
            dst_ref=target,
            send_sem=sum_send.at[index, k],
            recv_sem=sum_recv.at[index, k],
            device_id=device,
            device_id_type=MESH,
        )

    here = pl.ds(place(*plan[0]) * size, size)
    for index in range(5):
        count = plan[index % 4][2]
        if index == 0:
            value = sums[here]
        if index < 4:
            stages[index, place(*plan[index])] = value
        else:
            totals[here] = value
        for k in range(1, count):
            sum_copy(index, k).start()
        for k in range(1, count):
            sum_copy(index, k).wait_recv()
        if index < 4:
            value = functools.reduce(jnp.add, [stages[index, i] for i in range(count)])
    gain_grads[...] = totals[...].reshape(2, HEADS, 2, HD)
    for index in range(5):
        for k in range(1, plan[index % 4][2]):
            sum_copy(index, k).wait_send()

    def finish(u):
        for slot in (1, 2, 3):
            in_copy(u, slot).wait_send()
            out_copy(u, slot).wait()

    each(HEADS, finish)


def solution(mesh):
    n_t, n_h = mesh.shape["tm"], mesh.shape["height"]
    dma = pltpu.SemaphoreType.DMA
    far = pl.BlockSpec(memory_space=pl.ANY)
    near = pl.BlockSpec(memory_space=pltpu.VMEM)
    quads = (4, HALF_H, WW, HD)
    gain_shape = jax.ShapeDtypeStruct((2, HEADS, 2, HD), jnp.float32)

    def shards(saved, gains):
        saved = pltpu.with_memory_space_constraint(saved, pltpu.HBM)
        gains = pltpu.with_memory_space_constraint(gains.transpose(0, 2, 1, 3), pltpu.HBM)
        grads_shape = (2, 3) + saved.shape[2:]
        grads, gain_grads = pl.pallas_call(
            functools.partial(grad_kernel, n_t, n_h),
            out_shape=(pltpu.VMEM(grads_shape, jnp.bfloat16), gain_shape),
            in_specs=[far, far],
            out_specs=(near, near),
            scratch_shapes=[
                pltpu.VMEM(saved.shape[1:], jnp.bfloat16),
                pltpu.VMEM((HEADS, 4) + quads, jnp.bfloat16),
                pltpu.VMEM((HEADS, 3, 3) + quads[1:], jnp.bfloat16),
                pltpu.VMEM((2, HEADS, 2, HD), jnp.float32),
                pltpu.VMEM((2 * HEADS, 2, HD), jnp.float32),
                pltpu.VMEM((4, 4, 2 * HEADS // min(n_h, 4), 2, HD), jnp.float32),
                pltpu.VMEM((2 * HEADS, 2, HD), jnp.float32),
                dma,
                dma((4,)),
                dma((HEADS,)),
                dma((HEADS, 3)),
                dma((HEADS, 3)),
                dma((HEADS, 3)),
                dma((HEADS, 3)),
                dma((5, 4)),
                dma((5, 4)),
            ],
            compiler_params=pltpu.CompilerParams(
                collective_id=0, has_side_effects=True, vmem_limit_bytes=40 * 2**20
            ),
        )(saved, gains)
        return grads, gain_grads.transpose(0, 2, 1, 3)

    return jax.shard_map(
        shards,
        mesh=mesh,
        in_specs=(P(None, None, "tm", "height", None, None), P()),
        out_specs=(P(None, None, "tm", "height", None, None), P()),
        check_vma=False,
    )
```

```python
import functools
import math

import jax
import jax.numpy as jnp
from jax import lax
from jax.experimental import pallas as pl
from jax.experimental.pallas import tpu as pltpu
from jax.sharding import PartitionSpec as P

HEADS = 12
HD = 128
WT = 2
WH = 8
WW = 16
HALF_H = WH // 2
TOKENS = WT * WH * WW
ROLES = 4

EPSILON = 1e-06
SCALE = HD ** (-0.5)
EXP2_SCALE = SCALE * math.log2(math.e)

MESH = pl.DeviceIdType.MESH
NT = (((1,), (1,)), ((), ()))
NN = (((1,), (0,)), ((), ()))
TN = (((0,), (0,)), ((), ()))


def matmul(a, b, dims):
    return lax.dot_general(a, b, dims, preferred_element_type=jnp.float32)


def head_grad(q_raw, k_raw, values_in, out_grad, gain_q, gain_k):
    q_full = q_raw.astype(jnp.float32)
    k_full = k_raw.astype(jnp.float32)
    inv_q = lax.rsqrt(jnp.mean(q_full * q_full, -1, keepdims=True) + EPSILON)
    inv_k = lax.rsqrt(jnp.mean(k_full * k_full, -1, keepdims=True) + EPSILON)
    unit_q = q_full * inv_q
    unit_k = k_full * inv_k
    q_norm = (unit_q * gain_q).astype(jnp.bfloat16)
    k_norm = (unit_k * gain_k).astype(jnp.bfloat16)
    scores = matmul(k_norm, q_norm, NT)
    prob_grad = matmul(values_in, out_grad, NT)
    top = jnp.max(scores, 0, keepdims=True)
    probs = jnp.exp2((scores - top) * EXP2_SCALE)
    probs = probs * (1.0 / jnp.sum(probs, 0, keepdims=True))
    delta = jnp.sum(probs * prob_grad, 0, keepdims=True)
    score_grad = (probs * (prob_grad - delta)).astype(jnp.bfloat16)
    value_grad = matmul(probs.astype(jnp.bfloat16), out_grad, NN).astype(jnp.bfloat16)
    kn_grad = matmul(score_grad, q_norm, NN)
    qn_grad = matmul(score_grad, k_norm, TN)

    def raw_grad(norm_grad, unit, inverse, gain):
        along = norm_grad * unit
        gain_grad = jnp.sum(along, 0, keepdims=True) * SCALE
        scaled_gain = gain * SCALE
        mean = jnp.mean(along * scaled_gain, -1, keepdims=True)
        raw = inverse * (norm_grad * scaled_gain - unit * mean)
        return raw.astype(jnp.bfloat16), gain_grad

    q_grad, gain_q_grad = raw_grad(qn_grad, unit_q, inv_q, gain_q)
    k_grad, gain_k_grad = raw_grad(kn_grad, unit_k, inv_k, gain_k)
    return (q_grad, k_grad, value_grad), gain_q_grad, gain_k_grad


def each(count, body):
    lax.fori_loop(0, count, lambda i, carry: (body(i), carry)[1], 0)


def groups(size):
    low = min(size, 4)
    return (1, low), (low, size // low)


def grad_kernel(
    n_t, n_h,
    saved, gains_far, grads, sums,
    x0, x1, w1, gains,
    load_gains, load0, load1, in_send, in_recv, out_send, out_recv,
):
    t = lax.axis_index("tm")
    h = lax.axis_index("height")

    def at(dt, dh):
        return (lax.rem(t + dt + n_t, n_t), lax.rem(h + dh + n_h, n_h))

    def features(head):
        return pl.ds(pl.multiple_of(head * HD, HD), HD)

    def unit(u):
        role = lax.rem(u, ROLES)
        return lax.rem(role, 2), role // 2, role * (HEADS // ROLES) + u // ROLES

    def holder(u, slot):
        rt, rh, _ = unit(u)
        return (rt if slot < 2 else 1 - rt), (rh if slot % 2 == 0 else 1 - rh)

    def quadrant(u, slot):
        a, b = holder(u, slot)
        return 1 - a, pl.ds((1 - b) * HALF_H, HALF_H), slice(None), features(unit(u)[2])

    def owner(u, slot):
        (rt, rh, _), (a, b) = unit(u), holder(u, slot)
        return at(a - rt, b - rh)

    def worker(u, slot):
        (rt, rh, _), (a, b) = unit(u), holder(u, slot)
        return at(rt - a, rh - b)

    def in_copy(u, slot):
        return pltpu.make_async_remote_copy(
            src_ref=saved.at[(1, slice(None)) + quadrant(u, slot)],
            dst_ref=x1.at[u, :, slot],
            send_sem=in_send.at[u, slot - 1],
            recv_sem=in_recv.at[u, slot - 1],
            device_id=worker(u, slot),
            device_id_type=MESH,
        )

    def in_local(u):
        return pltpu.make_async_copy(
            saved.at[(1, slice(None)) + quadrant(u, 0)], x1.at[u, :, 0], load1.at[u]
        )

    def out_copy(u, slot):
        return pltpu.make_async_remote_copy(
            src_ref=w1.at[u, :, slot - 1],
            dst_ref=grads.at[(1, slice(None)) + quadrant(u, slot)],
            send_sem=out_send.at[u, slot - 1],
            recv_sem=out_recv.at[u, slot - 1],
            device_id=owner(u, slot),
            device_id_type=MESH,
        )

    def load(a):
        return pltpu.make_async_copy(saved.at[0, a], x0.at[a], load0.at[a])

    gains_copy = pltpu.make_async_copy(gains_far, gains, load_gains)
    gains_copy.start()
    each(4, lambda a: load(a).start())
    each(HEADS, lambda u: in_local(u).start())

    barrier = pltpu.get_barrier_semaphore()

    def greet(device):
        pl.semaphore_signal(barrier, inc=1, device_id=device, device_id_type=MESH)

    greeted = 0
    for dt in (-1, 0, 1):
        for dh in (-1, 0, 1):
            if dt or dh:
                greet(at(dt, dh))
                greeted += 1
    pl.semaphore_wait(barrier, greeted)

    def start_inputs(u):
        for slot in (2, 3, 1):
            in_copy(u, slot).start()

    each(HEADS, start_inputs)
    gains_copy.wait()
    each(4, lambda a: load(a).wait())

    def compute(operands, block, head):
        results, gain_q_grad, gain_k_grad = head_grad(
            *(x.reshape(TOKENS, HD) for x in operands),
            gains[block, head, 0:1, :],
            gains[block, head, 1:2, :],
        )
        sums[block * HEADS + head, 0:1, :] = gain_q_grad
        sums[block * HEADS + head, 1:2, :] = gain_k_grad
        return results

    def step(u):
        results = compute([x0[a, :, :, :, features(u)] for a in range(4)], 0, u)
        for a in range(3):
            grads[0, a, :, :, :, features(u)] = results[a].reshape(WT, WH, WW, HD)
        in_local(u).wait()
        for slot in (1, 2, 3):
            in_copy(u, slot).wait_recv()
        results = compute([x1[u, a] for a in range(4)], 1, unit(u)[2])
        for a in range(3):
            quads = results[a].reshape(4, HALF_H, WW, HD)
            w1[u, a] = quads[1:]
            grads[(1, a) + quadrant(u, 0)] = quads[0]

        for slot in (2, 3, 1):
            out_copy(u, slot).start()

    each(HEADS, step)

    def finish(u):
        for slot in (1, 2, 3):
            in_copy(u, slot).wait_send()
            out_copy(u, slot).wait()

    each(HEADS, finish)


def sum_kernel(n_t, n_h, sums, gain_grads, stages, totals, sum_send, sum_recv):
    t = lax.axis_index("tm")
    h = lax.axis_index("height")

    def at(dt, dh):
        return (lax.rem(t + dt + n_t, n_t), lax.rem(h + dh + n_h, n_h))

    (h_low, h_high), (t_low, t_high) = groups(n_h), groups(n_t)
    plan = [("height",) + h_low, ("height",) + h_high, ("tm",) + t_low, ("tm",) + t_high]

    def place(axis, stride, count):
        return lax.rem((h if axis == "height" else t) // stride, count)

    def peer(axis, stride, count, k):
        mine = place(axis, stride, count)
        other = lax.rem(mine + k, count)
        shift = (other - mine) * stride
        return other, (at(0, shift) if axis == "height" else at(shift, 0))

    barrier = pltpu.get_barrier_semaphore()
    greeted = 0
    for group in plan:
        for k in range(1, group[2]):
            device = peer(*group, k)[1]
            pl.semaphore_signal(barrier, inc=1, device_id=device, device_id_type=MESH)
            greeted += 1
    pl.semaphore_wait(barrier, greeted)

    size = 2 * HEADS // h_low[1]

    def sum_copy(index, k):
        other, device = peer(*plan[index % 4], k)
        mine = place(*plan[index % 4])
        if index == 0:
            source, target = sums.at[pl.ds(other * size, size)], stages.at[0, mine]
        elif index < 4:
            source = target = stages.at[index, mine]
        else:
            source = target = totals.at[pl.ds(mine * size, size)]
        return pltpu.make_async_remote_copy(
            src_ref=source,
            dst_ref=target,
            send_sem=sum_send.at[index, k],
            recv_sem=sum_recv.at[index, k],
            device_id=device,
            device_id_type=MESH,
        )

    here = pl.ds(place(*plan[0]) * size, size)
    for index in range(5):
        count = plan[index % 4][2]
        if index == 0:
            value = sums[here]
        if index < 4:
            stages[index, place(*plan[index])] = value
        else:
            totals[here] = value
        for k in range(1, count):
            sum_copy(index, k).start()
        for k in range(1, count):
            sum_copy(index, k).wait_recv()
        if index < 4:
            value = functools.reduce(jnp.add, [stages[index, i] for i in range(count)])
    gain_grads[...] = totals[...].reshape(2, HEADS, 2, HD)
    for index in range(5):
        for k in range(1, plan[index % 4][2]):
            sum_copy(index, k).wait_send()


def solution(mesh):
    n_t, n_h = mesh.shape["tm"], mesh.shape["height"]
    dma = pltpu.SemaphoreType.DMA
    far = pl.BlockSpec(memory_space=pl.ANY)
    near = pl.BlockSpec(memory_space=pltpu.VMEM)
    quads = (4, HALF_H, WW, HD)
    gain_shape = jax.ShapeDtypeStruct((2, HEADS, 2, HD), jnp.float32)

    def shards(saved, gains):
        saved = pltpu.with_memory_space_constraint(saved, pltpu.HBM)
        gains = pltpu.with_memory_space_constraint(gains.transpose(0, 2, 1, 3), pltpu.HBM)
        grads_shape = (2, 3) + saved.shape[2:]
        grads, sums = pl.pallas_call(
            functools.partial(grad_kernel, n_t, n_h),
            out_shape=(
                pltpu.VMEM(grads_shape, jnp.bfloat16),
                pltpu.VMEM((2 * HEADS, 2, HD), jnp.float32),
            ),
            in_specs=[far, far],
            out_specs=(near, near),
            scratch_shapes=[
                pltpu.VMEM(saved.shape[1:], jnp.bfloat16),
                pltpu.VMEM((HEADS, 4) + quads, jnp.bfloat16),
                pltpu.VMEM((HEADS, 3, 3) + quads[1:], jnp.bfloat16),
                pltpu.VMEM((2, HEADS, 2, HD), jnp.float32),
                dma,
                dma((4,)),
                dma((HEADS,)),
                dma((HEADS, 3)),
                dma((HEADS, 3)),
                dma((HEADS, 3)),
                dma((HEADS, 3)),
            ],
            compiler_params=pltpu.CompilerParams(
                collective_id=0, has_side_effects=True, vmem_limit_bytes=40 * 2**20
            ),
        )(saved, gains)
        gain_grads = pl.pallas_call(
            functools.partial(sum_kernel, n_t, n_h),
            out_shape=gain_shape,
            in_specs=[near],
            out_specs=near,
            scratch_shapes=[
                pltpu.VMEM((4, 4, 2 * HEADS // min(n_h, 4), 2, HD), jnp.float32),
                pltpu.VMEM((2 * HEADS, 2, HD), jnp.float32),
                dma((5, 4)),
                dma((5, 4)),
            ],
            compiler_params=pltpu.CompilerParams(collective_id=1, has_side_effects=True),
        )(pltpu.with_memory_space_constraint(sums, pltpu.VMEM))
        return grads, gain_grads.transpose(0, 2, 1, 3)

    return jax.shard_map(
        shards,
        mesh=mesh,
        in_specs=(P(None, None, "tm", "height", None, None), P()),
        out_specs=(P(None, None, "tm", "height", None, None), P()),
        check_vma=False,
    )
```

```python
import functools
import math

import jax
import jax.numpy as jnp
from jax import lax
from jax.experimental import pallas as pl
from jax.experimental.pallas import tpu as pltpu
from jax.sharding import PartitionSpec as P

HEADS = 12
HD = 128
WT = 2
WH = 8
WW = 16
HALF_H = WH // 2
TOKENS = WT * WH * WW
ROLES = 4
HELD = 3
GROUP = 8

EPSILON = 1e-06
SCALE = HD ** (-0.5)
EXP2_SCALE = SCALE * math.log2(math.e)

MESH = pl.DeviceIdType.MESH
NT = (((1,), (1,)), ((), ()))
NN = (((1,), (0,)), ((), ()))
TN = (((0,), (0,)), ((), ()))


def matmul(a, b, dims):
    return lax.dot_general(a, b, dims, preferred_element_type=jnp.float32)


def head_grad(q_raw, k_raw, values_in, out_grad, gain_q, gain_k):
    q_full = q_raw.astype(jnp.float32)
    k_full = k_raw.astype(jnp.float32)
    inv_q = lax.rsqrt(jnp.mean(q_full * q_full, -1, keepdims=True) + EPSILON)
    inv_k = lax.rsqrt(jnp.mean(k_full * k_full, -1, keepdims=True) + EPSILON)
    unit_q = q_full * inv_q
    unit_k = k_full * inv_k
    q_norm = (unit_q * gain_q).astype(jnp.bfloat16)
    k_norm = (unit_k * gain_k).astype(jnp.bfloat16)
    scores = matmul(k_norm, q_norm, NT)
    prob_grad = matmul(values_in, out_grad, NT)
    top = jnp.max(scores, 0, keepdims=True)
    probs = jnp.exp2((scores - top) * EXP2_SCALE)
    probs = probs * (1.0 / jnp.sum(probs, 0, keepdims=True))
    delta = jnp.sum(probs * prob_grad, 0, keepdims=True)
    score_grad = (probs * (prob_grad - delta)).astype(jnp.bfloat16)
    value_grad = matmul(probs.astype(jnp.bfloat16), out_grad, NN).astype(jnp.bfloat16)
    kn_grad = matmul(score_grad, q_norm, NN)
    qn_grad = matmul(score_grad, k_norm, TN)

    def raw_grad(norm_grad, unit, inverse, gain):
        along = norm_grad * unit
        gain_grad = jnp.sum(along, 0, keepdims=True) * SCALE
        scaled_gain = gain * SCALE
        mean = jnp.mean(along * scaled_gain, -1, keepdims=True)
        raw = inverse * (norm_grad * scaled_gain - unit * mean)
        return raw.astype(jnp.bfloat16), gain_grad

    q_grad, gain_q_grad = raw_grad(qn_grad, unit_q, inv_q, gain_q)
    k_grad, gain_k_grad = raw_grad(kn_grad, unit_k, inv_k, gain_k)
    return (q_grad, k_grad, value_grad), gain_q_grad, gain_k_grad


def each(count, body):
    lax.fori_loop(0, count, lambda i, carry: (body(i), carry)[1], 0)


def grad_kernel(
    n_t, n_h,
    saved, gains_far, grads, gain_grads,
    x0, x1, w1, gains, sums, stages, totals,
    load_gains, load0, load1, in_send, in_recv, out_send, out_recv, sum_send, sum_recv,
):
    t = lax.axis_index("tm")
    h = lax.axis_index("height")

    def at(dt, dh):
        return (lax.rem(t + dt + n_t, n_t), lax.rem(h + dh + n_h, n_h))

    def features(head):
        return pl.ds(pl.multiple_of(head * HD, HD), HD)

    def unit(u):
        role = lax.rem(u, ROLES)
        return lax.rem(role, 2), role // 2, role * (HEADS // ROLES) + u // ROLES

    def holder(u, slot):
        rt, rh, _ = unit(u)
        return (rt if slot < 2 else 1 - rt), (rh if slot % 2 == 0 else 1 - rh)

    def quadrant(u, slot):
        a, b = holder(u, slot)
        return 1 - a, pl.ds((1 - b) * HALF_H, HALF_H), slice(None), features(unit(u)[2])

    def owner(u, slot):
        (rt, rh, _), (a, b) = unit(u), holder(u, slot)
        return at(a - rt, b - rh)

    def worker(u, slot):
        (rt, rh, _), (a, b) = unit(u), holder(u, slot)
        return at(rt - a, rh - b)

    def in_copy(u, slot):
        return pltpu.make_async_remote_copy(
            src_ref=saved.at[(1, slice(None)) + quadrant(u, slot)],
            dst_ref=x1.at[u, :, slot],
            send_sem=in_send.at[u, slot - 1],
            recv_sem=in_recv.at[u, slot - 1],
            device_id=worker(u, slot),
            device_id_type=MESH,
        )

    def in_local(u):
        return pltpu.make_async_copy(
            saved.at[(1, slice(None)) + quadrant(u, 0)], x1.at[u, :, 0], load1.at[u]
        )

    def out_copy(u, slot):
        return pltpu.make_async_remote_copy(
            src_ref=w1.at[u, :, slot - 1],
            dst_ref=grads.at[(1, slice(None)) + quadrant(u, slot)],
            send_sem=out_send.at[u, slot - 1],
            recv_sem=out_recv.at[u, slot - 1],
            device_id=owner(u, slot),
            device_id_type=MESH,
        )

    def load(a):
        return pltpu.make_async_copy(saved.at[0, a], x0.at[a], load0.at[a])

    near_h, near_t = min(n_h, GROUP), min(n_t, GROUP)
    far_h, far_t = n_h // near_h, n_t // near_t
    counts = (near_h, far_h * far_t, near_t, near_h)

    def place(stage):
        if stage == 1:
            return t // near_t * far_h + h // near_h
        return lax.rem(t, near_t) if stage == 2 else lax.rem(h, near_h)

    def peer(stage, k):
        if stage == 1:
            other_t = lax.rem(t // near_t + k // far_h, far_t)
            other_h = lax.rem(h // near_h + lax.rem(k, far_h), far_h)
            return other_t * far_h + other_h, (
                other_t * near_t + lax.rem(t, near_t),
                other_h * near_h + lax.rem(h, near_h),
            )
        other = lax.rem(place(stage) + k, counts[stage])
        shift = other - place(stage)
        return other, ((t + shift, h) if stage == 2 else (t, h + shift))

    gains_copy = pltpu.make_async_copy(gains_far, gains, load_gains)
    gains_copy.start()
    each(4, lambda a: load(a).start())
    each(HEADS, lambda u: in_local(u).start())

    barrier = pltpu.get_barrier_semaphore()

    def greet(device):
        pl.semaphore_signal(barrier, inc=1, device_id=device, device_id_type=MESH)

    greeted = 0
    for dt in (-1, 0, 1):
        for dh in (-1, 0, 1):
            if dt or dh:
                greet(at(dt, dh))
                greeted += 1
    for stage in range(3):
        for k in range(1, counts[stage]):
            greet(peer(stage, k)[1])
            greeted += 1
    pl.semaphore_wait(barrier, greeted)

    def start_inputs(u):
        for slot in (2, 3, 1):
            in_copy(u, slot).start()

    each(HEADS, start_inputs)
    gains_copy.wait()
    each(4, lambda a: load(a).wait())

    def compute(operands, block, head):
        results, gain_q_grad, gain_k_grad = head_grad(
            *(x.reshape(TOKENS, HD) for x in operands),
            gains[block, head, 0:1, :],
            gains[block, head, 1:2, :],
        )
        sums[block * HEADS + head, 0:1, :] = gain_q_grad
        sums[block * HEADS + head, 1:2, :] = gain_k_grad
        return results

    def start_outputs(u):
        for slot in (2, 3, 1):
            out_copy(u, slot).start()

    def step(u):
        results = compute([x0[a, :, :, :, features(u)] for a in range(4)], 0, u)
        for a in range(3):
            grads[0, a, :, :, :, features(u)] = results[a].reshape(WT, WH, WW, HD)
        in_local(u).wait()
        for slot in (1, 2, 3):
            in_copy(u, slot).wait_recv()
        results = compute([x1[u, a] for a in range(4)], 1, unit(u)[2])
        for a in range(3):
            quads = results[a].reshape(4, HALF_H, WW, HD)
            w1[u, a] = quads[1:]
            grads[(1, a) + quadrant(u, 0)] = quads[0]

        @pl.when(u >= HEADS - HELD)
        def _():
            start_outputs(2 * (u - HEADS + HELD))
            start_outputs(2 * (u - HEADS + HELD) + 1)

    each(HEADS, step)

    size = 2 * HEADS // near_h

    def sum_copy(stage, k):
        other, device = peer(stage, k)
        mine = place(stage)
        if stage == 0:
            source, target = sums.at[pl.ds(other * size, size)], stages.at[0, mine]
        elif stage < 3:
            source = target = stages.at[stage, mine]
        else:
            source = target = totals.at[pl.ds(mine * size, size)]
        return pltpu.make_async_remote_copy(
            src_ref=source,
            dst_ref=target,
            send_sem=sum_send.at[stage, k],
            recv_sem=sum_recv.at[stage, k],
            device_id=device,
            device_id_type=MESH,
        )

    here = pl.ds(place(0) * size, size)
    value = sums[here]
    sent = 2 * HELD
    for stage in range(4):
        count = counts[stage]
        if stage < 3:
            stages[stage, place(stage)] = value
        else:
            totals[here] = value
        for k in range(1, count):
            sum_copy(stage, k).start()
        batch = -(-(HEADS - sent) // (4 - stage))
        for u in range(sent, sent + batch):
            start_outputs(u)
        sent += batch
        for k in range(1, count):
            sum_copy(stage, k).wait_recv()
        if stage < 3:
            value = functools.reduce(jnp.add, [stages[stage, i] for i in range(count)])
    gain_grads[...] = totals[...].reshape(2, HEADS, 2, HD)
    for stage in range(4):
        for k in range(1, counts[stage]):
            sum_copy(stage, k).wait_send()

    def finish(u):
        for slot in (1, 2, 3):
            in_copy(u, slot).wait_send()
            out_copy(u, slot).wait()

    each(HEADS, finish)


def solution(mesh):
    n_t, n_h = mesh.shape["tm"], mesh.shape["height"]
    dma = pltpu.SemaphoreType.DMA
    far = pl.BlockSpec(memory_space=pl.ANY)
    near = pl.BlockSpec(memory_space=pltpu.VMEM)
    quads = (4, HALF_H, WW, HD)
    gain_shape = jax.ShapeDtypeStruct((2, HEADS, 2, HD), jnp.float32)

    def shards(saved, gains):
        saved = pltpu.with_memory_space_constraint(saved, pltpu.HBM)
        gains = pltpu.with_memory_space_constraint(gains.transpose(0, 2, 1, 3), pltpu.HBM)
        grads_shape = (2, 3) + saved.shape[2:]
        grads, gain_grads = pl.pallas_call(
            functools.partial(grad_kernel, n_t, n_h),
            out_shape=(pltpu.VMEM(grads_shape, jnp.bfloat16), gain_shape),
            in_specs=[far, far],
            out_specs=(near, near),
            scratch_shapes=[
                pltpu.VMEM(saved.shape[1:], jnp.bfloat16),
                pltpu.VMEM((HEADS, 4) + quads, jnp.bfloat16),
                pltpu.VMEM((HEADS, 3, 3) + quads[1:], jnp.bfloat16),
                pltpu.VMEM((2, HEADS, 2, HD), jnp.float32),
                pltpu.VMEM((2 * HEADS, 2, HD), jnp.float32),
                pltpu.VMEM((3, GROUP, 2 * HEADS // min(n_h, GROUP), 2, HD), jnp.float32),
                pltpu.VMEM((2 * HEADS, 2, HD), jnp.float32),
                dma,
                dma((4,)),
                dma((HEADS,)),
                dma((HEADS, 3)),
                dma((HEADS, 3)),
                dma((HEADS, 3)),
                dma((HEADS, 3)),
                dma((4, GROUP)),
                dma((4, GROUP)),
            ],
            compiler_params=pltpu.CompilerParams(
                collective_id=0, has_side_effects=True, vmem_limit_bytes=40 * 2**20
            ),
        )(saved, gains)
        return grads, gain_grads.transpose(0, 2, 1, 3)

    return jax.shard_map(
        shards,
        mesh=mesh,
        in_specs=(P(None, None, "tm", "height", None, None), P()),
        out_specs=(P(None, None, "tm", "height", None, None), P()),
        check_vma=False,
    )
```

```python
import functools
import math

import jax
import jax.numpy as jnp
from jax import lax
from jax.experimental import pallas as pl
from jax.experimental.pallas import tpu as pltpu
from jax.sharding import PartitionSpec as P

HEADS = 12
HD = 128
WT = 2
WH = 8
WW = 16
HALF_H = WH // 2
TOKENS = WT * WH * WW
ROLES = 4
GROUP = 8

EPSILON = 1e-06
SCALE = HD ** (-0.5)
EXP2_SCALE = SCALE * math.log2(math.e)

MESH = pl.DeviceIdType.MESH
NT = (((1,), (1,)), ((), ()))
NN = (((1,), (0,)), ((), ()))
TN = (((0,), (0,)), ((), ()))


def matmul(a, b, dims):
    return lax.dot_general(a, b, dims, preferred_element_type=jnp.float32)


def head_grad(q_raw, k_raw, values_in, out_grad, gain_q, gain_k):
    q_full = q_raw.astype(jnp.float32)
    k_full = k_raw.astype(jnp.float32)
    inv_q = lax.rsqrt(jnp.mean(q_full * q_full, -1, keepdims=True) + EPSILON)
    inv_k = lax.rsqrt(jnp.mean(k_full * k_full, -1, keepdims=True) + EPSILON)
    unit_q = q_full * inv_q
    unit_k = k_full * inv_k
    q_norm = (unit_q * gain_q).astype(jnp.bfloat16)
    k_norm = (unit_k * gain_k).astype(jnp.bfloat16)
    scores = matmul(k_norm, q_norm, NT)
    prob_grad = matmul(values_in, out_grad, NT)
    top = jnp.max(scores, 0, keepdims=True)
    probs = jnp.exp2((scores - top) * EXP2_SCALE)
    probs = probs * (1.0 / jnp.sum(probs, 0, keepdims=True))
    delta = jnp.sum(probs * prob_grad, 0, keepdims=True)
    score_grad = (probs * (prob_grad - delta)).astype(jnp.bfloat16)
    value_grad = matmul(probs.astype(jnp.bfloat16), out_grad, NN).astype(jnp.bfloat16)
    kn_grad = matmul(score_grad, q_norm, NN)
    qn_grad = matmul(score_grad, k_norm, TN)

    def raw_grad(norm_grad, unit, inverse, gain):
        along = norm_grad * unit
        gain_grad = jnp.sum(along, 0, keepdims=True) * SCALE
        scaled_gain = gain * SCALE
        mean = jnp.mean(along * scaled_gain, -1, keepdims=True)
        raw = inverse * (norm_grad * scaled_gain - unit * mean)
        return raw.astype(jnp.bfloat16), gain_grad

    q_grad, gain_q_grad = raw_grad(qn_grad, unit_q, inv_q, gain_q)
    k_grad, gain_k_grad = raw_grad(kn_grad, unit_k, inv_k, gain_k)
    return (q_grad, k_grad, value_grad), gain_q_grad, gain_k_grad


def each(count, body):
    lax.fori_loop(0, count, lambda i, carry: (body(i), carry)[1], 0)


def grad_kernel(
    n_t, n_h,
    saved, gains_far, grads, gain_grads,
    x0, x1, w1, gains, sums, stages, totals,
    load_gains, load0, load1, in_send, in_recv, out_send, out_recv, sum_send, sum_recv,
):
    t = lax.axis_index("tm")
    h = lax.axis_index("height")

    def at(dt, dh):
        return (lax.rem(t + dt + n_t, n_t), lax.rem(h + dh + n_h, n_h))

    def features(head):
        return pl.ds(pl.multiple_of(head * HD, HD), HD)

    def unit(u):
        role = lax.rem(u, ROLES)
        return lax.rem(role, 2), role // 2, role * (HEADS // ROLES) + u // ROLES

    def holder(u, slot):
        rt, rh, _ = unit(u)
        return (rt if slot < 2 else 1 - rt), (rh if slot % 2 == 0 else 1 - rh)

    def quadrant(u, slot):
        a, b = holder(u, slot)
        return 1 - a, pl.ds((1 - b) * HALF_H, HALF_H), slice(None), features(unit(u)[2])

    def owner(u, slot):
        (rt, rh, _), (a, b) = unit(u), holder(u, slot)
        return at(a - rt, b - rh)

    def worker(u, slot):
        (rt, rh, _), (a, b) = unit(u), holder(u, slot)
        return at(rt - a, rh - b)

    def in_copy(u, slot):
        return pltpu.make_async_remote_copy(
            src_ref=saved.at[(1, slice(None)) + quadrant(u, slot)],
            dst_ref=x1.at[u, :, slot],
            send_sem=in_send.at[u, slot - 1],
            recv_sem=in_recv.at[u, slot - 1],
            device_id=worker(u, slot),
            device_id_type=MESH,
        )

    def in_local(u):
        return pltpu.make_async_copy(
            saved.at[(1, slice(None)) + quadrant(u, 0)], x1.at[u, :, 0], load1.at[u]
        )

    def out_copy(u, slot):
        return pltpu.make_async_remote_copy(
            src_ref=w1.at[u, :, slot - 1],
            dst_ref=grads.at[(1, slice(None)) + quadrant(u, slot)],
            send_sem=out_send.at[u, slot - 1],
            recv_sem=out_recv.at[u, slot - 1],
            device_id=owner(u, slot),
            device_id_type=MESH,
        )

    def load(a):
        return pltpu.make_async_copy(saved.at[0, a], x0.at[a], load0.at[a])

    near_h, near_t = min(n_h, GROUP), min(n_t, GROUP)
    far_h, far_t = n_h // near_h, n_t // near_t
    counts = (near_h, far_h * far_t, near_t, near_h)

    def place(stage):
        if stage == 1:
            return t // near_t * far_h + h // near_h
        return lax.rem(t, near_t) if stage == 2 else lax.rem(h, near_h)

    def peer(stage, k):
        if stage == 1:
            other_t = lax.rem(t // near_t + k // far_h, far_t)
            other_h = lax.rem(h // near_h + lax.rem(k, far_h), far_h)
            return other_t * far_h + other_h, (
                other_t * near_t + lax.rem(t, near_t),
                other_h * near_h + lax.rem(h, near_h),
            )
        other = lax.rem(place(stage) + k, counts[stage])
        shift = other - place(stage)
        return other, ((t + shift, h) if stage == 2 else (t, h + shift))

    gains_copy = pltpu.make_async_copy(gains_far, gains, load_gains)
    gains_copy.start()
    each(4, lambda a: load(a).start())
    each(HEADS, lambda u: in_local(u).start())

    barrier = pltpu.get_barrier_semaphore()

    def greet(device):
        pl.semaphore_signal(barrier, inc=1, device_id=device, device_id_type=MESH)

    greeted = 0
    for dt in (-1, 0, 1):
        for dh in (-1, 0, 1):
            if dt or dh:
                greet(at(dt, dh))
                greeted += 1
    for stage in range(3):
        for k in range(1, counts[stage]):
            greet(peer(stage, k)[1])
            greeted += 1
    pl.semaphore_wait(barrier, greeted)

    def start_inputs(u):
        for slot in (2, 3, 1):
            in_copy(u, slot).start()

    each(HEADS, start_inputs)
    gains_copy.wait()
    each(4, lambda a: load(a).wait())

    def compute(operands, block, head):
        results, gain_q_grad, gain_k_grad = head_grad(
            *(x.reshape(TOKENS, HD) for x in operands),
            gains[block, head, 0:1, :],
            gains[block, head, 1:2, :],
        )
        sums[block * HEADS + head, 0:1, :] = gain_q_grad
        sums[block * HEADS + head, 1:2, :] = gain_k_grad
        return results

    def start_outputs(u):
        for slot in (2, 3, 1):
            out_copy(u, slot).start()

    def wait_outputs(u):
        for slot in (2, 3, 1):
            out_copy(u, slot).wait_send()

    edge = lax.rem(t, min(n_t, GROUP))
    held = jnp.logical_or(edge == 0, edge == min(n_t, GROUP) - 1)

    def step(u):
        results = compute([x0[a, :, :, :, features(u)] for a in range(4)], 0, u)
        for a in range(3):
            grads[0, a, :, :, :, features(u)] = results[a].reshape(WT, WH, WW, HD)
        in_local(u).wait()
        for slot in (1, 2, 3):
            in_copy(u, slot).wait_recv()
        results = compute([x1[u, a] for a in range(4)], 1, unit(u)[2])
        for a in range(3):
            quads = results[a].reshape(4, HALF_H, WW, HD)
            w1[u, a] = quads[1:]
            grads[(1, a) + quadrant(u, 0)] = quads[0]

        @pl.when(jnp.logical_not(held))
        def _():
            start_outputs(u)

    each(HEADS, step)

    size = 2 * HEADS // near_h

    def sum_copy(stage, k):
        other, device = peer(stage, k)
        mine = place(stage)
        if stage == 0:
            source, target = sums.at[pl.ds(other * size, size)], stages.at[0, mine]
        elif stage < 3:
            source = target = stages.at[stage, mine]
        else:
            source = target = totals.at[pl.ds(mine * size, size)]
        return pltpu.make_async_remote_copy(
            src_ref=source,
            dst_ref=target,
            send_sem=sum_send.at[stage, k],
            recv_sem=sum_recv.at[stage, k],
            device_id=device,
            device_id_type=MESH,
        )

    here = pl.ds(place(0) * size, size)
    value = sums[here]
    batch = HEADS // 4
    for stage in range(4):
        count = counts[stage]
        if stage < 3:
            stages[stage, place(stage)] = value
        else:
            totals[here] = value
        for k in range(1, count):
            sum_copy(stage, k).start()

        @pl.when(held)
        def _():
            def send(i):
                u = stage * batch + i
                start_outputs(u)

                @pl.when(u > 0)
                def _():
                    wait_outputs(u - 1)

            each(batch, send)

        for k in range(1, count):
            sum_copy(stage, k).wait_recv()
        if stage < 3:
            value = functools.reduce(jnp.add, [stages[stage, i] for i in range(count)])
    gain_grads[...] = totals[...].reshape(2, HEADS, 2, HD)
    for stage in range(4):
        for k in range(1, counts[stage]):
            sum_copy(stage, k).wait_send()

    def finish(u):
        for slot in (1, 2, 3):
            in_copy(u, slot).wait_send()
            out_copy(u, slot).wait_recv()

        @pl.when(jnp.logical_or(jnp.logical_not(held), u == HEADS - 1))
        def _():
            wait_outputs(u)

    each(HEADS, finish)


def solution(mesh):
    n_t, n_h = mesh.shape["tm"], mesh.shape["height"]
    dma = pltpu.SemaphoreType.DMA
    far = pl.BlockSpec(memory_space=pl.ANY)
    near = pl.BlockSpec(memory_space=pltpu.VMEM)
    quads = (4, HALF_H, WW, HD)
    gain_shape = jax.ShapeDtypeStruct((2, HEADS, 2, HD), jnp.float32)

    def shards(saved, gains):
        saved = pltpu.with_memory_space_constraint(saved, pltpu.HBM)
        gains = pltpu.with_memory_space_constraint(gains.transpose(0, 2, 1, 3), pltpu.HBM)
        grads_shape = (2, 3) + saved.shape[2:]
        grads, gain_grads = pl.pallas_call(
            functools.partial(grad_kernel, n_t, n_h),
            out_shape=(pltpu.VMEM(grads_shape, jnp.bfloat16), gain_shape),
            in_specs=[far, far],
            out_specs=(near, near),
            scratch_shapes=[
                pltpu.VMEM(saved.shape[1:], jnp.bfloat16),
                pltpu.VMEM((HEADS, 4) + quads, jnp.bfloat16),
                pltpu.VMEM((HEADS, 3, 3) + quads[1:], jnp.bfloat16),
                pltpu.VMEM((2, HEADS, 2, HD), jnp.float32),
                pltpu.VMEM((2 * HEADS, 2, HD), jnp.float32),
                pltpu.VMEM((3, GROUP, 2 * HEADS // min(n_h, GROUP), 2, HD), jnp.float32),
                pltpu.VMEM((2 * HEADS, 2, HD), jnp.float32),
                dma,
                dma((4,)),
                dma((HEADS,)),
                dma((HEADS, 3)),
                dma((HEADS, 3)),
                dma((HEADS, 3)),
                dma((HEADS, 3)),
                dma((4, GROUP)),
                dma((4, GROUP)),
            ],
            compiler_params=pltpu.CompilerParams(
                collective_id=0, has_side_effects=True, vmem_limit_bytes=40 * 2**20
            ),
        )(saved, gains)
        return grads, gain_grads.transpose(0, 2, 1, 3)

    return jax.shard_map(
        shards,
        mesh=mesh,
        in_specs=(P(None, None, "tm", "height", None, None), P()),
        out_specs=(P(None, None, "tm", "height", None, None), P()),
        check_vma=False,
    )
```

```python
import functools
import math

import jax
import jax.numpy as jnp
from jax import lax
from jax.experimental import pallas as pl
from jax.experimental.pallas import tpu as pltpu
from jax.sharding import PartitionSpec as P

HEADS = 12
HD = 128
WT = 2
WH = 8
WW = 16
HALF_H = WH // 2
TOKENS = WT * WH * WW
PART = 128
ROLES = 4
GROUP = 8

EPSILON = 1e-06
SCALE = HD ** (-0.5)
EXP2_SCALE = SCALE * math.log2(math.e)

MESH = pl.DeviceIdType.MESH
NT = (((1,), (1,)), ((), ()))
NN = (((1,), (0,)), ((), ()))
TN = (((0,), (0,)), ((), ()))


def matmul(a, b, dims):
    return lax.dot_general(a, b, dims, preferred_element_type=jnp.float32)


def head_grad(q_raw, k_raw, values_in, out_grad, gain_q, gain_k):
    def normed(raw, gain):
        full = raw.astype(jnp.float32)
        inverse = lax.rsqrt(jnp.mean(full * full, -1, keepdims=True) + EPSILON)
        unit = full * inverse
        return unit, inverse, (unit * gain).astype(jnp.bfloat16)

    unit_q, inv_q, q_norm = normed(q_raw, gain_q)
    unit_k, inv_k, k_norm = normed(k_raw, gain_k)
    yield
    scores = matmul(k_norm, q_norm, NT)
    prob_grad = matmul(values_in, out_grad, NT)
    yield
    probs_parts, score_grad_parts = [], []
    for first in range(0, TOKENS, PART):
        part = scores[:, first : first + PART]
        grad_part = prob_grad[:, first : first + PART]
        top = jnp.max(part, 0, keepdims=True)
        probs = jnp.exp2((part - top) * EXP2_SCALE)
        probs = probs * (1.0 / jnp.sum(probs, 0, keepdims=True))
        delta = jnp.sum(probs * grad_part, 0, keepdims=True)
        probs_parts.append(probs.astype(jnp.bfloat16))
        score_grad_parts.append((probs * (grad_part - delta)).astype(jnp.bfloat16))
        yield
    probs_low = jnp.concatenate(probs_parts, 1)
    score_grad = jnp.concatenate(score_grad_parts, 1)
    value_grad = matmul(probs_low, out_grad, NN).astype(jnp.bfloat16)
    kn_grad = matmul(score_grad, q_norm, NN)
    qn_grad = matmul(score_grad, k_norm, TN)
    yield

    def raw_grad(norm_grad, unit, inverse, gain):
        along = norm_grad * unit
        gain_grad = jnp.sum(along, 0, keepdims=True) * SCALE
        scaled_gain = gain * SCALE
        mean = jnp.mean(along * scaled_gain, -1, keepdims=True)
        raw = inverse * (norm_grad * scaled_gain - unit * mean)
        return raw.astype(jnp.bfloat16), gain_grad

    k_grad, gain_k_grad = raw_grad(kn_grad, unit_k, inv_k, gain_k)
    yield
    q_grad, gain_q_grad = raw_grad(qn_grad, unit_q, inv_q, gain_q)
    return (q_grad, k_grad, value_grad), gain_q_grad, gain_k_grad


def side_by_side(heads):
    results = [None] * len(heads)
    left, turn = set(range(len(heads))), 0
    while left:
        for index in sorted(left):
            if index <= turn:
                try:
                    next(heads[index])
                except StopIteration as end:
                    results[index] = end.value
                    left.discard(index)
        turn += 1
    return results


def each(count, body):
    lax.fori_loop(0, count, lambda i, carry: (body(i), carry)[1], 0)


def grad_kernel(
    n_t, n_h,
    saved, gains_far, grads, gain_grads,
    x0, x1, w1, gains, sums, stages, totals,
    load_gains, load0, load1, in_send, in_recv, out_send, out_recv, sum_send, sum_recv,
):
    t = lax.axis_index("tm")
    h = lax.axis_index("height")

    def at(dt, dh):
        return (lax.rem(t + dt + n_t, n_t), lax.rem(h + dh + n_h, n_h))

    def features(head):
        return pl.ds(pl.multiple_of(head * HD, HD), HD)

    def unit(u):
        role = lax.rem(u, ROLES)
        return lax.rem(role, 2), role // 2, role * (HEADS // ROLES) + u // ROLES

    def holder(u, slot):
        rt, rh, _ = unit(u)
        return (rt if slot < 2 else 1 - rt), (rh if slot % 2 == 0 else 1 - rh)

    def quadrant(u, slot):
        a, b = holder(u, slot)
        return 1 - a, pl.ds((1 - b) * HALF_H, HALF_H), slice(None), features(unit(u)[2])

    def owner(u, slot):
        (rt, rh, _), (a, b) = unit(u), holder(u, slot)
        return at(a - rt, b - rh)

    def worker(u, slot):
        (rt, rh, _), (a, b) = unit(u), holder(u, slot)
        return at(rt - a, rh - b)

    def in_copy(u, slot):
        return pltpu.make_async_remote_copy(
            src_ref=saved.at[(1, slice(None)) + quadrant(u, slot)],
            dst_ref=x1.at[u, :, slot],
            send_sem=in_send.at[u, slot - 1],
            recv_sem=in_recv.at[u, slot - 1],
            device_id=worker(u, slot),
            device_id_type=MESH,
        )

    def in_local(u):
        return pltpu.make_async_copy(
            saved.at[(1, slice(None)) + quadrant(u, 0)], x1.at[u, :, 0], load1.at[u]
        )

    def out_copy(u, slot):
        return pltpu.make_async_remote_copy(
            src_ref=w1.at[u, :, slot - 1],
            dst_ref=grads.at[(1, slice(None)) + quadrant(u, slot)],
            send_sem=out_send.at[u, slot - 1],
            recv_sem=out_recv.at[u, slot - 1],
            device_id=owner(u, slot),
            device_id_type=MESH,
        )

    def load(a):
        return pltpu.make_async_copy(saved.at[0, a], x0.at[a], load0.at[a])

    near_h, near_t = min(n_h, GROUP), min(n_t, GROUP)
    far_h, far_t = n_h // near_h, n_t // near_t
    counts = (near_h, far_h * far_t, near_t, near_h)

    def place(stage):
        if stage == 1:
            return t // near_t * far_h + h // near_h
        return lax.rem(t, near_t) if stage == 2 else lax.rem(h, near_h)

    def peer(stage, k):
        if stage == 1:
            other_t = lax.rem(t // near_t + k // far_h, far_t)
            other_h = lax.rem(h // near_h + lax.rem(k, far_h), far_h)
            return other_t * far_h + other_h, (
                other_t * near_t + lax.rem(t, near_t),
                other_h * near_h + lax.rem(h, near_h),
            )
        other = lax.rem(place(stage) + k, counts[stage])
        shift = other - place(stage)
        return other, ((t + shift, h) if stage == 2 else (t, h + shift))

    gains_copy = pltpu.make_async_copy(gains_far, gains, load_gains)
    gains_copy.start()
    each(4, lambda a: load(a).start())
    each(HEADS, lambda u: in_local(u).start())

    barrier = pltpu.get_barrier_semaphore()

    def greet(device):
        pl.semaphore_signal(barrier, inc=1, device_id=device, device_id_type=MESH)

    greeted = 0
    for dt in (-1, 0, 1):
        for dh in (-1, 0, 1):
            if dt or dh:
                greet(at(dt, dh))
                greeted += 1
    for stage in range(3):
        for k in range(1, counts[stage]):
            greet(peer(stage, k)[1])
            greeted += 1
    pl.semaphore_wait(barrier, greeted)

    def start_inputs(u):
        for slot in (2, 3, 1):
            in_copy(u, slot).start()

    each(HEADS, start_inputs)
    gains_copy.wait()
    each(4, lambda a: load(a).wait())

    def operands(block, u):
        if block == 0:
            return [x0[a, :, :, :, features(u)].reshape(TOKENS, HD) for a in range(4)]
        return [x1[u, a].reshape(TOKENS, HD) for a in range(4)]

    def compute(pair):
        heads = [u if block == 0 else unit(u)[2] for block, u in pair]
        running = [
            head_grad(*operands(block, u), gains[block, head, 0:1, :], gains[block, head, 1:2, :])
            for (block, u), head in zip(pair, heads)
        ]
        for (block, u), head, result in zip(pair, heads, side_by_side(running)):
            results, gain_q_grad, gain_k_grad = result
            sums[block * HEADS + head, 0:1, :] = gain_q_grad
            sums[block * HEADS + head, 1:2, :] = gain_k_grad
            for a in range(3):
                if block == 0:
                    grads[0, a, :, :, :, features(u)] = results[a].reshape(WT, WH, WW, HD)
                else:
                    quads = results[a].reshape(4, HALF_H, WW, HD)
                    w1[u, a] = quads[1:]
                    grads[(1, a) + quadrant(u, 0)] = quads[0]

    def start_outputs(u):
        for slot in (2, 3, 1):
            out_copy(u, slot).start()

    def wait_outputs(u):
        for slot in (2, 3, 1):
            out_copy(u, slot).wait_send()

    edge = lax.rem(t, min(n_t, GROUP))
    held = jnp.logical_or(edge == 0, edge == min(n_t, GROUP) - 1)

    def wait_inputs(u):
        in_local(u).wait()
        for slot in (1, 2, 3):
            in_copy(u, slot).wait_recv()

    def step(u):
        wait_inputs(u)
        compute([(0, u + 2), (1, u)])

        @pl.when(jnp.logical_not(held))
        def _():
            start_outputs(u)

    compute([(0, 0), (0, 1)])
    each(HEADS - 2, step)
    wait_inputs(HEADS - 2)
    wait_inputs(HEADS - 1)
    compute([(1, HEADS - 2), (1, HEADS - 1)])

    @pl.when(jnp.logical_not(held))
    def _():
        start_outputs(HEADS - 2)
        start_outputs(HEADS - 1)

    size = 2 * HEADS // near_h

    def sum_copy(stage, k):
        other, device = peer(stage, k)
        mine = place(stage)
        if stage == 0:
            source, target = sums.at[pl.ds(other * size, size)], stages.at[0, mine]
        elif stage < 3:
            source = target = stages.at[stage, mine]
        else:
            source = target = totals.at[pl.ds(mine * size, size)]
        return pltpu.make_async_remote_copy(
            src_ref=source,
            dst_ref=target,
            send_sem=sum_send.at[stage, k],
            recv_sem=sum_recv.at[stage, k],
            device_id=device,
            device_id_type=MESH,
        )

    here = pl.ds(place(0) * size, size)
    value = sums[here]
    batch = HEADS // 4
    for stage in range(4):
        count = counts[stage]
        if stage < 3:
            stages[stage, place(stage)] = value
        else:
            totals[here] = value
        for k in range(1, count):
            sum_copy(stage, k).start()

        @pl.when(held)
        def _():
            for u in range(stage * batch, (stage + 1) * batch):
                start_outputs(u)
                if u > 0:
                    wait_outputs(u - 1)

        for k in range(1, count):
            sum_copy(stage, k).wait_recv()
        if stage < 3:
            value = functools.reduce(jnp.add, [stages[stage, i] for i in range(count)])
    gain_grads[...] = totals[...].reshape(2, HEADS, 2, HD)
    for stage in range(4):
        for k in range(1, counts[stage]):
            sum_copy(stage, k).wait_send()

    def finish(u):
        for slot in (1, 2, 3):
            in_copy(u, slot).wait_send()
            out_copy(u, slot).wait_recv()

        @pl.when(jnp.logical_or(jnp.logical_not(held), u == HEADS - 1))
        def _():
            wait_outputs(u)

    each(HEADS, finish)


def solution(mesh):
    n_t, n_h = mesh.shape["tm"], mesh.shape["height"]
    dma = pltpu.SemaphoreType.DMA
    far = pl.BlockSpec(memory_space=pl.ANY)
    near = pl.BlockSpec(memory_space=pltpu.VMEM)
    quads = (4, HALF_H, WW, HD)
    gain_shape = jax.ShapeDtypeStruct((2, HEADS, 2, HD), jnp.float32)

    def shards(saved, gains):
        saved = pltpu.with_memory_space_constraint(saved, pltpu.HBM)
        gains = pltpu.with_memory_space_constraint(gains.transpose(0, 2, 1, 3), pltpu.HBM)
        grads_shape = (2, 3) + saved.shape[2:]
        grads, gain_grads = pl.pallas_call(
            functools.partial(grad_kernel, n_t, n_h),
            out_shape=(pltpu.VMEM(grads_shape, jnp.bfloat16), gain_shape),
            in_specs=[far, far],
            out_specs=(near, near),
            scratch_shapes=[
                pltpu.VMEM(saved.shape[1:], jnp.bfloat16),
                pltpu.VMEM((HEADS, 4) + quads, jnp.bfloat16),
                pltpu.VMEM((HEADS, 3, 3) + quads[1:], jnp.bfloat16),
                pltpu.VMEM((2, HEADS, 2, HD), jnp.float32),
                pltpu.VMEM((2 * HEADS, 2, HD), jnp.float32),
                pltpu.VMEM((3, GROUP, 2 * HEADS // min(n_h, GROUP), 2, HD), jnp.float32),
                pltpu.VMEM((2 * HEADS, 2, HD), jnp.float32),
                dma,
                dma((4,)),
                dma((HEADS,)),
                dma((HEADS, 3)),
                dma((HEADS, 3)),
                dma((HEADS, 3)),
                dma((HEADS, 3)),
                dma((4, GROUP)),
                dma((4, GROUP)),
            ],
            compiler_params=pltpu.CompilerParams(
                collective_id=0, has_side_effects=True, vmem_limit_bytes=40 * 2**20
            ),
        )(saved, gains)
        return grads, gain_grads.transpose(0, 2, 1, 3)

    return jax.shard_map(
        shards,
        mesh=mesh,
        in_specs=(P(None, None, "tm", "height", None, None), P()),
        out_specs=(P(None, None, "tm", "height", None, None), P()),
        check_vma=False,
    )
```

```python
import functools
import math

import jax
import jax.numpy as jnp
from jax import lax
from jax.experimental import pallas as pl
from jax.experimental.pallas import tpu as pltpu
from jax.sharding import PartitionSpec as P

HEADS = 12
HD = 128
WT = 2
WH = 8
WW = 16
HALF_H = WH // 2
TOKENS = WT * WH * WW
PART = 128
ROLES = 4
GROUP = 8

EPSILON = 1e-06
SCALE = HD ** (-0.5)
EXP2_SCALE = SCALE * math.log2(math.e)

MESH = pl.DeviceIdType.MESH
NT = (((1,), (1,)), ((), ()))
NN = (((1,), (0,)), ((), ()))
TN = (((0,), (0,)), ((), ()))


def matmul(a, b, dims):
    return lax.dot_general(a, b, dims, preferred_element_type=jnp.float32)


def head_grad(q_raw, k_raw, values_in, out_grad, gain_q, gain_k):
    def normed(raw, gain):
        full = raw.astype(jnp.float32)
        inverse = lax.rsqrt(jnp.mean(full * full, -1, keepdims=True) + EPSILON)
        unit = full * inverse
        return unit, inverse, (unit * gain).astype(jnp.bfloat16)

    unit_q, inv_q, q_norm = normed(q_raw, gain_q)
    unit_k, inv_k, k_norm = normed(k_raw, gain_k)
    yield
    scores = matmul(k_norm, q_norm, NT)
    prob_grad = matmul(values_in, out_grad, NT)
    yield
    probs_parts, score_grad_parts = [], []
    for first in range(0, TOKENS, PART):
        part = scores[:, first : first + PART]
        grad_part = prob_grad[:, first : first + PART]
        top = jnp.max(part, 0, keepdims=True)
        probs = jnp.exp2((part - top) * EXP2_SCALE)
        probs = probs * (1.0 / jnp.sum(probs, 0, keepdims=True))
        delta = jnp.sum(probs * grad_part, 0, keepdims=True)
        probs_parts.append(probs.astype(jnp.bfloat16))
        score_grad_parts.append((probs * (grad_part - delta)).astype(jnp.bfloat16))
        yield
    probs_low = jnp.concatenate(probs_parts, 1)
    score_grad = jnp.concatenate(score_grad_parts, 1)
    value_grad = matmul(probs_low, out_grad, NN).astype(jnp.bfloat16)
    kn_grad = matmul(score_grad, q_norm, NN)
    qn_grad = matmul(score_grad, k_norm, TN)
    yield

    def raw_grad(norm_grad, unit, inverse, gain):
        along = norm_grad * unit
        gain_grad = jnp.sum(along, 0, keepdims=True) * SCALE
        scaled_gain = gain * SCALE
        mean = jnp.mean(along * scaled_gain, -1, keepdims=True)
        raw = inverse * (norm_grad * scaled_gain - unit * mean)
        return raw.astype(jnp.bfloat16), gain_grad

    k_grad, gain_k_grad = raw_grad(kn_grad, unit_k, inv_k, gain_k)
    yield
    q_grad, gain_q_grad = raw_grad(qn_grad, unit_q, inv_q, gain_q)
    return (q_grad, k_grad, value_grad), gain_q_grad, gain_k_grad


def side_by_side(heads):
    results = [None] * len(heads)
    left, turn = set(range(len(heads))), 0
    while left:
        for index in sorted(left):
            if index <= turn:
                try:
                    next(heads[index])
                except StopIteration as end:
                    results[index] = end.value
                    left.discard(index)
        turn += 1
    return results


def each(count, body):
    lax.fori_loop(0, count, lambda i, carry: (body(i), carry)[1], 0)


def grad_kernel(
    n_t, n_h,
    saved, gains_far, grads, gain_grads,
    x0, x1, w1, gains, sums, stages, totals,
    load_gains, load0, load1, in_send, in_recv, out_send, out_recv, sum_send, sum_recv,
):
    t = lax.axis_index("tm")
    h = lax.axis_index("height")

    def at(dt, dh):
        return (lax.rem(t + dt + n_t, n_t), lax.rem(h + dh + n_h, n_h))

    def features(head):
        return pl.ds(pl.multiple_of(head * HD, HD), HD)

    def unit(u):
        role = lax.rem(u, ROLES)
        return lax.rem(role, 2), role // 2, role * (HEADS // ROLES) + u // ROLES

    def holder(u, slot):
        rt, rh, _ = unit(u)
        return (rt if slot < 2 else 1 - rt), (rh if slot % 2 == 0 else 1 - rh)

    def quadrant(u, slot):
        a, b = holder(u, slot)
        return 1 - a, pl.ds((1 - b) * HALF_H, HALF_H), slice(None), features(unit(u)[2])

    def owner(u, slot):
        (rt, rh, _), (a, b) = unit(u), holder(u, slot)
        return at(a - rt, b - rh)

    def worker(u, slot):
        (rt, rh, _), (a, b) = unit(u), holder(u, slot)
        return at(rt - a, rh - b)

    def in_copy(u, slot):
        return pltpu.make_async_remote_copy(
            src_ref=saved.at[(1, slice(None)) + quadrant(u, slot)],
            dst_ref=x1.at[u, :, slot],
            send_sem=in_send.at[u, slot - 1],
            recv_sem=in_recv.at[u, slot - 1],
            device_id=worker(u, slot),
            device_id_type=MESH,
        )

    def in_local(u):
        return pltpu.make_async_copy(
            saved.at[(1, slice(None)) + quadrant(u, 0)], x1.at[u, :, 0], load1.at[u]
        )

    def out_copy(u, slot):
        return pltpu.make_async_remote_copy(
            src_ref=w1.at[u, :, slot - 1],
            dst_ref=grads.at[(1, slice(None)) + quadrant(u, slot)],
            send_sem=out_send.at[u, slot - 1],
            recv_sem=out_recv.at[u, slot - 1],
            device_id=owner(u, slot),
            device_id_type=MESH,
        )

    def load(a):
        return pltpu.make_async_copy(saved.at[0, a], x0.at[a], load0.at[a])

    near_h, near_t = min(n_h, GROUP), min(n_t, GROUP)
    far_h, far_t = n_h // near_h, n_t // near_t
    counts = (near_h, far_h * far_t, near_t, near_h)

    def place(stage):
        if stage == 1:
            return t // near_t * far_h + h // near_h
        return lax.rem(t, near_t) if stage == 2 else lax.rem(h, near_h)

    def peer(stage, k):
        if stage == 1:
            other_t = lax.rem(t // near_t + k // far_h, far_t)
            other_h = lax.rem(h // near_h + lax.rem(k, far_h), far_h)
            return other_t * far_h + other_h, (
                other_t * near_t + lax.rem(t, near_t),
                other_h * near_h + lax.rem(h, near_h),
            )
        other = lax.rem(place(stage) + k, counts[stage])
        shift = other - place(stage)
        return other, ((t + shift, h) if stage == 2 else (t, h + shift))

    gains_copy = pltpu.make_async_copy(gains_far, gains, load_gains)
    gains_copy.start()
    each(4, lambda a: load(a).start())
    each(HEADS, lambda u: in_local(u).start())

    barrier = pltpu.get_barrier_semaphore()

    def greet(device):
        pl.semaphore_signal(barrier, inc=1, device_id=device, device_id_type=MESH)

    greeted = 0
    for dt in (-1, 0, 1):
        for dh in (-1, 0, 1):
            if dt or dh:
                greet(at(dt, dh))
                greeted += 1
    for stage in range(3):
        for k in range(1, counts[stage]):
            greet(peer(stage, k)[1])
            greeted += 1
    pl.semaphore_wait(barrier, greeted)

    def start_inputs(u):
        for slot in (2, 3, 1):
            in_copy(u, slot).start()

    each(HEADS, start_inputs)
    gains_copy.wait()
    each(4, lambda a: load(a).wait())

    def operands(block, u):
        if block == 0:
            return [x0[a, :, :, :, features(u)].reshape(TOKENS, HD) for a in range(4)]
        return [x1[u, a].reshape(TOKENS, HD) for a in range(4)]

    def compute(pair):
        heads = [u if block == 0 else unit(u)[2] for block, u in pair]
        running = [
            head_grad(*operands(block, u), gains[block, head, 0:1, :], gains[block, head, 1:2, :])
            for (block, u), head in zip(pair, heads)
        ]
        for (block, u), head, result in zip(pair, heads, side_by_side(running)):
            results, gain_q_grad, gain_k_grad = result
            sums[block * HEADS + head, 0:1, :] = gain_q_grad
            sums[block * HEADS + head, 1:2, :] = gain_k_grad
            for a in range(3):
                if block == 0:
                    grads[0, a, :, :, :, features(u)] = results[a].reshape(WT, WH, WW, HD)
                else:
                    quads = results[a].reshape(4, HALF_H, WW, HD)
                    w1[u, a] = quads[1:]
                    grads[(1, a) + quadrant(u, 0)] = quads[0]

    def start_outputs(u):
        for slot in (2, 3, 1):
            out_copy(u, slot).start()

    def wait_outputs(u):
        for slot in (2, 3, 1):
            out_copy(u, slot).wait_send()

    def wait_inputs(u):
        in_local(u).wait()
        for slot in (1, 2, 3):
            in_copy(u, slot).wait_recv()

    def step(u):
        wait_inputs(u)
        compute([(0, u + 2), (1, u)])

    compute([(0, 0), (0, 1)])
    each(HEADS - 2, step)
    wait_inputs(HEADS - 2)
    wait_inputs(HEADS - 1)
    compute([(1, HEADS - 2), (1, HEADS - 1)])

    size = 2 * HEADS // near_h

    def sum_copy(stage, k):
        other, device = peer(stage, k)
        mine = place(stage)
        if stage == 0:
            source, target = sums.at[pl.ds(other * size, size)], stages.at[0, mine]
        elif stage < 3:
            source = target = stages.at[stage, mine]
        else:
            source = target = totals.at[pl.ds(mine * size, size)]
        return pltpu.make_async_remote_copy(
            src_ref=source,
            dst_ref=target,
            send_sem=sum_send.at[stage, k],
            recv_sem=sum_recv.at[stage, k],
            device_id=device,
            device_id_type=MESH,
        )

    here = pl.ds(place(0) * size, size)
    value = sums[here]
    batch = HEADS // 4
    for stage in range(4):
        count = counts[stage]
        if stage < 3:
            stages[stage, place(stage)] = value
        else:
            totals[here] = value
        for k in range(1, count):
            sum_copy(stage, k).start()
        for u in range(stage * batch, (stage + 1) * batch):
            start_outputs(u)
            if u > 0:
                wait_outputs(u - 1)
        for k in range(1, count):
            sum_copy(stage, k).wait_recv()
        if stage < 3:
            value = functools.reduce(jnp.add, [stages[stage, i] for i in range(count)])
    gain_grads[...] = totals[...].reshape(2, HEADS, 2, HD)
    for stage in range(4):
        for k in range(1, counts[stage]):
            sum_copy(stage, k).wait_send()

    def finish(u):
        for slot in (1, 2, 3):
            in_copy(u, slot).wait_send()
            out_copy(u, slot).wait_recv()

    wait_outputs(HEADS - 1)
    each(HEADS, finish)


def solution(mesh):
    n_t, n_h = mesh.shape["tm"], mesh.shape["height"]
    dma = pltpu.SemaphoreType.DMA
    far = pl.BlockSpec(memory_space=pl.ANY)
    near = pl.BlockSpec(memory_space=pltpu.VMEM)
    quads = (4, HALF_H, WW, HD)
    gain_shape = jax.ShapeDtypeStruct((2, HEADS, 2, HD), jnp.float32)

    def shards(saved, gains):
        saved = pltpu.with_memory_space_constraint(saved, pltpu.HBM)
        gains = pltpu.with_memory_space_constraint(gains.transpose(0, 2, 1, 3), pltpu.HBM)
        grads_shape = (2, 3) + saved.shape[2:]
        grads, gain_grads = pl.pallas_call(
            functools.partial(grad_kernel, n_t, n_h),
            out_shape=(pltpu.VMEM(grads_shape, jnp.bfloat16), gain_shape),
            in_specs=[far, far],
            out_specs=(near, near),
            scratch_shapes=[
                pltpu.VMEM(saved.shape[1:], jnp.bfloat16),
                pltpu.VMEM((HEADS, 4) + quads, jnp.bfloat16),
                pltpu.VMEM((HEADS, 3, 3) + quads[1:], jnp.bfloat16),
                pltpu.VMEM((2, HEADS, 2, HD), jnp.float32),
                pltpu.VMEM((2 * HEADS, 2, HD), jnp.float32),
                pltpu.VMEM((3, GROUP, 2 * HEADS // min(n_h, GROUP), 2, HD), jnp.float32),
                pltpu.VMEM((2 * HEADS, 2, HD), jnp.float32),
                dma,
                dma((4,)),
                dma((HEADS,)),
                dma((HEADS, 3)),
                dma((HEADS, 3)),
                dma((HEADS, 3)),
                dma((HEADS, 3)),
                dma((4, GROUP)),
                dma((4, GROUP)),
            ],
            compiler_params=pltpu.CompilerParams(
                collective_id=0, has_side_effects=True, vmem_limit_bytes=40 * 2**20
            ),
        )(saved, gains)
        return grads, gain_grads.transpose(0, 2, 1, 3)

    return jax.shard_map(
        shards,
        mesh=mesh,
        in_specs=(P(None, None, "tm", "height", None, None), P()),
        out_specs=(P(None, None, "tm", "height", None, None), P()),
        check_vma=False,
    )
```

```python
import functools
import math

import jax
import jax.numpy as jnp
from jax import lax
from jax.experimental import pallas as pl
from jax.experimental.pallas import tpu as pltpu
from jax.sharding import PartitionSpec as P

HEADS = 12
HD = 128
WT = 2
WH = 8
WW = 16
HALF_H = WH // 2
TOKENS = WT * WH * WW
PART = 128
ROLES = 4
GROUP = 8

EPSILON = 1e-06
SCALE = HD ** (-0.5)
EXP2_SCALE = SCALE * math.log2(math.e)

MESH = pl.DeviceIdType.MESH
NT = (((1,), (1,)), ((), ()))
NN = (((1,), (0,)), ((), ()))
TN = (((0,), (0,)), ((), ()))


def matmul(a, b, dims):
    return lax.dot_general(a, b, dims, preferred_element_type=jnp.float32)


def feature_means(*arrays):
    full = jnp.concatenate(arrays, 0)
    high = full.astype(jnp.bfloat16)
    low = (full - high.astype(jnp.float32)).astype(jnp.bfloat16)
    weights = jnp.full((2 * HD, HD), 1.0 / HD, jnp.bfloat16)
    means = matmul(jnp.concatenate([high, low], 1), weights, NN)
    return [means[i * TOKENS : (i + 1) * TOKENS] for i in range(len(arrays))]


def head_grad(q_raw, k_raw, values_in, out_grad, gain_q, gain_k):
    q_full = q_raw.astype(jnp.float32)
    k_full = k_raw.astype(jnp.float32)
    square_q, square_k = feature_means(q_full * q_full, k_full * k_full)
    yield
    inv_q = lax.rsqrt(square_q + EPSILON)
    inv_k = lax.rsqrt(square_k + EPSILON)
    unit_q = q_full * inv_q
    unit_k = k_full * inv_k
    q_norm = (unit_q * gain_q).astype(jnp.bfloat16)
    k_norm = (unit_k * gain_k).astype(jnp.bfloat16)
    yield
    scores = matmul(k_norm, q_norm, NT)
    prob_grad = matmul(values_in, out_grad, NT)
    yield
    probs_parts, score_grad_parts = [], []
    for first in range(0, TOKENS, PART):
        part = scores[:, first : first + PART]
        grad_part = prob_grad[:, first : first + PART]
        top = jnp.max(part, 0, keepdims=True)
        probs = jnp.exp2((part - top) * EXP2_SCALE)
        probs = probs * (1.0 / jnp.sum(probs, 0, keepdims=True))
        delta = jnp.sum(probs * grad_part, 0, keepdims=True)
        probs_parts.append(probs.astype(jnp.bfloat16))
        score_grad_parts.append((probs * (grad_part - delta)).astype(jnp.bfloat16))
        yield
    probs_low = jnp.concatenate(probs_parts, 1)
    score_grad = jnp.concatenate(score_grad_parts, 1)
    value_grad = matmul(probs_low, out_grad, NN).astype(jnp.bfloat16)
    kn_grad = matmul(score_grad, q_norm, NN)
    qn_grad = matmul(score_grad, k_norm, TN)
    yield

    along_q = qn_grad * unit_q
    along_k = kn_grad * unit_k
    gain_q_grad = jnp.sum(along_q, 0, keepdims=True) * SCALE
    gain_k_grad = jnp.sum(along_k, 0, keepdims=True) * SCALE
    scaled_q = gain_q * SCALE
    scaled_k = gain_k * SCALE
    mean_q, mean_k = feature_means(along_q * scaled_q, along_k * scaled_k)
    yield
    q_grad = (inv_q * (qn_grad * scaled_q - unit_q * mean_q)).astype(jnp.bfloat16)
    k_grad = (inv_k * (kn_grad * scaled_k - unit_k * mean_k)).astype(jnp.bfloat16)
    return (q_grad, k_grad, value_grad), gain_q_grad, gain_k_grad


def side_by_side(heads):
    results = [None] * len(heads)
    left, turn = set(range(len(heads))), 0
    while left:
        for index in sorted(left):
            if index <= turn:
                try:
                    next(heads[index])
                except StopIteration as end:
                    results[index] = end.value
                    left.discard(index)
        turn += 1
    return results


def each(count, body):
    lax.fori_loop(0, count, lambda i, carry: (body(i), carry)[1], 0)


def grad_kernel(
    n_t, n_h,
    saved, gains_far, grads, gain_grads,
    x0, x1, w1, gains, sums, stages, totals,
    load_gains, load0, load1, in_send, in_recv, out_send, out_recv, sum_send, sum_recv,
):
    t = lax.axis_index("tm")
    h = lax.axis_index("height")

    def at(dt, dh):
        return (lax.rem(t + dt + n_t, n_t), lax.rem(h + dh + n_h, n_h))

    def features(head):
        return pl.ds(pl.multiple_of(head * HD, HD), HD)

    def unit(u):
        role = lax.rem(u, ROLES)
        return lax.rem(role, 2), role // 2, role * (HEADS // ROLES) + u // ROLES

    def holder(u, slot):
        rt, rh, _ = unit(u)
        return (rt if slot < 2 else 1 - rt), (rh if slot % 2 == 0 else 1 - rh)

    def quadrant(u, slot):
        a, b = holder(u, slot)
        return 1 - a, pl.ds((1 - b) * HALF_H, HALF_H), slice(None), features(unit(u)[2])

    def owner(u, slot):
        (rt, rh, _), (a, b) = unit(u), holder(u, slot)
        return at(a - rt, b - rh)

    def worker(u, slot):
        (rt, rh, _), (a, b) = unit(u), holder(u, slot)
        return at(rt - a, rh - b)

    def in_copy(u, slot):
        return pltpu.make_async_remote_copy(
            src_ref=saved.at[(1, slice(None)) + quadrant(u, slot)],
            dst_ref=x1.at[u, :, slot],
            send_sem=in_send.at[u, slot - 1],
            recv_sem=in_recv.at[u, slot - 1],
            device_id=worker(u, slot),
            device_id_type=MESH,
        )

    def in_local(u):
        return pltpu.make_async_copy(
            saved.at[(1, slice(None)) + quadrant(u, 0)], x1.at[u, :, 0], load1.at[u]
        )

    def out_copy(u, slot):
        return pltpu.make_async_remote_copy(
            src_ref=w1.at[u, :, slot - 1],
            dst_ref=grads.at[(1, slice(None)) + quadrant(u, slot)],
            send_sem=out_send.at[u, slot - 1],
            recv_sem=out_recv.at[u, slot - 1],
            device_id=owner(u, slot),
            device_id_type=MESH,
        )

    def load(a):
        return pltpu.make_async_copy(saved.at[0, a], x0.at[a], load0.at[a])

    near_h, near_t = min(n_h, GROUP), min(n_t, GROUP)
    far_h, far_t = n_h // near_h, n_t // near_t
    counts = (near_h, far_h * far_t, near_t, near_h)

    def place(stage):
        if stage == 1:
            return t // near_t * far_h + h // near_h
        return lax.rem(t, near_t) if stage == 2 else lax.rem(h, near_h)

    def peer(stage, k):
        if stage == 1:
            other_t = lax.rem(t // near_t + k // far_h, far_t)
            other_h = lax.rem(h // near_h + lax.rem(k, far_h), far_h)
            return other_t * far_h + other_h, (
                other_t * near_t + lax.rem(t, near_t),
                other_h * near_h + lax.rem(h, near_h),
            )
        other = lax.rem(place(stage) + k, counts[stage])
        shift = other - place(stage)
        return other, ((t + shift, h) if stage == 2 else (t, h + shift))

    gains_copy = pltpu.make_async_copy(gains_far, gains, load_gains)
    gains_copy.start()
    each(4, lambda a: load(a).start())
    each(HEADS, lambda u: in_local(u).start())

    barrier = pltpu.get_barrier_semaphore()

    def greet(device):
        pl.semaphore_signal(barrier, inc=1, device_id=device, device_id_type=MESH)

    greeted = 0
    for dt in (-1, 0, 1):
        for dh in (-1, 0, 1):
            if dt or dh:
                greet(at(dt, dh))
                greeted += 1
    for stage in range(3):
        for k in range(1, counts[stage]):
            greet(peer(stage, k)[1])
            greeted += 1
    pl.semaphore_wait(barrier, greeted)

    def start_inputs(u):
        for slot in (2, 3, 1):
            in_copy(u, slot).start()

    each(HEADS, start_inputs)
    gains_copy.wait()
    each(4, lambda a: load(a).wait())

    def operands(block, u):
        if block == 0:
            return [x0[a, :, :, :, features(u)].reshape(TOKENS, HD) for a in range(4)]
        return [x1[u, a].reshape(TOKENS, HD) for a in range(4)]

    def compute(pair):
        heads = [u if block == 0 else unit(u)[2] for block, u in pair]
        running = [
            head_grad(*operands(block, u), gains[block, head, 0:1, :], gains[block, head, 1:2, :])
            for (block, u), head in zip(pair, heads)
        ]
        for (block, u), head, result in zip(pair, heads, side_by_side(running)):
            results, gain_q_grad, gain_k_grad = result
            sums[block * HEADS + head, 0:1, :] = gain_q_grad
            sums[block * HEADS + head, 1:2, :] = gain_k_grad
            for a in range(3):
                if block == 0:
                    grads[0, a, :, :, :, features(u)] = results[a].reshape(WT, WH, WW, HD)
                else:
                    quads = results[a].reshape(4, HALF_H, WW, HD)
                    w1[u, a] = quads[1:]
                    grads[(1, a) + quadrant(u, 0)] = quads[0]

    def start_outputs(u):
        for slot in (2, 3, 1):
            out_copy(u, slot).start()

    def wait_inputs(u):
        in_local(u).wait()
        for slot in (1, 2, 3):
            in_copy(u, slot).wait_recv()

    def step(u):
        wait_inputs(u)
        compute([(0, u + 2), (1, u)])
        start_outputs(u)

    compute([(0, 0), (0, 1)])
    each(HEADS - 2, step)
    wait_inputs(HEADS - 2)
    wait_inputs(HEADS - 1)
    compute([(1, HEADS - 2), (1, HEADS - 1)])
    start_outputs(HEADS - 2)
    start_outputs(HEADS - 1)

    size = 2 * HEADS // near_h

    def sum_copy(stage, k):
        other, device = peer(stage, k)
        mine = place(stage)
        if stage == 0:
            source, target = sums.at[pl.ds(other * size, size)], stages.at[0, mine]
        elif stage < 3:
            source = target = stages.at[stage, mine]
        else:
            source = target = totals.at[pl.ds(mine * size, size)]
        return pltpu.make_async_remote_copy(
            src_ref=source,
            dst_ref=target,
            send_sem=sum_send.at[stage, k],
            recv_sem=sum_recv.at[stage, k],
            device_id=device,
            device_id_type=MESH,
        )

    here = pl.ds(place(0) * size, size)
    value = sums[here]
    for stage in range(4):
        count = counts[stage]
        if stage < 3:
            stages[stage, place(stage)] = value
        else:
            totals[here] = value
        for k in range(1, count):
            sum_copy(stage, k).start()
        for k in range(1, count):
            sum_copy(stage, k).wait_recv()
        if stage < 3:
            value = functools.reduce(jnp.add, [stages[stage, i] for i in range(count)])
    gain_grads[...] = totals[...].reshape(2, HEADS, 2, HD)
    for stage in range(4):
        for k in range(1, counts[stage]):
            sum_copy(stage, k).wait_send()

    def finish(u):
        for slot in (1, 2, 3):
            in_copy(u, slot).wait_send()
            out_copy(u, slot).wait()

    each(HEADS, finish)


def solution(mesh):
    n_t, n_h = mesh.shape["tm"], mesh.shape["height"]
    dma = pltpu.SemaphoreType.DMA
    far = pl.BlockSpec(memory_space=pl.ANY)
    near = pl.BlockSpec(memory_space=pltpu.VMEM)
    quads = (4, HALF_H, WW, HD)
    gain_shape = jax.ShapeDtypeStruct((2, HEADS, 2, HD), jnp.float32)

    def shards(saved, gains):
        saved = pltpu.with_memory_space_constraint(saved, pltpu.HBM)
        gains = pltpu.with_memory_space_constraint(gains.transpose(0, 2, 1, 3), pltpu.HBM)
        grads_shape = (2, 3) + saved.shape[2:]
        grads, gain_grads = pl.pallas_call(
            functools.partial(grad_kernel, n_t, n_h),
            out_shape=(pltpu.VMEM(grads_shape, jnp.bfloat16), gain_shape),
            in_specs=[far, far],
            out_specs=(near, near),
            scratch_shapes=[
                pltpu.VMEM(saved.shape[1:], jnp.bfloat16),
                pltpu.VMEM((HEADS, 4) + quads, jnp.bfloat16),
                pltpu.VMEM((HEADS, 3, 3) + quads[1:], jnp.bfloat16),
                pltpu.VMEM((2, HEADS, 2, HD), jnp.float32),
                pltpu.VMEM((2 * HEADS, 2, HD), jnp.float32),
                pltpu.VMEM((3, GROUP, 2 * HEADS // min(n_h, GROUP), 2, HD), jnp.float32),
                pltpu.VMEM((2 * HEADS, 2, HD), jnp.float32),
                dma,
                dma((4,)),
                dma((HEADS,)),
                dma((HEADS, 3)),
                dma((HEADS, 3)),
                dma((HEADS, 3)),
                dma((HEADS, 3)),
                dma((4, GROUP)),
                dma((4, GROUP)),
            ],
            compiler_params=pltpu.CompilerParams(
                collective_id=0, has_side_effects=True, vmem_limit_bytes=40 * 2**20
            ),
        )(saved, gains)
        return grads, gain_grads.transpose(0, 2, 1, 3)

    return jax.shard_map(
        shards,
        mesh=mesh,
        in_specs=(P(None, None, "tm", "height", None, None), P()),
        out_specs=(P(None, None, "tm", "height", None, None), P()),
        check_vma=False,
    )
```

```python
import functools
import math

import jax
import jax.numpy as jnp
from jax import lax
from jax.experimental import pallas as pl
from jax.experimental.pallas import tpu as pltpu
from jax.sharding import PartitionSpec as P

HEADS = 12
HD = 128
WT = 2
WH = 8
WW = 16
HALF_H = WH // 2
TOKENS = WT * WH * WW
PART = 128
ROLES = 4
SHARE = HEADS // ROLES
GROUP = 8

EPSILON = 1e-06
SCALE = HD ** (-0.5)
EXP2_SCALE = SCALE * math.log2(math.e)

MESH = pl.DeviceIdType.MESH
NT = (((1,), (1,)), ((), ()))
NN = (((1,), (0,)), ((), ()))
TN = (((0,), (0,)), ((), ()))


def matmul(a, b, dims):
    return lax.dot_general(a, b, dims, preferred_element_type=jnp.float32)


def feature_means(*arrays):
    full = jnp.concatenate(arrays, 0)
    high = full.astype(jnp.bfloat16)
    low = (full - high.astype(jnp.float32)).astype(jnp.bfloat16)
    weights = jnp.full((2 * HD, HD), 1.0 / HD, jnp.bfloat16)
    means = matmul(jnp.concatenate([high, low], 1), weights, NN)
    return [means[i * TOKENS : (i + 1) * TOKENS] for i in range(len(arrays))]


def head_grad(q_raw, k_raw, values_in, out_grad, gain_q, gain_k):
    q_full = q_raw.astype(jnp.float32)
    k_full = k_raw.astype(jnp.float32)
    square_q, square_k = feature_means(q_full * q_full, k_full * k_full)
    yield
    inv_q = lax.rsqrt(square_q + EPSILON)
    inv_k = lax.rsqrt(square_k + EPSILON)
    unit_q = q_full * inv_q
    unit_k = k_full * inv_k
    q_norm = (unit_q * gain_q).astype(jnp.bfloat16)
    k_norm = (unit_k * gain_k).astype(jnp.bfloat16)
    yield
    scores = matmul(k_norm, q_norm, NT)
    prob_grad = matmul(values_in, out_grad, NT)
    yield
    probs_parts, score_grad_parts = [], []
    for first in range(0, TOKENS, PART):
        part = scores[:, first : first + PART]
        grad_part = prob_grad[:, first : first + PART]
        top = jnp.max(part, 0, keepdims=True)
        probs = jnp.exp2((part - top) * EXP2_SCALE)
        probs = probs * (1.0 / jnp.sum(probs, 0, keepdims=True))
        delta = jnp.sum(probs * grad_part, 0, keepdims=True)
        probs_parts.append(probs.astype(jnp.bfloat16))
        score_grad_parts.append((probs * (grad_part - delta)).astype(jnp.bfloat16))
        yield
    probs_low = jnp.concatenate(probs_parts, 1)
    score_grad = jnp.concatenate(score_grad_parts, 1)
    value_grad = matmul(probs_low, out_grad, NN).astype(jnp.bfloat16)
    kn_grad = matmul(score_grad, q_norm, NN)
    qn_grad = matmul(score_grad, k_norm, TN)
    yield

    along_q = qn_grad * unit_q
    along_k = kn_grad * unit_k
    gain_q_grad = jnp.sum(along_q, 0, keepdims=True) * SCALE
    gain_k_grad = jnp.sum(along_k, 0, keepdims=True) * SCALE
    scaled_q = gain_q * SCALE
    scaled_k = gain_k * SCALE
    mean_q, mean_k = feature_means(along_q * scaled_q, along_k * scaled_k)
    yield
    q_grad = (inv_q * (qn_grad * scaled_q - unit_q * mean_q)).astype(jnp.bfloat16)
    k_grad = (inv_k * (kn_grad * scaled_k - unit_k * mean_k)).astype(jnp.bfloat16)
    return (q_grad, k_grad, value_grad), gain_q_grad, gain_k_grad


def side_by_side(heads):
    results = [None] * len(heads)
    left, turn = set(range(len(heads))), 0
    while left:
        for index in sorted(left):
            if index <= turn:
                try:
                    next(heads[index])
                except StopIteration as end:
                    results[index] = end.value
                    left.discard(index)
        turn += 1
    return results


def each(count, body):
    lax.fori_loop(0, count, lambda i, carry: (body(i), carry)[1], 0)


def grad_kernel(
    n_t, n_h,
    saved, gains_far, grads, gain_grads,
    x0, x1, w1, gains, sums, stages, totals,
    load_gains, load0, load1, in_send, in_recv, out_send, out_recv, sum_send, sum_recv,
):
    t = lax.axis_index("tm")
    h = lax.axis_index("height")
    near_h, near_t = min(n_h, GROUP), min(n_t, GROUP)
    far_h, far_t = n_h // near_h, n_t // near_t

    def at(dt, dh):
        return (lax.rem(t + dt + n_t, n_t), lax.rem(h + dh + n_h, n_h))

    def features(head):
        return pl.ds(pl.multiple_of(head * HD, HD), HD)

    in_t, in_h = lax.rem(t, near_t), lax.rem(h, near_h)
    across = jnp.logical_and(near_t >= 4, jnp.logical_or(in_h == 0, in_h == near_h - 1))
    outer = jnp.logical_and(across, jnp.logical_or(in_t == 0, in_t == near_t - 1))
    inner = jnp.logical_and(across, jnp.logical_or(in_t == 1, in_t == near_t - 2))
    own_a = jnp.where(jnp.logical_or(in_t == 1, in_t == near_t - 1), 1, 0)
    own_b = jnp.where(in_h == 0, 1, 0)
    side = jnp.where(outer, 1 - own_a, own_a)

    def unit(u):
        taken = u >= HEADS
        role = jnp.where(taken, side + 2 * own_b, lax.rem(u, ROLES))
        first = jnp.where(taken, (1 - side + 2 * own_b) * SHARE - HEADS, role * SHARE)
        return lax.rem(role, 2), role // 2, first + jnp.where(taken, u, u // ROLES)

    def holder(u, slot):
        rt, rh, _ = unit(u)
        return (rt if slot < 2 else 1 - rt), (rh if slot % 2 == 0 else 1 - rh)

    def quadrant(u, slot):
        a, b = holder(u, slot)
        return 1 - a, pl.ds((1 - b) * HALF_H, HALF_H), slice(None), features(unit(u)[2])

    def regular(u, slot):
        (rt, _, _), (a, b) = unit(u), holder(u, slot)
        here = jnp.logical_and(a == own_a, b == own_b)
        moved = jnp.logical_and(jnp.logical_or(outer, inner), rt != side)
        return jnp.logical_not(jnp.logical_and(here, moved))

    def owner(u, slot):
        (rt, rh, _), (a, b) = unit(u), holder(u, slot)
        return at(a - rt, b - rh)

    def worker(u, slot):
        (rt, rh, _), (a, b) = unit(u), holder(u, slot)
        return at(rt - a, rh - b)

    def in_copy(u, slot):
        return pltpu.make_async_remote_copy(
            src_ref=saved.at[(1, slice(None)) + quadrant(u, slot)],
            dst_ref=x1.at[u, :, slot],
            send_sem=in_send.at[u, slot - 1],
            recv_sem=in_recv.at[u, slot - 1],
            device_id=worker(u, slot),
            device_id_type=MESH,
        )

    def taken_copy(j, slot):
        rh = own_b if slot % 2 == 0 else 1 - own_b
        head = (1 - side + 2 * rh) * SHARE + j
        band = pl.ds((1 - own_b) * HALF_H, HALF_H)
        return pltpu.make_async_remote_copy(
            src_ref=saved.at[1, :, 1 - own_a, band, :, features(head)],
            dst_ref=x1.at[HEADS + j, :, slot],
            send_sem=in_send.at[HEADS + j, slot - 1],
            recv_sem=in_recv.at[HEADS + j, slot - 1],
            device_id=at(side - own_a, rh - own_b),
            device_id_type=MESH,
        )

    def in_local(u):
        return pltpu.make_async_copy(
            saved.at[(1, slice(None)) + quadrant(u, 0)], x1.at[u, :, 0], load1.at[u]
        )

    def out_copy(u, slot):
        return pltpu.make_async_remote_copy(
            src_ref=w1.at[u, :, slot - 1],
            dst_ref=grads.at[(1, slice(None)) + quadrant(u, slot)],
            send_sem=out_send.at[u, slot - 1],
            recv_sem=out_recv.at[u, slot - 1],
            device_id=owner(u, slot),
            device_id_type=MESH,
        )

    def load(a):
        return pltpu.make_async_copy(saved.at[0, a], x0.at[a], load0.at[a])

    counts = (near_h, far_h * far_t, near_t, near_h)

    def place(stage):
        if stage == 1:
            return t // near_t * far_h + h // near_h
        return lax.rem(t, near_t) if stage == 2 else lax.rem(h, near_h)

    def peer(stage, k):
        if stage == 1:
            other_t = lax.rem(t // near_t + k // far_h, far_t)
            other_h = lax.rem(h // near_h + lax.rem(k, far_h), far_h)
            return other_t * far_h + other_h, (
                other_t * near_t + lax.rem(t, near_t),
                other_h * near_h + lax.rem(h, near_h),
            )
        other = lax.rem(place(stage) + k, counts[stage])
        shift = other - place(stage)
        return other, ((t + shift, h) if stage == 2 else (t, h + shift))

    barrier = pltpu.get_barrier_semaphore()

    def greet(device):
        pl.semaphore_signal(barrier, inc=1, device_id=device, device_id_type=MESH)

    greeted = 0
    for dt in (-1, 0, 1):
        for dh in (-1, 0, 1):
            if dt or dh:
                greet(at(dt, dh))
                greeted += 1
    for stage in range(3):
        for k in range(1, counts[stage]):
            greet(peer(stage, k)[1])
            greeted += 1
    gains_copy = pltpu.make_async_copy(gains_far, gains, load_gains)
    gains_copy.start()
    each(4, lambda a: load(a).start())
    each(HEADS, lambda u: pl.when(regular(u, 0))(lambda: in_local(u).start()))
    pl.when(inner)(lambda: each(SHARE, lambda j: in_local(HEADS + j).start()))
    pl.semaphore_wait(barrier, greeted)

    def start_inputs(u):
        for slot in (2, 3, 1):
            pl.when(regular(u, slot))(in_copy(u, slot).start)

    def start_taken(j):
        pl.when(outer)(taken_copy(j, 2).start)
        pl.when(outer)(taken_copy(j, 3).start)
        pl.when(inner)(taken_copy(j, 1).start)

    each(HEADS, start_inputs)
    each(SHARE, start_taken)
    gains_copy.wait()
    each(4, lambda a: load(a).wait())

    def operands(block, u):
        if block == 0:
            return [x0[a, :, :, :, features(u)].reshape(TOKENS, HD) for a in range(4)]
        return [x1[u, a].reshape(TOKENS, HD) for a in range(4)]

    def compute(pair, twice=False):
        heads = [u if block == 0 else unit(u)[2] for block, u in pair]
        running = [
            head_grad(*operands(block, u), gains[block, head, 0:1, :], gains[block, head, 1:2, :])
            for (block, u), head in zip(pair, heads)
        ]
        for index, result in enumerate(side_by_side(running)):
            (block, u), head = pair[index], heads[index]
            results, gain_q_grad, gain_k_grad = result
            for i, gain_grad in enumerate((gain_q_grad, gain_k_grad)):
                row = (block * HEADS + head, slice(i, i + 1))
                if block == 0:
                    sums[row] = gain_grad
                elif index == 0:
                    sums[row] += gain_grad
                else:
                    sums[row] += jnp.where(twice, 0.0, gain_grad)
            for a in range(3):
                if block == 0:
                    grads[0, a, :, :, :, features(u)] = results[a].reshape(WT, WH, WW, HD)
                else:
                    quads = results[a].reshape(4, HALF_H, WW, HD)
                    w1[u, a] = quads[1:]
                    grads[(1, a) + quadrant(u, 0)] = quads[0]

    def start_outputs(u):
        for slot in (2, 3, 1):
            out_copy(u, slot).start()

    def wait_inputs(u):
        in_local(u).wait()
        for slot in (1, 2, 3):
            in_copy(u, slot).wait_recv()

    def listed(position):
        role = lax.rem(position, ROLES - 1)
        role = role + jnp.where(role >= own_a + 2 * own_b, 1, 0)
        return jnp.where(outer, position // (ROLES - 1) * ROLES + role, position)

    ahead = jnp.where(outer, 2, 1)

    def still_pair(i):
        compute([(0, 2 * i), (0, 2 * i + 1)])

    def mixed_pair(i):
        u = listed(i)
        wait_inputs(u)
        compute([(0, jnp.minimum(i + 2 * ahead, HEADS - 1)), (1, u)])
        start_outputs(u)

    def shifted_pair(i):
        u = HEADS - 2 + 2 * i
        v = jnp.minimum(u + 1, HEADS + SHARE - 1)
        wait_inputs(u)
        pl.when(u != v)(lambda: wait_inputs(v))
        compute([(1, u), (1, v)], u == v)
        start_outputs(u)
        pl.when(u != v)(lambda: start_outputs(v))

    sums[...] = jnp.zeros_like(sums)
    each(ahead, still_pair)
    each(jnp.where(outer, HEADS - SHARE, HEADS - 2), mixed_pair)
    each(jnp.where(outer, 0, jnp.where(inner, 3, 1)), shifted_pair)

    size = 2 * HEADS // near_h

    def sum_copy(stage, k):
        other, device = peer(stage, k)
        mine = place(stage)
        if stage == 0:
            source, target = sums.at[pl.ds(other * size, size)], stages.at[0, mine]
        elif stage < 3:
            source = target = stages.at[stage, mine]
        else:
            source = target = totals.at[pl.ds(mine * size, size)]
        return pltpu.make_async_remote_copy(
            src_ref=source,
            dst_ref=target,
            send_sem=sum_send.at[stage, k],
            recv_sem=sum_recv.at[stage, k],
            device_id=device,
            device_id_type=MESH,
        )

    here = pl.ds(place(0) * size, size)
    value = sums[here]
    for stage in range(4):
        count = counts[stage]
        if stage < 3:
            stages[stage, place(stage)] = value
        else:
            totals[here] = value
        for k in range(1, count):
            sum_copy(stage, k).start()
        for k in range(1, count):
            sum_copy(stage, k).wait_recv()
        if stage < 3:
            value = functools.reduce(jnp.add, [stages[stage, i] for i in range(count)])
    gain_grads[...] = totals[...].reshape(2, HEADS, 2, HD)
    for stage in range(4):
        for k in range(1, counts[stage]):
            sum_copy(stage, k).wait_send()

    def finish(u):
        for slot in (1, 2, 3):
            pl.when(regular(u, slot))(in_copy(u, slot).wait_send)
            pl.when(regular(u, slot))(out_copy(u, slot).wait_recv)
            pl.when(regular(u, 0))(out_copy(u, slot).wait_send)

    def finish_taken(j):
        for slot in (1, 2, 3):
            holds = inner if slot == 1 else outer
            pl.when(holds)(taken_copy(j, slot).wait_send)
            pl.when(holds)(out_copy(HEADS + j, slot).wait_recv)
            pl.when(inner)(out_copy(HEADS + j, slot).wait_send)

    each(HEADS, finish)
    each(SHARE, finish_taken)


def solution(mesh):
    n_t, n_h = mesh.shape["tm"], mesh.shape["height"]
    dma = pltpu.SemaphoreType.DMA
    far = pl.BlockSpec(memory_space=pl.ANY)
    near = pl.BlockSpec(memory_space=pltpu.VMEM)
    quads = (4, HALF_H, WW, HD)
    gain_shape = jax.ShapeDtypeStruct((2, HEADS, 2, HD), jnp.float32)

    def shards(saved, gains):
        saved = pltpu.with_memory_space_constraint(saved, pltpu.HBM)
        gains = pltpu.with_memory_space_constraint(gains.transpose(0, 2, 1, 3), pltpu.HBM)
        grads_shape = (2, 3) + saved.shape[2:]
        grads, gain_grads = pl.pallas_call(
            functools.partial(grad_kernel, n_t, n_h),
            out_shape=(pltpu.VMEM(grads_shape, jnp.bfloat16), gain_shape),
            in_specs=[far, far],
            out_specs=(near, near),
            scratch_shapes=[
                pltpu.VMEM(saved.shape[1:], jnp.bfloat16),
                pltpu.VMEM((HEADS + SHARE, 4) + quads, jnp.bfloat16),
                pltpu.VMEM((HEADS + SHARE, 3, 3) + quads[1:], jnp.bfloat16),
                pltpu.VMEM((2, HEADS, 2, HD), jnp.float32),
                pltpu.VMEM((2 * HEADS, 2, HD), jnp.float32),
                pltpu.VMEM((3, GROUP, 2 * HEADS // min(n_h, GROUP), 2, HD), jnp.float32),
                pltpu.VMEM((2 * HEADS, 2, HD), jnp.float32),
                dma,
                dma((4,)),
                dma((HEADS + SHARE,)),
                dma((HEADS + SHARE, 3)),
                dma((HEADS + SHARE, 3)),
                dma((HEADS + SHARE, 3)),
                dma((HEADS + SHARE, 3)),
                dma((4, GROUP)),
                dma((4, GROUP)),
            ],
            compiler_params=pltpu.CompilerParams(
                collective_id=0, has_side_effects=True, vmem_limit_bytes=40 * 2**20
            ),
        )(saved, gains)
        return grads, gain_grads.transpose(0, 2, 1, 3)

    return jax.shard_map(
        shards,
        mesh=mesh,
        in_specs=(P(None, None, "tm", "height", None, None), P()),
        out_specs=(P(None, None, "tm", "height", None, None), P()),
        check_vma=False,
    )
```

```python
import functools
import math

import jax
import jax.numpy as jnp
from jax import lax
from jax.experimental import pallas as pl
from jax.experimental.pallas import tpu as pltpu
from jax.sharding import PartitionSpec as P

HEADS = 12
HD = 128
WT = 2
WH = 8
WW = 16
HALF_H = WH // 2
TOKENS = WT * WH * WW
PART = 128
ROWS = 64
ROLES = 4
GROUP = 8

EPSILON = 1e-06
SCALE = HD ** (-0.5)
EXP2_SCALE = SCALE * math.log2(math.e)

MESH = pl.DeviceIdType.MESH
NT = (((1,), (1,)), ((), ()))
NN = (((1,), (0,)), ((), ()))
TN = (((0,), (0,)), ((), ()))


def matmul(a, b, dims):
    return lax.dot_general(a, b, dims, preferred_element_type=jnp.float32)


def rows_of(array, first):
    return array[first : first + ROWS]


def column_sum(blocks):
    tiles = [block.reshape(-1, 8, block.shape[-1]).sum(0) for block in blocks]
    return jnp.sum(functools.reduce(jnp.add, tiles), 0, keepdims=True)


def head_grad(q_raw, k_raw, values_in, out_grad, gain_q, gain_k):
    blocks = range(0, TOKENS, ROWS)

    def normed(raw, gain):
        units, inverses, norms = [], [], []
        for first in blocks:
            full = rows_of(raw, first).astype(jnp.float32)
            inverse = lax.rsqrt(jnp.mean(full * full, -1, keepdims=True) + EPSILON)
            unit = full * inverse
            units.append(unit)
            inverses.append(inverse)
            norms.append((unit * gain).astype(jnp.bfloat16))
        return units, inverses, jnp.concatenate(norms, 0)

    unit_q, inv_q, q_norm = normed(q_raw, gain_q)
    unit_k, inv_k, k_norm = normed(k_raw, gain_k)
    yield
    scores = matmul(k_norm, q_norm, NT)
    prob_grad = matmul(values_in, out_grad, NT)
    yield
    low_parts, score_grad_parts = [], []
    for first_query in range(0, TOKENS, PART):
        part = scores[:, first_query : first_query + PART]
        grad_part = prob_grad[:, first_query : first_query + PART]
        top = jnp.max(part, 0, keepdims=True)
        powers = [jnp.exp2((rows_of(part, first) - top) * EXP2_SCALE) for first in blocks]
        inverse = 1.0 / column_sum(powers)
        probs, weighted, low = [], [], []
        for first, power in zip(blocks, powers):
            probs.append(power * inverse)
            weighted.append(probs[-1] * rows_of(grad_part, first))
            low.append(probs[-1].astype(jnp.bfloat16))
        delta = column_sum(weighted)
        score_grad_parts.append(
            jnp.concatenate(
                [
                    (prob * (rows_of(grad_part, first) - delta)).astype(jnp.bfloat16)
                    for first, prob in zip(blocks, probs)
                ],
                0,
            )
        )
        low_parts.append(jnp.concatenate(low, 0))
        yield
    score_grad = jnp.concatenate(score_grad_parts, 1)
    value_grad = matmul(jnp.concatenate(low_parts, 1), out_grad, NN).astype(jnp.bfloat16)
    kn_grad = matmul(score_grad, q_norm, NN)
    qn_grad = matmul(score_grad, k_norm, TN)
    yield

    def raw_grad(norm_grad, units, inverses, gain):
        scaled_gain = gain * SCALE
        alongs, raws = [], []
        for first, unit, inverse in zip(blocks, units, inverses):
            grad = rows_of(norm_grad, first)
            along = grad * unit
            mean = jnp.mean(along * scaled_gain, -1, keepdims=True)
            raws.append((inverse * (grad * scaled_gain - unit * mean)).astype(jnp.bfloat16))
            alongs.append(along)
        return jnp.concatenate(raws, 0), column_sum(alongs) * SCALE

    k_grad, gain_k_grad = raw_grad(kn_grad, unit_k, inv_k, gain_k)
    yield
    q_grad, gain_q_grad = raw_grad(qn_grad, unit_q, inv_q, gain_q)
    return (q_grad, k_grad, value_grad), gain_q_grad, gain_k_grad


def side_by_side(heads):
    results = [None] * len(heads)
    left, turn = set(range(len(heads))), 0
    while left:
        for index in sorted(left):
            if index <= turn:
                try:
                    next(heads[index])
                except StopIteration as end:
                    results[index] = end.value
                    left.discard(index)
        turn += 1
    return results


def each(count, body):
    lax.fori_loop(0, count, lambda i, carry: (body(i), carry)[1], 0)


def grad_kernel(
    n_t, n_h,
    saved, gains_far, grads, gain_grads,
    x0, x1, w1, gains, sums, stages, totals,
    load_gains, load0, load1, in_send, in_recv, out_send, out_recv, sum_send, sum_recv,
):
    t = lax.axis_index("tm")
    h = lax.axis_index("height")

    def at(dt, dh):
        return (lax.rem(t + dt + n_t, n_t), lax.rem(h + dh + n_h, n_h))

    def features(head):
        return pl.ds(pl.multiple_of(head * HD, HD), HD)

    def unit(u):
        role = lax.rem(u, ROLES)
        return lax.rem(role, 2), role // 2, role * (HEADS // ROLES) + u // ROLES

    def holder(u, slot):
        rt, rh, _ = unit(u)
        return (rt if slot < 2 else 1 - rt), (rh if slot % 2 == 0 else 1 - rh)

    def quadrant(u, slot):
        a, b = holder(u, slot)
        return 1 - a, pl.ds((1 - b) * HALF_H, HALF_H), slice(None), features(unit(u)[2])

    def owner(u, slot):
        (rt, rh, _), (a, b) = unit(u), holder(u, slot)
        return at(a - rt, b - rh)

    def worker(u, slot):
        (rt, rh, _), (a, b) = unit(u), holder(u, slot)
        return at(rt - a, rh - b)

    def in_copy(u, slot):
        return pltpu.make_async_remote_copy(
            src_ref=saved.at[(1, slice(None)) + quadrant(u, slot)],
            dst_ref=x1.at[u, :, slot],
            send_sem=in_send.at[u, slot - 1],
            recv_sem=in_recv.at[u, slot - 1],
            device_id=worker(u, slot),
            device_id_type=MESH,
        )

    def in_local(u):
        return pltpu.make_async_copy(
            saved.at[(1, slice(None)) + quadrant(u, 0)], x1.at[u, :, 0], load1.at[u]
        )

    def out_copy(u, slot):
        return pltpu.make_async_remote_copy(
            src_ref=w1.at[u, :, slot - 1],
            dst_ref=grads.at[(1, slice(None)) + quadrant(u, slot)],
            send_sem=out_send.at[u, slot - 1],
            recv_sem=out_recv.at[u, slot - 1],
            device_id=owner(u, slot),
            device_id_type=MESH,
        )

    def load(a):
        return pltpu.make_async_copy(saved.at[0, a], x0.at[a], load0.at[a])

    near_h, near_t = min(n_h, GROUP), min(n_t, GROUP)
    far_h, far_t = n_h // near_h, n_t // near_t
    counts = (near_h, far_h * far_t, near_t, near_h)

    def place(stage):
        if stage == 1:
            return t // near_t * far_h + h // near_h
        return lax.rem(t, near_t) if stage == 2 else lax.rem(h, near_h)

    def peer(stage, k):
        if stage == 1:
            other_t = lax.rem(t // near_t + k // far_h, far_t)
            other_h = lax.rem(h // near_h + lax.rem(k, far_h), far_h)
            return other_t * far_h + other_h, (
                other_t * near_t + lax.rem(t, near_t),
                other_h * near_h + lax.rem(h, near_h),
            )
        other = lax.rem(place(stage) + k, counts[stage])
        shift = other - place(stage)
        return other, ((t + shift, h) if stage == 2 else (t, h + shift))

    barrier = pltpu.get_barrier_semaphore()

    def greet(device):
        pl.semaphore_signal(barrier, inc=1, device_id=device, device_id_type=MESH)

    greeted = 0
    for dt in (-1, 0, 1):
        for dh in (-1, 0, 1):
            if dt or dh:
                greet(at(dt, dh))
                greeted += 1
    for stage in range(3):
        for k in range(1, counts[stage]):
            greet(peer(stage, k)[1])
            greeted += 1
    gains_copy = pltpu.make_async_copy(gains_far, gains, load_gains)
    gains_copy.start()
    each(4, lambda a: load(a).start())
    each(HEADS, lambda u: in_local(u).start())
    pl.semaphore_wait(barrier, greeted)

    def start_inputs(u):
        for slot in (2, 3, 1):
            in_copy(u, slot).start()

    each(HEADS, start_inputs)
    gains_copy.wait()
    each(4, lambda a: load(a).wait())

    def operands(block, u):
        if block == 0:
            return [x0[a, :, :, :, features(u)].reshape(TOKENS, HD) for a in range(4)]
        return [x1[u, a].reshape(TOKENS, HD) for a in range(4)]

    def compute(pair):
        heads = [u if block == 0 else unit(u)[2] for block, u in pair]
        running = [
            head_grad(*operands(block, u), gains[block, head, 0:1, :], gains[block, head, 1:2, :])
            for (block, u), head in zip(pair, heads)
        ]
        for (block, u), head, result in zip(pair, heads, side_by_side(running)):
            results, gain_q_grad, gain_k_grad = result
            sums[block * HEADS + head, 0:1, :] = gain_q_grad
            sums[block * HEADS + head, 1:2, :] = gain_k_grad
            for a in range(3):
                if block == 0:
                    grads[0, a, :, :, :, features(u)] = results[a].reshape(WT, WH, WW, HD)
                else:
                    quads = results[a].reshape(4, HALF_H, WW, HD)
                    w1[u, a] = quads[1:]
                    grads[(1, a) + quadrant(u, 0)] = quads[0]

    def start_outputs(u):
        for slot in (2, 3, 1):
            out_copy(u, slot).start()

    def wait_inputs(u):
        in_local(u).wait()
        for slot in (1, 2, 3):
            in_copy(u, slot).wait_recv()

    def step(u):
        wait_inputs(u)
        compute([(0, u + 2), (1, u)])

    compute([(0, 0), (0, 1)])
    each(HEADS - 2, step)
    wait_inputs(HEADS - 2)
    wait_inputs(HEADS - 1)
    compute([(1, HEADS - 2), (1, HEADS - 1)])

    batch = HEADS // 4
    size = 2 * HEADS // near_h

    def sum_copy(stage, k):
        other, device = peer(stage, k)
        mine = place(stage)
        if stage == 0:
            source, target = sums.at[pl.ds(other * size, size)], stages.at[0, mine]
        elif stage < 3:
            source = target = stages.at[stage, mine]
        else:
            source = target = totals.at[pl.ds(mine * size, size)]
        return pltpu.make_async_remote_copy(
            src_ref=source,
            dst_ref=target,
            send_sem=sum_send.at[stage, k],
            recv_sem=sum_recv.at[stage, k],
            device_id=device,
            device_id_type=MESH,
        )

    here = pl.ds(place(0) * size, size)
    value = sums[here]
    for stage in range(4):
        count = counts[stage]
        if stage < 3:
            stages[stage, place(stage)] = value
        else:
            totals[here] = value
        for k in range(1, count):
            sum_copy(stage, k).start()
        each(batch, lambda i: start_outputs(stage * batch + i))
        for k in range(1, count):
            sum_copy(stage, k).wait_recv()
        if stage < 3:
            value = functools.reduce(jnp.add, [stages[stage, i] for i in range(count)])
    gain_grads[...] = totals[...].reshape(2, HEADS, 2, HD)
    for stage in range(4):
        for k in range(1, counts[stage]):
            sum_copy(stage, k).wait_send()

    def finish(u):
        for slot in (1, 2, 3):
            in_copy(u, slot).wait_send()
            out_copy(u, slot).wait()

    each(HEADS, finish)


def solution(mesh):
    n_t, n_h = mesh.shape["tm"], mesh.shape["height"]
    dma = pltpu.SemaphoreType.DMA
    far = pl.BlockSpec(memory_space=pl.ANY)
    near = pl.BlockSpec(memory_space=pltpu.VMEM)
    quads = (4, HALF_H, WW, HD)
    gain_shape = jax.ShapeDtypeStruct((2, HEADS, 2, HD), jnp.float32)

    def shards(saved, gains):
        saved = pltpu.with_memory_space_constraint(saved, pltpu.HBM)
        gains = pltpu.with_memory_space_constraint(gains.transpose(0, 2, 1, 3), pltpu.HBM)
        grads_shape = (2, 3) + saved.shape[2:]
        grads, gain_grads = pl.pallas_call(
            functools.partial(grad_kernel, n_t, n_h),
            out_shape=(pltpu.VMEM(grads_shape, jnp.bfloat16), gain_shape),
            in_specs=[far, far],
            out_specs=(near, near),
            scratch_shapes=[
                pltpu.VMEM(saved.shape[1:], jnp.bfloat16),
                pltpu.VMEM((HEADS, 4) + quads, jnp.bfloat16),
                pltpu.VMEM((HEADS, 3, 3) + quads[1:], jnp.bfloat16),
                pltpu.VMEM((2, HEADS, 2, HD), jnp.float32),
                pltpu.VMEM((2 * HEADS, 2, HD), jnp.float32),
                pltpu.VMEM((3, GROUP, 2 * HEADS // min(n_h, GROUP), 2, HD), jnp.float32),
                pltpu.VMEM((2 * HEADS, 2, HD), jnp.float32),
                dma,
                dma((4,)),
                dma((HEADS,)),
                dma((HEADS, 3)),
                dma((HEADS, 3)),
                dma((HEADS, 3)),
                dma((HEADS, 3)),
                dma((4, GROUP)),
                dma((4, GROUP)),
            ],
            compiler_params=pltpu.CompilerParams(
                collective_id=0, has_side_effects=True, vmem_limit_bytes=40 * 2**20
            ),
        )(saved, gains)
        return grads, gain_grads.transpose(0, 2, 1, 3)

    return jax.shard_map(
        shards,
        mesh=mesh,
        in_specs=(P(None, None, "tm", "height", None, None), P()),
        out_specs=(P(None, None, "tm", "height", None, None), P()),
        check_vma=False,
    )
```

```python
import functools
import math

import jax
import jax.numpy as jnp
from jax import lax
from jax.experimental import pallas as pl
from jax.experimental.pallas import tpu as pltpu
from jax.sharding import PartitionSpec as P

HEADS = 12
HD = 128
WT = 2
WH = 8
WW = 16
HALF_H = WH // 2
TOKENS = WT * WH * WW
PART = 128
ROWS = 64
ROLES = 4
GROUP = 8

EPSILON = 1e-06
SCALE = HD ** (-0.5)
EXP2_SCALE = SCALE * math.log2(math.e)

MESH = pl.DeviceIdType.MESH
NT = (((1,), (1,)), ((), ()))
NN = (((1,), (0,)), ((), ()))
TN = (((0,), (0,)), ((), ()))


def matmul(a, b, dims):
    return lax.dot_general(a, b, dims, preferred_element_type=jnp.float32)


def rows_of(array, first):
    return array[first : first + ROWS]


def column_sum(blocks):
    tiles = [block.reshape(-1, 8, block.shape[-1]).sum(0) for block in blocks]
    return jnp.sum(functools.reduce(jnp.add, tiles), 0, keepdims=True)


def head_grad(q_raw, k_raw, values_in, out_grad, gain_q, gain_k):
    blocks = range(0, TOKENS, ROWS)

    def normed(raw, gain):
        units, inverses, norms = [], [], []
        for first in blocks:
            full = rows_of(raw, first).astype(jnp.float32)
            inverse = lax.rsqrt(jnp.mean(full * full, -1, keepdims=True) + EPSILON)
            unit = full * inverse
            units.append(unit)
            inverses.append(inverse)
            norms.append((unit * gain).astype(jnp.bfloat16))
        return units, inverses, jnp.concatenate(norms, 0)

    unit_q, inv_q, q_norm = normed(q_raw, gain_q)
    unit_k, inv_k, k_norm = normed(k_raw, gain_k)
    yield
    scores = matmul(k_norm, q_norm, NT)
    prob_grad = matmul(values_in, out_grad, NT)
    yield
    low_parts, score_grad_parts = [], []
    for first_query in range(0, TOKENS, PART):
        part = scores[:, first_query : first_query + PART]
        grad_part = prob_grad[:, first_query : first_query + PART]
        top = jnp.max(part, 0, keepdims=True)
        powers = [jnp.exp2((rows_of(part, first) - top) * EXP2_SCALE) for first in blocks]
        inverse = 1.0 / column_sum(powers)
        probs, weighted, low = [], [], []
        for first, power in zip(blocks, powers):
            probs.append(power * inverse)
            weighted.append(probs[-1] * rows_of(grad_part, first))
            low.append(probs[-1].astype(jnp.bfloat16))
        delta = column_sum(weighted)
        score_grad_parts.append(
            jnp.concatenate(
                [
                    (prob * (rows_of(grad_part, first) - delta)).astype(jnp.bfloat16)
                    for first, prob in zip(blocks, probs)
                ],
                0,
            )
        )
        low_parts.append(jnp.concatenate(low, 0))
        yield
    score_grad = jnp.concatenate(score_grad_parts, 1)
    value_grad = matmul(jnp.concatenate(low_parts, 1), out_grad, NN).astype(jnp.bfloat16)
    kn_grad = matmul(score_grad, q_norm, NN)
    qn_grad = matmul(score_grad, k_norm, TN)
    yield

    def raw_grad(norm_grad, units, inverses, gain):
        scaled_gain = gain * SCALE
        alongs, raws = [], []
        for first, unit, inverse in zip(blocks, units, inverses):
            grad = rows_of(norm_grad, first)
            along = grad * unit
            mean = jnp.mean(along * scaled_gain, -1, keepdims=True)
            raws.append((inverse * (grad * scaled_gain - unit * mean)).astype(jnp.bfloat16))
            alongs.append(along)
        return jnp.concatenate(raws, 0), column_sum(alongs) * SCALE

    k_grad, gain_k_grad = raw_grad(kn_grad, unit_k, inv_k, gain_k)
    yield
    q_grad, gain_q_grad = raw_grad(qn_grad, unit_q, inv_q, gain_q)
    return (q_grad, k_grad, value_grad), gain_q_grad, gain_k_grad


def side_by_side(heads):
    results = [None] * len(heads)
    left, turn = set(range(len(heads))), 0
    while left:
        for index in sorted(left):
            if index <= turn:
                try:
                    next(heads[index])
                except StopIteration as end:
                    results[index] = end.value
                    left.discard(index)
        turn += 1
    return results


def each(count, body):
    lax.fori_loop(0, count, lambda i, carry: (body(i), carry)[1], 0)


def grad_kernel(
    n_t, n_h,
    saved, gains_far, grads, gain_grads,
    x0, x1, w1, gains, sums, stages, totals,
    load_gains, load0, load1, in_send, in_recv, out_send, out_recv, sum_send, sum_recv,
):
    t = lax.axis_index("tm")
    h = lax.axis_index("height")

    def at(dt, dh):
        return (lax.rem(t + dt + n_t, n_t), lax.rem(h + dh + n_h, n_h))

    def features(head):
        return pl.ds(pl.multiple_of(head * HD, HD), HD)

    def unit(u):
        role = lax.rem(u, ROLES)
        return lax.rem(role, 2), role // 2, role * (HEADS // ROLES) + u // ROLES

    def holder(u, slot):
        rt, rh, _ = unit(u)
        return (rt if slot < 2 else 1 - rt), (rh if slot % 2 == 0 else 1 - rh)

    def quadrant(u, slot):
        a, b = holder(u, slot)
        return 1 - a, pl.ds((1 - b) * HALF_H, HALF_H), slice(None), features(unit(u)[2])

    def owner(u, slot):
        (rt, rh, _), (a, b) = unit(u), holder(u, slot)
        return at(a - rt, b - rh)

    def worker(u, slot):
        (rt, rh, _), (a, b) = unit(u), holder(u, slot)
        return at(rt - a, rh - b)

    def in_copy(u, slot):
        return pltpu.make_async_remote_copy(
            src_ref=saved.at[(1, slice(None)) + quadrant(u, slot)],
            dst_ref=x1.at[u, :, slot],
            send_sem=in_send.at[u, slot - 1],
            recv_sem=in_recv.at[u, slot - 1],
            device_id=worker(u, slot),
            device_id_type=MESH,
        )

    def in_local(u):
        return pltpu.make_async_copy(
            saved.at[(1, slice(None)) + quadrant(u, 0)], x1.at[u, :, 0], load1.at[u]
        )

    def out_copy(u, slot):
        return pltpu.make_async_remote_copy(
            src_ref=w1.at[u, :, slot - 1],
            dst_ref=grads.at[(1, slice(None)) + quadrant(u, slot)],
            send_sem=out_send.at[u, slot - 1],
            recv_sem=out_recv.at[u, slot - 1],
            device_id=owner(u, slot),
            device_id_type=MESH,
        )

    def load(a):
        return pltpu.make_async_copy(saved.at[0, a], x0.at[a], load0.at[a])

    near_h, near_t = min(n_h, GROUP), min(n_t, GROUP)
    far_h, far_t = n_h // near_h, n_t // near_t
    counts = (near_h, far_h * far_t, near_t, near_h)

    def place(stage):
        if stage == 1:
            return t // near_t * far_h + h // near_h
        return lax.rem(t, near_t) if stage == 2 else lax.rem(h, near_h)

    def peer(stage, k):
        if stage == 1:
            other_t = lax.rem(t // near_t + k // far_h, far_t)
            other_h = lax.rem(h // near_h + lax.rem(k, far_h), far_h)
            return other_t * far_h + other_h, (
                other_t * near_t + lax.rem(t, near_t),
                other_h * near_h + lax.rem(h, near_h),
            )
        other = lax.rem(place(stage) + k, counts[stage])
        shift = other - place(stage)
        return other, ((t + shift, h) if stage == 2 else (t, h + shift))

    barrier = pltpu.get_barrier_semaphore()

    def greet(device):
        pl.semaphore_signal(barrier, inc=1, device_id=device, device_id_type=MESH)

    greeted = 0
    for dt in (-1, 0, 1):
        for dh in (-1, 0, 1):
            if dt or dh:
                greet(at(dt, dh))
                greeted += 1
    for stage in range(3):
        for k in range(1, counts[stage]):
            greet(peer(stage, k)[1])
            greeted += 1
    gains_copy = pltpu.make_async_copy(gains_far, gains, load_gains)
    gains_copy.start()
    each(4, lambda a: load(a).start())
    each(HEADS, lambda u: in_local(u).start())
    pl.semaphore_wait(barrier, greeted)

    def start_inputs(u):
        for slot in (2, 3, 1):
            in_copy(u, slot).start()

    each(HEADS, start_inputs)
    gains_copy.wait()
    each(4, lambda a: load(a).wait())

    def operands(block, u):
        if block == 0:
            return [x0[a, :, :, :, features(u)].reshape(TOKENS, HD) for a in range(4)]
        return [x1[u, a].reshape(TOKENS, HD) for a in range(4)]

    def compute(pair):
        heads = [u if block == 0 else unit(u)[2] for block, u in pair]
        running = [
            head_grad(*operands(block, u), gains[block, head, 0:1, :], gains[block, head, 1:2, :])
            for (block, u), head in zip(pair, heads)
        ]
        for (block, u), head, result in zip(pair, heads, side_by_side(running)):
            results, gain_q_grad, gain_k_grad = result
            sums[block * HEADS + head, 0:1, :] = gain_q_grad
            sums[block * HEADS + head, 1:2, :] = gain_k_grad
            for a in range(3):
                if block == 0:
                    grads[0, a, :, :, :, features(u)] = results[a].reshape(WT, WH, WW, HD)
                else:
                    quads = results[a].reshape(4, HALF_H, WW, HD)
                    w1[u, a] = quads[1:]
                    grads[(1, a) + quadrant(u, 0)] = quads[0]

    def start_outputs(u):
        for slot in (2, 3, 1):
            out_copy(u, slot).start()

    def wait_inputs(u):
        in_local(u).wait()
        for slot in (1, 2, 3):
            in_copy(u, slot).wait_recv()

    def step(u):
        wait_inputs(u)
        compute([(0, u + 2), (1, u)])
        start_outputs(u)

    compute([(0, 0), (0, 1)])
    each(HEADS - 2, step)
    wait_inputs(HEADS - 2)
    wait_inputs(HEADS - 1)
    compute([(1, HEADS - 2), (1, HEADS - 1)])

    size = 2 * HEADS // near_h

    def sum_copy(stage, k):
        other, device = peer(stage, k)
        mine = place(stage)
        if stage == 0:
            source, target = sums.at[pl.ds(other * size, size)], stages.at[0, mine]
        elif stage < 3:
            source = target = stages.at[stage, mine]
        else:
            source = target = totals.at[pl.ds(mine * size, size)]
        return pltpu.make_async_remote_copy(
            src_ref=source,
            dst_ref=target,
            send_sem=sum_send.at[stage, k],
            recv_sem=sum_recv.at[stage, k],
            device_id=device,
            device_id_type=MESH,
        )

    here = pl.ds(place(0) * size, size)
    value = sums[here]
    for stage in range(4):
        count = counts[stage]
        if stage < 3:
            stages[stage, place(stage)] = value
        else:
            totals[here] = value
        for k in sorted(range(1, count), key=lambda k: -min(k, count - k)):
            sum_copy(stage, k).start()
        if stage == 0:
            start_outputs(HEADS - 2)
            start_outputs(HEADS - 1)
        for k in range(1, count):
            sum_copy(stage, k).wait_recv()
        if stage < 3:
            value = functools.reduce(jnp.add, [stages[stage, i] for i in range(count)])
    gain_grads[...] = totals[...].reshape(2, HEADS, 2, HD)
    for stage in range(4):
        for k in range(1, counts[stage]):
            sum_copy(stage, k).wait_send()

    def finish(u):
        for slot in (1, 2, 3):
            in_copy(u, slot).wait_send()
            out_copy(u, slot).wait()

    each(HEADS, finish)


def solution(mesh):
    n_t, n_h = mesh.shape["tm"], mesh.shape["height"]
    dma = pltpu.SemaphoreType.DMA
    far = pl.BlockSpec(memory_space=pl.ANY)
    near = pl.BlockSpec(memory_space=pltpu.VMEM)
    quads = (4, HALF_H, WW, HD)
    gain_shape = jax.ShapeDtypeStruct((2, HEADS, 2, HD), jnp.float32)

    def shards(saved, gains):
        saved = pltpu.with_memory_space_constraint(saved, pltpu.HBM)
        gains = pltpu.with_memory_space_constraint(gains.transpose(0, 2, 1, 3), pltpu.HBM)
        grads_shape = (2, 3) + saved.shape[2:]
        grads, gain_grads = pl.pallas_call(
            functools.partial(grad_kernel, n_t, n_h),
            out_shape=(pltpu.VMEM(grads_shape, jnp.bfloat16), gain_shape),
            in_specs=[far, far],
            out_specs=(near, near),
            scratch_shapes=[
                pltpu.VMEM(saved.shape[1:], jnp.bfloat16),
                pltpu.VMEM((HEADS, 4) + quads, jnp.bfloat16),
                pltpu.VMEM((HEADS, 3, 3) + quads[1:], jnp.bfloat16),
                pltpu.VMEM((2, HEADS, 2, HD), jnp.float32),
                pltpu.VMEM((2 * HEADS, 2, HD), jnp.float32),
                pltpu.VMEM((3, GROUP, 2 * HEADS // min(n_h, GROUP), 2, HD), jnp.float32),
                pltpu.VMEM((2 * HEADS, 2, HD), jnp.float32),
                dma,
                dma((4,)),
                dma((HEADS,)),
                dma((HEADS, 3)),
                dma((HEADS, 3)),
                dma((HEADS, 3)),
                dma((HEADS, 3)),
                dma((4, GROUP)),
                dma((4, GROUP)),
            ],
            compiler_params=pltpu.CompilerParams(
                collective_id=0, has_side_effects=True, vmem_limit_bytes=40 * 2**20
            ),
        )(saved, gains)
        return grads, gain_grads.transpose(0, 2, 1, 3)

    return jax.shard_map(
        shards,
        mesh=mesh,
        in_specs=(P(None, None, "tm", "height", None, None), P()),
        out_specs=(P(None, None, "tm", "height", None, None), P()),
        check_vma=False,
    )
```

```python
import functools
import math

import jax
import jax.numpy as jnp
from jax import lax
from jax.experimental import pallas as pl
from jax.experimental.pallas import tpu as pltpu
from jax.sharding import PartitionSpec as P

HEADS = 12
HD = 128
WT = 2
WH = 8
WW = 16
HALF_H = WH // 2
TOKENS = WT * WH * WW
PART = 128
ROWS = 64
ROLES = 4
GROUP = 8
LAST = 3

EPSILON = 1e-06
SCALE = HD ** (-0.5)
EXP2_SCALE = SCALE * math.log2(math.e)

MESH = pl.DeviceIdType.MESH
NT = (((1,), (1,)), ((), ()))
NN = (((1,), (0,)), ((), ()))
TN = (((0,), (0,)), ((), ()))


def matmul(a, b, dims):
    return lax.dot_general(a, b, dims, preferred_element_type=jnp.float32)


def rows_of(array, first):
    return array[first : first + ROWS]


def column_sum(blocks):
    tiles = [block.reshape(-1, 8, block.shape[-1]).sum(0) for block in blocks]
    return jnp.sum(functools.reduce(jnp.add, tiles), 0, keepdims=True)


def head_grad(q_raw, k_raw, values_in, out_grad, gain_q, gain_k):
    blocks = range(0, TOKENS, ROWS)

    def normed(raw, gain):
        units, inverses, norms = [], [], []
        for first in blocks:
            full = rows_of(raw, first).astype(jnp.float32)
            inverse = lax.rsqrt(jnp.mean(full * full, -1, keepdims=True) + EPSILON)
            unit = full * inverse
            units.append(unit)
            inverses.append(inverse)
            norms.append((unit * gain).astype(jnp.bfloat16))
        return units, inverses, jnp.concatenate(norms, 0)

    unit_q, inv_q, q_norm = normed(q_raw, gain_q)
    unit_k, inv_k, k_norm = normed(k_raw, gain_k)
    yield
    scores = matmul(k_norm, q_norm, NT)
    prob_grad = matmul(values_in, out_grad, NT)
    yield
    low_parts, score_grad_parts = [], []
    for first_query in range(0, TOKENS, PART):
        part = scores[:, first_query : first_query + PART]
        grad_part = prob_grad[:, first_query : first_query + PART]
        top = jnp.max(part, 0, keepdims=True)
        powers = [jnp.exp2((rows_of(part, first) - top) * EXP2_SCALE) for first in blocks]
        inverse = 1.0 / column_sum(powers)
        probs, weighted, low = [], [], []
        for first, power in zip(blocks, powers):
            probs.append(power * inverse)
            weighted.append(probs[-1] * rows_of(grad_part, first))
            low.append(probs[-1].astype(jnp.bfloat16))
        delta = column_sum(weighted)
        score_grad_parts.append(
            jnp.concatenate(
                [
                    (prob * (rows_of(grad_part, first) - delta)).astype(jnp.bfloat16)
                    for first, prob in zip(blocks, probs)
                ],
                0,
            )
        )
        low_parts.append(jnp.concatenate(low, 0))
        yield
    score_grad = jnp.concatenate(score_grad_parts, 1)
    value_grad = matmul(jnp.concatenate(low_parts, 1), out_grad, NN).astype(jnp.bfloat16)
    kn_grad = matmul(score_grad, q_norm, NN)
    qn_grad = matmul(score_grad, k_norm, TN)
    yield

    def raw_grad(norm_grad, units, inverses, gain):
        scaled_gain = gain * SCALE
        alongs, raws = [], []
        for first, unit, inverse in zip(blocks, units, inverses):
            grad = rows_of(norm_grad, first)
            along = grad * unit
            mean = jnp.mean(along * scaled_gain, -1, keepdims=True)
            raws.append((inverse * (grad * scaled_gain - unit * mean)).astype(jnp.bfloat16))
            alongs.append(along)
        return jnp.concatenate(raws, 0), column_sum(alongs) * SCALE

    k_grad, gain_k_grad = raw_grad(kn_grad, unit_k, inv_k, gain_k)
    yield
    q_grad, gain_q_grad = raw_grad(qn_grad, unit_q, inv_q, gain_q)
    return (q_grad, k_grad, value_grad), gain_q_grad, gain_k_grad


def side_by_side(heads):
    results = [None] * len(heads)
    left, turn = set(range(len(heads))), 0
    while left:
        for index in sorted(left):
            if index <= turn:
                try:
                    next(heads[index])
                except StopIteration as end:
                    results[index] = end.value
                    left.discard(index)
        turn += 1
    return results


def each(count, body):
    lax.fori_loop(0, count, lambda i, carry: (body(i), carry)[1], 0)


def farthest_first(count):
    return sorted(range(1, count), key=lambda k: -min(k, count - k))


def grad_kernel(
    n_t, n_h,
    saved, gains_far, grads, gain_grads,
    x0, x1, w1, gains, sums, stages, totals,
    load_gains, load0, in_send, in_recv, out_send, out_recv, sum_send, sum_recv,
):
    t = lax.axis_index("tm")
    h = lax.axis_index("height")

    def at(dt, dh):
        return (lax.rem(t + dt + n_t, n_t), lax.rem(h + dh + n_h, n_h))

    def features(head):
        return pl.ds(pl.multiple_of(head * HD, HD), HD)

    def unit(u):
        role = lax.rem(u, ROLES)
        return lax.rem(role, 2), role // 2, role * (HEADS // ROLES) + u // ROLES

    def holder(u, slot):
        rt, rh, _ = unit(u)
        return (rt if slot < 2 else 1 - rt), (rh if slot % 2 == 0 else 1 - rh)

    def quadrant(u, slot):
        a, b = holder(u, slot)
        return 1 - a, pl.ds((1 - b) * HALF_H, HALF_H), slice(None), features(unit(u)[2])

    def owner(u, slot):
        (rt, rh, _), (a, b) = unit(u), holder(u, slot)
        return at(a - rt, b - rh)

    def worker(u, slot):
        (rt, rh, _), (a, b) = unit(u), holder(u, slot)
        return at(rt - a, rh - b)

    def in_copy(u, slot):
        return pltpu.make_async_remote_copy(
            src_ref=saved.at[(1, slice(None)) + quadrant(u, slot)],
            dst_ref=x1.at[u, :, slot],
            send_sem=in_send,
            recv_sem=in_recv.at[u],
            device_id=worker(u, slot),
            device_id_type=MESH,
        )

    def in_local(u):
        return pltpu.make_async_copy(
            saved.at[(1, slice(None)) + quadrant(u, 0)], x1.at[u, :, 0], in_recv.at[u]
        )

    def out_copy(u, slot):
        return pltpu.make_async_remote_copy(
            src_ref=w1.at[u, :, slot - 1],
            dst_ref=grads.at[(1, slice(None)) + quadrant(u, slot)],
            send_sem=out_send,
            recv_sem=out_recv,
            device_id=owner(u, slot),
            device_id_type=MESH,
        )

    def load(a):
        return pltpu.make_async_copy(saved.at[0, a], x0.at[a], load0.at[a])

    near_h, near_t = min(n_h, GROUP), min(n_t, GROUP)
    far_h, far_t = n_h // near_h, n_t // near_t
    counts = (near_h, far_h * far_t, near_t, near_h)

    def place(stage):
        if stage == 1:
            return t // near_t * far_h + h // near_h
        return lax.rem(t, near_t) if stage == 2 else lax.rem(h, near_h)

    def peer(stage, k):
        if stage == 1:
            other_t = lax.rem(t // near_t + k // far_h, far_t)
            other_h = lax.rem(h // near_h + lax.rem(k, far_h), far_h)
            return other_t * far_h + other_h, (
                other_t * near_t + lax.rem(t, near_t),
                other_h * near_h + lax.rem(h, near_h),
            )
        other = lax.rem(place(stage) + k, counts[stage])
        shift = other - place(stage)
        return other, ((t + shift, h) if stage == 2 else (t, h + shift))

    barrier = pltpu.get_barrier_semaphore()

    def greet(device):
        pl.semaphore_signal(barrier, inc=1, device_id=device, device_id_type=MESH)

    greeted = 0
    for stage in (2, 1, 0):
        for k in farthest_first(counts[stage]):
            greet(peer(stage, k)[1])
            greeted += 1
    for dt in (-1, 0, 1):
        for dh in (-1, 0, 1):
            if dt or dh:
                greet(at(dt, dh))
                greeted += 1
    gains_copy = pltpu.make_async_copy(gains_far, gains, load_gains)
    gains_copy.start()
    each(4, lambda a: load(a).start())
    each(HEADS, lambda u: in_local(u).start())
    pl.semaphore_wait(barrier, greeted)

    def start_inputs(u):
        for slot in (2, 3, 1):
            in_copy(u, slot).start()

    each(HEADS, start_inputs)
    gains_copy.wait()
    each(4, lambda a: load(a).wait())

    def operands(block, u):
        if block == 0:
            return [x0[a, :, :, :, features(u)].reshape(TOKENS, HD) for a in range(4)]
        return [x1[u, a].reshape(TOKENS, HD) for a in range(4)]

    def compute(pair):
        heads = [u if block == 0 else unit(u)[2] for block, u in pair]
        running = [
            head_grad(*operands(block, u), gains[block, head, 0:1, :], gains[block, head, 1:2, :])
            for (block, u), head in zip(pair, heads)
        ]
        for (block, u), head, result in zip(pair, heads, side_by_side(running)):
            results, gain_q_grad, gain_k_grad = result
            sums[block * HEADS + head, 0:1, :] = gain_q_grad
            sums[block * HEADS + head, 1:2, :] = gain_k_grad
            for a in range(3):
                if block == 0:
                    grads[0, a, :, :, :, features(u)] = results[a].reshape(WT, WH, WW, HD)
                else:
                    quads = results[a].reshape(4, HALF_H, WW, HD)
                    w1[u, a] = quads[1:]
                    grads[(1, a) + quadrant(u, 0)] = quads[0]

    def start_outputs(u):
        for slot in (2, 3, 1):
            out_copy(u, slot).start()

    def drain(semaphore, ref):
        pltpu.make_async_copy(ref, ref, semaphore).wait()

    def wait_inputs(u):
        drain(in_recv.at[u], x1.at[u])

    def step(u):
        wait_inputs(u)
        compute([(0, u + 2), (1, u)])
        pl.when(u < HEADS - LAST)(lambda: start_outputs(u))

    compute([(0, 0), (0, 1)])
    each(HEADS - 2, step)
    wait_inputs(HEADS - 2)
    wait_inputs(HEADS - 1)
    compute([(1, HEADS - 2), (1, HEADS - 1)])

    size = 2 * HEADS // near_h

    def sum_copy(stage, k):
        other, device = peer(stage, k)
        mine = place(stage)
        if stage == 0:
            source, target = sums.at[pl.ds(other * size, size)], stages.at[0, mine]
        elif stage < 3:
            source = target = stages.at[stage, mine]
        else:
            source = target = totals.at[pl.ds(mine * size, size)]
        return pltpu.make_async_remote_copy(
            src_ref=source,
            dst_ref=target,
            send_sem=sum_send.at[stage, k],
            recv_sem=sum_recv.at[stage, k],
            device_id=device,
            device_id_type=MESH,
        )

    here = pl.ds(place(0) * size, size)
    value = sums[here]
    for stage in range(4):
        count = counts[stage]
        if stage < 3:
            stages[stage, place(stage)] = value
        else:
            totals[here] = value
        for k in farthest_first(count):
            sum_copy(stage, k).start()
        for u in {0: (HEADS - 3, HEADS - 2), 1: (HEADS - 1,)}.get(stage, ()):
            start_outputs(u)
        for k in range(1, count):
            sum_copy(stage, k).wait_recv()
        if stage < 3:
            value = functools.reduce(jnp.add, [stages[stage, i] for i in range(count)])
    gain_grads[...] = totals[...].reshape(2, HEADS, 2, HD)
    for stage in range(4):
        for k in range(1, counts[stage]):
            sum_copy(stage, k).wait_send()

    drain(in_send, x1.at[pl.ds(0, HEADS * 3 // 4)])
    drain(out_send, w1)
    drain(out_recv, w1)


def solution(mesh):
    n_t, n_h = mesh.shape["tm"], mesh.shape["height"]
    dma = pltpu.SemaphoreType.DMA
    far = pl.BlockSpec(memory_space=pl.ANY)
    near = pl.BlockSpec(memory_space=pltpu.VMEM)
    quads = (4, HALF_H, WW, HD)
    gain_shape = jax.ShapeDtypeStruct((2, HEADS, 2, HD), jnp.float32)

    def shards(saved, gains):
        saved = pltpu.with_memory_space_constraint(saved, pltpu.HBM)
        gains = pltpu.with_memory_space_constraint(gains.transpose(0, 2, 1, 3), pltpu.HBM)
        grads_shape = (2, 3) + saved.shape[2:]
        grads, gain_grads = pl.pallas_call(
            functools.partial(grad_kernel, n_t, n_h),
            out_shape=(pltpu.VMEM(grads_shape, jnp.bfloat16), gain_shape),
            in_specs=[far, far],
            out_specs=(near, near),
            scratch_shapes=[
                pltpu.VMEM(saved.shape[1:], jnp.bfloat16),
                pltpu.VMEM((HEADS, 4) + quads, jnp.bfloat16),
                pltpu.VMEM((HEADS, 3, 3) + quads[1:], jnp.bfloat16),
                pltpu.VMEM((2, HEADS, 2, HD), jnp.float32),
                pltpu.VMEM((2 * HEADS, 2, HD), jnp.float32),
                pltpu.VMEM((3, GROUP, 2 * HEADS // min(n_h, GROUP), 2, HD), jnp.float32),
                pltpu.VMEM((2 * HEADS, 2, HD), jnp.float32),
                dma,
                dma((4,)),
                dma,
                dma((HEADS,)),
                dma,
                dma,
                dma((4, GROUP)),
                dma((4, GROUP)),
            ],
            compiler_params=pltpu.CompilerParams(
                collective_id=0, has_side_effects=True, vmem_limit_bytes=40 * 2**20
            ),
        )(saved, gains)
        return grads, gain_grads.transpose(0, 2, 1, 3)

    return jax.shard_map(
        shards,
        mesh=mesh,
        in_specs=(P(None, None, "tm", "height", None, None), P()),
        out_specs=(P(None, None, "tm", "height", None, None), P()),
        check_vma=False,
    )
```

```python
import functools
import math

import jax
import jax.numpy as jnp
from jax import lax
from jax.experimental import pallas as pl
from jax.experimental.pallas import tpu as pltpu
from jax.sharding import PartitionSpec as P

HEADS = 12
HD = 128
WT = 2
WH = 8
WW = 16
HALF_H = WH // 2
TOKENS = WT * WH * WW
PART = 128
ROWS = 64
ROLES = 4
GROUP = 8
LAST = 3

EPSILON = 1e-06
SCALE = HD ** (-0.5)
EXP2_SCALE = SCALE * math.log2(math.e)

MESH = pl.DeviceIdType.MESH
NT = (((1,), (1,)), ((), ()))
NN = (((1,), (0,)), ((), ()))
TN = (((0,), (0,)), ((), ()))


def matmul(a, b, dims):
    return lax.dot_general(a, b, dims, preferred_element_type=jnp.float32)


def rows_of(array, first):
    return array[first : first + ROWS]


def column_sum(blocks):
    tiles = [block.reshape(-1, 8, block.shape[-1]).sum(0) for block in blocks]
    return jnp.sum(functools.reduce(jnp.add, tiles), 0, keepdims=True)


def head_grad(q_raw, k_raw, values_in, out_grad, gain_q, gain_k):
    blocks = range(0, TOKENS, ROWS)

    def normed(raw, gain):
        units, inverses, norms = [], [], []
        for first in blocks:
            full = rows_of(raw, first).astype(jnp.float32)
            inverse = lax.rsqrt(jnp.mean(full * full, -1, keepdims=True) + EPSILON)
            unit = full * inverse
            units.append(unit)
            inverses.append(inverse)
            norms.append((unit * gain).astype(jnp.bfloat16))
        return units, inverses, jnp.concatenate(norms, 0)

    unit_q, inv_q, q_norm = normed(q_raw, gain_q)
    unit_k, inv_k, k_norm = normed(k_raw, gain_k)
    yield
    scores = matmul(k_norm, q_norm, NT)
    prob_grad = matmul(values_in, out_grad, NT)
    yield
    low_parts, score_grad_parts = [], []
    for first_query in range(0, TOKENS, PART):
        part = scores[:, first_query : first_query + PART]
        grad_part = prob_grad[:, first_query : first_query + PART]
        top = jnp.max(part, 0, keepdims=True)
        powers = [jnp.exp2((rows_of(part, first) - top) * EXP2_SCALE) for first in blocks]
        inverse = 1.0 / column_sum(powers)
        probs, weighted, low = [], [], []
        for first, power in zip(blocks, powers):
            probs.append(power * inverse)
            weighted.append(probs[-1] * rows_of(grad_part, first))
            low.append(probs[-1].astype(jnp.bfloat16))
        delta = column_sum(weighted)
        score_grad_parts.append(
            jnp.concatenate(
                [
                    (prob * (rows_of(grad_part, first) - delta)).astype(jnp.bfloat16)
                    for first, prob in zip(blocks, probs)
                ],
                0,
            )
        )
        low_parts.append(jnp.concatenate(low, 0))
        yield
    score_grad = jnp.concatenate(score_grad_parts, 1)
    value_grad = matmul(jnp.concatenate(low_parts, 1), out_grad, NN).astype(jnp.bfloat16)
    kn_grad = matmul(score_grad, q_norm, NN)
    qn_grad = matmul(score_grad, k_norm, TN)
    yield

    def raw_grad(norm_grad, units, inverses, gain):
        scaled_gain = gain * SCALE
        alongs, raws = [], []
        for first, unit, inverse in zip(blocks, units, inverses):
            grad = rows_of(norm_grad, first)
            along = grad * unit
            mean = jnp.mean(along * scaled_gain, -1, keepdims=True)
            raws.append((inverse * (grad * scaled_gain - unit * mean)).astype(jnp.bfloat16))
            alongs.append(along)
        return jnp.concatenate(raws, 0), column_sum(alongs) * SCALE

    k_grad, gain_k_grad = raw_grad(kn_grad, unit_k, inv_k, gain_k)
    yield
    q_grad, gain_q_grad = raw_grad(qn_grad, unit_q, inv_q, gain_q)
    return (q_grad, k_grad, value_grad), gain_q_grad, gain_k_grad


def side_by_side(heads):
    results = [None] * len(heads)
    left, turn = set(range(len(heads))), 0
    while left:
        for index in sorted(left):
            if index <= turn:
                try:
                    next(heads[index])
                except StopIteration as end:
                    results[index] = end.value
                    left.discard(index)
        turn += 1
    return results


def each(count, body):
    lax.fori_loop(0, count, lambda i, carry: (body(i), carry)[1], 0)


def farthest_first(count):
    return sorted(range(1, count), key=lambda k: -min(k, count - k))


def grad_kernel(
    n_t, n_h,
    saved, gains_far, grads, gain_grads,
    x0, x1, w1, gains, sums, stages, totals,
    load_gains, load0, in_send, in_recv, out_send, out_recv, sum_send, sum_recv,
):
    t = lax.axis_index("tm")
    h = lax.axis_index("height")

    def at(dt, dh):
        return (lax.rem(t + dt + n_t, n_t), lax.rem(h + dh + n_h, n_h))

    def features(head):
        return pl.ds(pl.multiple_of(head * HD, HD), HD)

    def unit(u):
        role = lax.rem(u, ROLES)
        return lax.rem(role, 2), role // 2, role * (HEADS // ROLES) + u // ROLES

    def holder(u, slot):
        rt, rh, _ = unit(u)
        return (rt if slot < 2 else 1 - rt), (rh if slot % 2 == 0 else 1 - rh)

    def quadrant(u, slot):
        a, b = holder(u, slot)
        return 1 - a, pl.ds((1 - b) * HALF_H, HALF_H), slice(None), features(unit(u)[2])

    def owner(u, slot):
        (rt, rh, _), (a, b) = unit(u), holder(u, slot)
        return at(a - rt, b - rh)

    def worker(u, slot):
        (rt, rh, _), (a, b) = unit(u), holder(u, slot)
        return at(rt - a, rh - b)

    def in_copy(u, slot):
        return pltpu.make_async_remote_copy(
            src_ref=saved.at[(1, slice(None)) + quadrant(u, slot)],
            dst_ref=x1.at[u, :, slot],
            send_sem=in_send,
            recv_sem=in_recv.at[u],
            device_id=worker(u, slot),
            device_id_type=MESH,
        )

    def in_local(u):
        return pltpu.make_async_copy(
            saved.at[(1, slice(None)) + quadrant(u, 0)], x1.at[u, :, 0], in_recv.at[u]
        )

    def out_copy(u, slot):
        return pltpu.make_async_remote_copy(
            src_ref=w1.at[u, :, slot - 1],
            dst_ref=grads.at[(1, slice(None)) + quadrant(u, slot)],
            send_sem=out_send,
            recv_sem=out_recv,
            device_id=owner(u, slot),
            device_id_type=MESH,
        )

    def load(a):
        return pltpu.make_async_copy(saved.at[0, a], x0.at[a], load0.at[a])

    near_h, near_t = min(n_h, GROUP), min(n_t, GROUP)
    far_h, far_t = n_h // near_h, n_t // near_t
    counts = (near_h, far_h * far_t, near_t, near_h)

    def place(stage):
        if stage == 1:
            return t // near_t * far_h + h // near_h
        return lax.rem(t, near_t) if stage == 2 else lax.rem(h, near_h)

    def peer(stage, k):
        if stage == 1:
            other_t = lax.rem(t // near_t + k // far_h, far_t)
            other_h = lax.rem(h // near_h + lax.rem(k, far_h), far_h)
            return other_t * far_h + other_h, (
                other_t * near_t + lax.rem(t, near_t),
                other_h * near_h + lax.rem(h, near_h),
            )
        other = lax.rem(place(stage) + k, counts[stage])
        shift = other - place(stage)
        return other, ((t + shift, h) if stage == 2 else (t, h + shift))

    barrier = pltpu.get_barrier_semaphore()

    def greet(device):
        pl.semaphore_signal(barrier, inc=1, device_id=device, device_id_type=MESH)

    greeted = 0
    for stage in (2, 1, 0):
        for k in farthest_first(counts[stage]):
            greet(peer(stage, k)[1])
            greeted += 1
    for dt in (-1, 0, 1):
        for dh in (-1, 0, 1):
            if dt or dh:
                greet(at(dt, dh))
                greeted += 1
    gains_copy = pltpu.make_async_copy(gains_far, gains, load_gains)
    gains_copy.start()
    each(4, lambda a: load(a).start())
    each(HEADS, lambda u: in_local(u).start())
    pl.semaphore_wait(barrier, greeted)

    def start_inputs(u):
        for slot in (2, 3, 1):
            in_copy(u, slot).start()

    each(HEADS, start_inputs)
    gains_copy.wait()
    each(4, lambda a: load(a).wait())

    def operands(block, u):
        if block == 0:
            return [x0[a, :, :, :, features(u)].reshape(TOKENS, HD) for a in range(4)]
        return [x1[u, a].reshape(TOKENS, HD) for a in range(4)]

    def compute(pair):
        heads = [u if block == 0 else unit(u)[2] for block, u in pair]
        running = [
            head_grad(*operands(block, u), gains[block, head, 0:1, :], gains[block, head, 1:2, :])
            for (block, u), head in zip(pair, heads)
        ]
        for (block, u), head, result in zip(pair, heads, side_by_side(running)):
            results, gain_q_grad, gain_k_grad = result
            sums[block * HEADS + head, 0:1, :] = gain_q_grad
            sums[block * HEADS + head, 1:2, :] = gain_k_grad
            for a in range(3):
                if block == 0:
                    grads[0, a, :, :, :, features(u)] = results[a].reshape(WT, WH, WW, HD)
                else:
                    quads = results[a].reshape(4, HALF_H, WW, HD)
                    w1[u, a] = quads[1:]
                    grads[(1, a) + quadrant(u, 0)] = quads[0]

    def start_outputs(u):
        for slot in (2, 3, 1):
            out_copy(u, slot).start()

    def drain(semaphore, ref):
        pltpu.make_async_copy(ref, ref, semaphore).wait()

    def wait_inputs(u):
        drain(in_recv.at[u], x1.at[u])

    def step(u):
        wait_inputs(u)
        compute([(0, u + 1), (1, u)])
        pl.when(u < HEADS - LAST)(lambda: start_outputs(u))

    compute([(0, 0)])
    each(HEADS - 1, step)
    wait_inputs(HEADS - 1)
    compute([(1, HEADS - 1)])

    size = 2 * HEADS // near_h

    def sum_copy(stage, k):
        other, device = peer(stage, k)
        mine = place(stage)
        if stage == 0:
            source, target = sums.at[pl.ds(other * size, size)], stages.at[0, mine]
        elif stage < 3:
            source = target = stages.at[stage, mine]
        else:
            source = target = totals.at[pl.ds(mine * size, size)]
        return pltpu.make_async_remote_copy(
            src_ref=source,
            dst_ref=target,
            send_sem=sum_send.at[stage, k],
            recv_sem=sum_recv.at[stage, k],
            device_id=device,
            device_id_type=MESH,
        )

    here = pl.ds(place(0) * size, size)
    value = sums[here]
    for stage in range(4):
        count = counts[stage]
        if stage < 3:
            stages[stage, place(stage)] = value
        else:
            totals[here] = value
        for k in farthest_first(count):
            sum_copy(stage, k).start()
        for u in {0: (HEADS - 3, HEADS - 2), 1: (HEADS - 1,)}.get(stage, ()):
            start_outputs(u)
        for k in range(1, count):
            sum_copy(stage, k).wait_recv()
        if stage < 3:
            value = functools.reduce(jnp.add, [stages[stage, i] for i in range(count)])
    gain_grads[...] = totals[...].reshape(2, HEADS, 2, HD)
    for stage in range(4):
        for k in range(1, counts[stage]):
            sum_copy(stage, k).wait_send()

    drain(in_send, x1.at[pl.ds(0, HEADS * 3 // 4)])
    drain(out_send, w1)
    drain(out_recv, w1)


def solution(mesh):
    n_t, n_h = mesh.shape["tm"], mesh.shape["height"]
    dma = pltpu.SemaphoreType.DMA
    far = pl.BlockSpec(memory_space=pl.ANY)
    near = pl.BlockSpec(memory_space=pltpu.VMEM)
    quads = (4, HALF_H, WW, HD)
    gain_shape = jax.ShapeDtypeStruct((2, HEADS, 2, HD), jnp.float32)

    def shards(saved, gains):
        saved = pltpu.with_memory_space_constraint(saved, pltpu.HBM)
        gains = pltpu.with_memory_space_constraint(gains.transpose(0, 2, 1, 3), pltpu.HBM)
        grads_shape = (2, 3) + saved.shape[2:]
        grads, gain_grads = pl.pallas_call(
            functools.partial(grad_kernel, n_t, n_h),
            out_shape=(pltpu.VMEM(grads_shape, jnp.bfloat16), gain_shape),
            in_specs=[far, far],
            out_specs=(near, near),
            scratch_shapes=[
                pltpu.VMEM(saved.shape[1:], jnp.bfloat16),
                pltpu.VMEM((HEADS, 4) + quads, jnp.bfloat16),
                pltpu.VMEM((HEADS, 3, 3) + quads[1:], jnp.bfloat16),
                pltpu.VMEM((2, HEADS, 2, HD), jnp.float32),
                pltpu.VMEM((2 * HEADS, 2, HD), jnp.float32),
                pltpu.VMEM((3, GROUP, 2 * HEADS // min(n_h, GROUP), 2, HD), jnp.float32),
                pltpu.VMEM((2 * HEADS, 2, HD), jnp.float32),
                dma,
                dma((4,)),
                dma,
                dma((HEADS,)),
                dma,
                dma,
                dma((4, GROUP)),
                dma((4, GROUP)),
            ],
            compiler_params=pltpu.CompilerParams(
                collective_id=0, has_side_effects=True, vmem_limit_bytes=40 * 2**20
            ),
        )(saved, gains)
        return grads, gain_grads.transpose(0, 2, 1, 3)

    return jax.shard_map(
        shards,
        mesh=mesh,
        in_specs=(P(None, None, "tm", "height", None, None), P()),
        out_specs=(P(None, None, "tm", "height", None, None), P()),
        check_vma=False,
    )
```
